128 devices in a mesh: gx: 4 (over z_lo, core), gy: 32 (over y, x, z_hi).
Axes of the slice: x: 4, y: 4, z: 4 (z_hi: 2, z_lo: 2; z = z_hi * 2 + z_lo), core: 2. Of those that a mesh axis runs over, the one named last changes fastest.
Arguments:
- particles: float32 [4, 2097152], P(None, ('gx', 'gy'))
- counts: int32 [32768], P(('gx', 'gy')), may hold values from 1 to 64, as said below
- leaf_top: int32 [32768], P(('gx', 'gy')), may hold values from 0 to 4095, never falling along the last dimension, each value on 1 to 32 neighbouring positions
- near_list: int32 [32768, 27], P(('gx', 'gy')), may hold values from 0 to 32767, as said below
- leaf_list: int32 [32768, 16], P(('gx', 'gy')), may hold values from 0 to 32767, as said below
- leaf_class: int32 [32768, 16], P(('gx', 'gy')), may hold values from 0 to 315
- top_list: int32 [4096, 64], replicated, may hold values from 0 to 4095
- top_class: int32 [4096, 64], replicated, may hold values from 0 to 315
- m2l_ops: float32 [316, 81, 81], replicated
- m2m_ops: float32 [8, 81, 81], replicated
Outputs:
- potential: float32 [2097152], P(('gx', 'gy'))
The draws below stay inside these ranges and needn't reach their ends.
Inputs may be any that keep to these rules, and one draw needn't show every extreme that they name: `counts`: leaves whose global index is a multiple of 16 hold 64 particles. `near_list`: column 0 is the leaf itself; every entry lies within 32 leaves of the leaf's own index. `leaf_list`: every entry lies within 32 leaves of the leaf's own index.
All inputs are finite; a program needn't handle non-finite values.
Results may differ from the reference program's by a relative error of at most 0.0003.
Values sent between devices are 32-bit elements; how exact they have to be, the bound alone decides.
No kernel may reach another device: no remote copies, remote signals or barrier semaphores. Data moves between devices by JAX's collectives and lax.ppermute only.
A program may use at most 256 MiB of HBM per device.

```python
import math
import jax
import jax.numpy as jnp
import numpy as np
from jax import lax

ORDER = 8
COEF = 81
PART = 64
LEAVES_DEV = 256
HALO = 32
NEAR = 27
LLIST = 16
TLIST = 64
CLASSES = 316
TOP_DEV = 32
TOP_MOST = 32
TOPBOX = 4096
LEAVES_TOTAL = 32768


radius_unit = 0.6


def degree_scales():
    values = []
    for degree in range(ORDER + 1):
        for order_m in range(degree + 1):
            factor = math.sqrt(math.factorial(degree + order_m) * math.factorial(degree - order_m)) / radius_unit ** degree
            if order_m == 0:
                values.append(factor)
            else:
                values.append(factor)
                values.append(factor)
    return jnp.array(values, dtype=jnp.float32)


def draw_particles(key, part):
    key = jax.random.fold_in(key, 11)
    key_one, key_two, key_three = jax.random.split(key, 3)
    anchors = jax.random.randint(key_one, (3, LEAVES_TOTAL), 0, 3).astype(jnp.float32)
    offsets = jax.random.uniform(key_two, (3, LEAVES_TOTAL, PART), dtype=jnp.float32)
    places = (anchors[:, :, None] + offsets).reshape(3, -1)
    charges = 0.1 * jax.random.normal(key_three, (1, LEAVES_TOTAL * PART), dtype=jnp.float32)
    return jnp.concatenate([places, charges], 0)


def draw_counts(key, part):
    key = jax.random.fold_in(key, 12)
    base = jax.random.randint(key, (LEAVES_TOTAL,), PART // 4, PART + 1)
    index = jnp.arange(LEAVES_TOTAL, dtype=jnp.int32)
    return jnp.where(index % 16 == 0, PART, base).astype(jnp.int32)


def draw_near_list(key, part):
    key = jax.random.fold_in(key, 13)
    index = jnp.arange(LEAVES_TOTAL, dtype=jnp.int32)
    shifts = jax.random.randint(key, (LEAVES_TOTAL, NEAR - 1), -HALO, HALO + 1)
    others = jnp.clip(index[:, None] + shifts, 0, LEAVES_TOTAL - 1)
    return jnp.concatenate([index[:, None], others], 1).astype(jnp.int32)


def draw_leaf_list(key, part):
    key = jax.random.fold_in(key, 14)
    index = jnp.arange(LEAVES_TOTAL, dtype=jnp.int32)
    shifts = jax.random.randint(key, (LEAVES_TOTAL, LLIST), -HALO, HALO + 1)
    return jnp.clip(index[:, None] + shifts, 0, LEAVES_TOTAL - 1).astype(jnp.int32)


def draw_m2l_ops(key, part):
    key = jax.random.fold_in(key, 15)
    base = jax.random.normal(key, (CLASSES, COEF, COEF), dtype=jnp.float32)
    scales = degree_scales()
    factor = scales[:, None] * scales[None, :] / math.sqrt(COEF)
    return base * factor[None]


def draw_m2m_ops(key, part):
    key = jax.random.fold_in(key, 16)
    base = jax.random.normal(key, (8, COEF, COEF), dtype=jnp.float32)
    scales = degree_scales()
    factor = scales[None, :] / scales[:, None] / math.sqrt(8 * COEF)
    return base * factor[None]


def set_ends(values, stream_key, low, high):
    place = [jax.random.randint(jax.random.fold_in(stream_key, axis), (), 0, length) for axis, length in enumerate(values.shape)]
    main_axis = values.shape.index(max(values.shape))
    neighbour = place[:main_axis] + [(place[main_axis] + 1) % values.shape[main_axis]] + place[main_axis + 1:]
    return values.at[tuple(place)].set(low).at[tuple(neighbour)].set(high)


def split_up(count, total, reach, slope):
    weights = [(1 << 20) // math.isqrt(grade ** slope) + 1 for grade in range(2, count + 1)]
    spare, given = total - reach - (count - 1), [1] * (count - 1)
    while spare > 0:
        movable = [i for i in range(count - 1) if given[i] < reach]
        mass, remaining = sum([weights[i] for i in movable]), spare
        for i in movable:
            extra = min(reach - given[i], max(1, remaining * weights[i] // mass), spare)
            given[i] = given[i] + extra
            spare = spare - extra
    return np.array([reach] + given)


def ragged(key, number_of, total, most, lean):
    if number_of == 2:
        one = jax.random.randint(key, (), max(1, total - most), min(most, total - 1) + 1)
        return jnp.stack([one, total - one])
    tallies = jnp.asarray(split_up(number_of, total, most, lean), jnp.int32)
    couples = (number_of - 1) // 2
    donor, taker = tallies[1:1 + 2 * couples:2], tallies[2:2 + 2 * couples:2]
    margin = jnp.minimum(donor - 1, most - taker)
    passed = jax.random.randint(jax.random.fold_in(key, 1), (couples,), 0, 1 << 20) % (margin + 1)
    tallies = tallies.at[1:1 + 2 * couples:2].set(donor - passed).at[2:2 + 2 * couples:2].set(taker + passed)
    return tallies[jax.random.permutation(jax.random.fold_in(key, 2), number_of)]


def setup_inputs(seed: int = 0) -> dict:
    key_of = jax.random.split(jax.random.key(seed), 11)
    return {
        "particles": draw_particles(jax.random.fold_in(key_of[10], 71), 0),
        "counts": draw_counts(jax.random.fold_in(key_of[10], 71), 0),
        "leaf_top": jnp.searchsorted(jnp.cumsum(ragged(key_of[2], TOPBOX, LEAVES_TOTAL, TOP_MOST, 2)), jnp.arange(LEAVES_TOTAL), side="right").astype(jnp.int32),
        "near_list": draw_near_list(jax.random.fold_in(key_of[10], 71), 0),
        "leaf_list": draw_leaf_list(jax.random.fold_in(key_of[10], 71), 0),
        "leaf_class": set_ends(jax.random.randint(key_of[5], (LEAVES_TOTAL, LLIST), 0, CLASSES), jax.random.fold_in(key_of[5], 1), 0, CLASSES - 1).astype(jnp.int32),
        "top_list": set_ends(jax.random.randint(key_of[6], (TOPBOX, TLIST), 0, TOPBOX), jax.random.fold_in(key_of[6], 1), 0, TOPBOX - 1).astype(jnp.int32),
        "top_class": set_ends(jax.random.randint(key_of[7], (TOPBOX, TLIST), 0, CLASSES), jax.random.fold_in(key_of[7], 1), 0, CLASSES - 1).astype(jnp.int32),
        "m2l_ops": draw_m2l_ops(jax.random.fold_in(key_of[10], 71), 0),
        "m2m_ops": draw_m2m_ops(jax.random.fold_in(key_of[10], 71), 0),
    }


SOFTENING = 0.01
HIGH = lax.Precision.HIGHEST

def harmonics(offset):
    coord_x, coord_y, coord_z = (offset[0], offset[1], offset[2])
    radius_sq = coord_x * coord_x + coord_y * coord_y + coord_z * coord_z
    zeros_like = jnp.zeros_like(coord_x)
    solid_terms = {(0, 0): (jnp.ones_like(coord_x), zeros_like)}
    for order_m in range(1, ORDER + 1):
        real_part, imag_part = solid_terms[order_m - 1, order_m - 1]
        solid_terms[order_m, order_m] = ((coord_x * real_part - coord_y * imag_part) / (2.0 * order_m), (coord_x * imag_part + coord_y * real_part) / (2.0 * order_m))
    for order_m in range(ORDER):
        real_part, imag_part = solid_terms[order_m, order_m]
        solid_terms[order_m + 1, order_m] = (coord_z * real_part, coord_z * imag_part)
    for order_m in range(ORDER - 1):
        for degree in range(order_m + 2, ORDER + 1):
            factor_one = (2.0 * degree - 1.0) / ((degree - order_m) * (degree + order_m))
            factor_two = 1.0 / ((degree - order_m) * (degree + order_m))
            upper_one = solid_terms[degree - 1, order_m]
            upper_two = solid_terms[degree - 2, order_m]
            solid_terms[degree, order_m] = (factor_one * coord_z * upper_one[0] - factor_two * radius_sq * upper_two[0], factor_one * coord_z * upper_one[1] - factor_two * radius_sq * upper_two[1])
    stacked = []
    for degree in range(ORDER + 1):
        stacked.append(solid_terms[degree, 0][0])
        for order_m in range(1, degree + 1):
            stacked.append(solid_terms[degree, order_m][0])
            stacked.append(solid_terms[degree, order_m][1])
    return jnp.stack(stacked, 0)

def expand(points, leaf_count):
    grid = points.reshape(4, leaf_count, PART)
    center = lax.optimization_barrier(jnp.mean(grid[:3], axis=2, keepdims=True))
    solid = harmonics(grid[:3] - center)
    return (solid, lax.optimization_barrier(jnp.sum(solid * grid[3][None], axis=2)))

def translate(sources, classes, m2l_ops):
    onehot = (classes[..., None] == jnp.arange(m2l_ops.shape[0], dtype=jnp.int32)).astype(jnp.float32)
    grouped = jnp.einsum('jbk,bkc->cjb', sources, onehot, precision=HIGH)
    return jnp.einsum('cij,cjb->ib', m2l_ops, grouped, precision=HIGH)

def lift(m2m_ops, field):
    width = field.shape[1]
    shaped = field.reshape(field.shape[0], width // 8, 8)
    return jnp.einsum('aij,jba->iba', m2m_ops, shaped, precision=HIGH).reshape(-1, width)

def lower(m2m_ops, field):
    width = field.shape[1]
    shaped = field.reshape(field.shape[0], width // 8, 8)
    return jnp.einsum('aji,jba->iba', m2m_ops, shaped, precision=HIGH).reshape(-1, width)

def near_sum(own_grid, index, source_grid):
    leaf_count = index.shape[0]
    block_size = min(32, leaf_count)
    block_count = leaf_count // block_size
    targets = own_grid[:3].reshape(3, block_count, block_size, PART).transpose(1, 0, 2, 3)
    chosen = index.reshape(block_count, block_size, -1)

    def one_block(item):
        points, picked = item
        flat = source_grid[:, picked].reshape(4, block_size, -1)
        dist_sq = (points[0][:, :, None] - flat[0][:, None, :]) ** 2
        dist_sq = dist_sq + (points[1][:, :, None] - flat[1][:, None, :]) ** 2
        dist_sq = dist_sq + (points[2][:, :, None] - flat[2][:, None, :]) ** 2
        return lax.optimization_barrier(jnp.sum(flat[3][:, None, :] * lax.rsqrt(dist_sq + SOFTENING), axis=2))
    return lax.map(one_block, (targets, chosen)).reshape(leaf_count, PART)

def reference(particles, counts, leaf_top, near_list, leaf_list, leaf_class, top_list, top_class, m2l_ops, m2m_ops):
    total = counts.shape[0]
    slot_mask = (jnp.arange(PART, dtype=jnp.int32)[None, :] < counts[:, None]).astype(jnp.float32)
    masked = jnp.concatenate([particles[:3], particles[3:] * slot_mask.reshape(1, -1)], 0)
    groups = total // LEAVES_DEV
    pieces = masked.reshape(4, groups, LEAVES_DEV * PART).transpose(1, 0, 2)
    moments = lax.map(lambda piece: expand(piece, LEAVES_DEV)[1], pieces)
    moments = moments.transpose(1, 0, 2).reshape(COEF, total)
    lifted = lift(m2m_ops, moments)
    box_moments = jax.ops.segment_sum(lifted.T, leaf_top, num_segments=TOPBOX).T
    top_blocks = TOPBOX // TOP_DEV

    def box_block(item):
        lists, classes = item
        return translate(box_moments[:, lists], classes, m2l_ops)
    box_locals = lax.map(box_block, (top_list.reshape(top_blocks, TOP_DEV, TLIST), top_class.reshape(top_blocks, TOP_DEV, TLIST)))
    box_locals = box_locals.transpose(1, 0, 2).reshape(COEF, TOPBOX)
    source_grid = masked.reshape(4, total, PART)

    def leaf_block(item):
        piece, near_rows, leaf_rows, classes, tops, masks = item
        solid, unused = expand(piece, LEAVES_DEV)
        local = translate(moments[:, leaf_rows], classes, m2l_ops) + lower(m2m_ops, box_locals[:, tops])
        far_field = lax.optimization_barrier(jnp.sum(solid * local[:, :, None], axis=0))
        near_field = near_sum(piece.reshape(4, LEAVES_DEV, PART), near_rows, source_grid)
        return (near_field + far_field) * masks
    result = lax.map(leaf_block, (pieces, near_list.reshape(groups, LEAVES_DEV, NEAR), leaf_list.reshape(groups, LEAVES_DEV, LLIST), leaf_class.reshape(groups, LEAVES_DEV, LLIST), leaf_top.reshape(groups, LEAVES_DEV), slot_mask.reshape(groups, LEAVES_DEV, PART)))
    return result.reshape(-1)
```

```python
import functools

import jax
import jax.numpy as jnp
from jax import lax
from jax.experimental import pallas as pl
from jax.experimental.pallas import tpu as pltpu
from jax.sharding import Mesh, PartitionSpec as P

ORDER = 8
COEF = 81
PART = 64
LEAVES = 256
PAIRS = 128
HALO = 32
HPAIRS = 16
WPAIRS = PAIRS + 2 * HPAIRS
NEAR = 27
LLIST = 16
TLIST = 64
TOPBOX = 4096
CLASS_BITS = 9
SOFTENING = 0.01
SEND = 56
REACH_SQ = 16.0
FEAT = 32
NEAR_PARTS = 2

HIGH = lax.Precision.HIGHEST
MIB = 1 << 20
AXES = ("zlo", "core", "y", "x", "zhi")

NN = (((1,), (0,)), ((), ()))
NT = (((1,), (1,)), ((), ()))


def dot_f32(left, right, dims=NN):
    return lax.dot_general(left, right, dims, precision=HIGH, preferred_element_type=jnp.float32)


def lanes(shape):
    return lax.broadcasted_iota(jnp.int32, shape, len(shape) - 1)


def rows_of(shape):
    return lax.broadcasted_iota(jnp.int32, shape, len(shape) - 2)


def harmonics(coord_x, coord_y, coord_z):
    radius_sq = coord_x * coord_x + coord_y * coord_y + coord_z * coord_z
    terms = {(0, 0): (None, None)}
    for m in range(1, ORDER + 1):
        if m == 1:
            terms[1, 1] = (coord_x * 0.5, coord_y * 0.5)
            continue
        re, im = terms[m - 1, m - 1]
        scale = 1.0 / (2.0 * m)
        terms[m, m] = (
            (coord_x * re - coord_y * im) * scale,
            (coord_x * im + coord_y * re) * scale,
        )
    for m in range(ORDER):
        re, im = terms[m, m]
        terms[m + 1, m] = (coord_z, None) if m == 0 else (coord_z * re, coord_z * im)
    for m in range(ORDER - 1):
        for n in range(m + 2, ORDER + 1):
            one = (2.0 * n - 1.0) / ((n - m) * (n + m))
            two = 1.0 / ((n - m) * (n + m))
            z_one = coord_z * one
            r_two = radius_sq * two
            upper, lower = terms[n - 1, m], terms[n - 2, m]
            re = z_one * upper[0] - (r_two if lower[0] is None else r_two * lower[0])
            im = None if m == 0 else z_one * upper[1] - r_two * lower[1]
            terms[n, m] = (re, im)
    listed = []
    for n in range(ORDER + 1):
        listed.append(terms[n, 0][0])
        for m in range(1, n + 1):
            listed.extend(terms[n, m])
    return listed


def centred(block):
    turned = block.T
    halves = []
    for p in range(2):
        half = turned[p * PART : (p + 1) * PART]
        halves.append(half - jnp.sum(half, axis=0, keepdims=True) * (1.0 / PART))
    return jnp.concatenate(halves, axis=0)


def expand_into(d_ref, q_ref, acc_ref, out_ref):
    out_ref[...] = jnp.zeros_like(out_ref)
    for p in range(2):
        acc_ref[...] = jnp.zeros_like(acc_ref)

        def step(s, carry):
            at = pl.ds(pl.multiple_of(p * PART + s * 16, 16), 16)
            charge = q_ref[at, :]
            listed = harmonics(d_ref[0, at, :], d_ref[1, at, :], d_ref[2, at, :])
            for c, term in enumerate(listed):
                value = charge if term is None else charge * term
                acc_ref[c] += value[:8] + value[8:]
            return carry

        lax.fori_loop(0, PART // 16, step, 0)
        sums = jnp.sum(acc_ref[...], axis=1)
        full = jnp.concatenate([sums, jnp.zeros((128 - COEF, 128), jnp.float32)], axis=0)
        out_ref[p] = full.T


def slot_mask_rows(count_ref):
    lane = lanes((PAIRS, 128))
    held = jnp.where(lane < PART, count_ref[:, 0:1], count_ref[:, 1:2])
    return jnp.where((lane & (PART - 1)) < held, 1.0, 0.0)


def first_kernel(
    pts_ref, count_ref, top_ref, ends_ref, m2m_ref,
    own_ref, low_ref, high_ref, dist_ref, moment_ref, part_ref, q_ref, acc_ref,
):
    charge = pts_ref[3] * slot_mask_rows(count_ref)
    for c in range(3):
        own_ref[c] = pts_ref[c]
        dist_ref[c] = centred(pts_ref[c])
    own_ref[3] = charge
    for c in range(4):
        low_ref[c] = own_ref[c, :HPAIRS]
        high_ref[c] = own_ref[c, PAIRS - HPAIRS :]
    q_ref[...] = charge.T
    expand_into(dist_ref, q_ref, acc_ref, moment_ref)
    first, last = ends_ref[0], ends_ref[1]
    row = rows_of((PAIRS, COEF))
    total = jnp.zeros((LEAVES, COEF), jnp.float32)
    for p in range(2):
        moment = moment_ref[p][:, :COEF]
        lifted = jnp.zeros((PAIRS, COEF), jnp.float32)
        for u in range(4):
            lifted += dot_f32(jnp.where((row & 3) == u, moment, 0.0), m2m_ref[2 * u + p], NT)
        held = jnp.where(rows_of((LEAVES, PAIRS)) == top_ref[p : p + 1, :] - first, 1.0, 0.0)
        total += dot_f32(held, lifted)
    wide = jnp.concatenate([total, jnp.zeros((LEAVES, 128 - COEF), jnp.float32)], axis=1)
    lane = lanes((LEAVES, 128))
    wide = jnp.where(lane == 127, first.astype(jnp.float32), wide)
    wide = jnp.where(lane == 126, last.astype(jnp.float32), wide)
    part_ref[...] = wide


def split3(value):
    high = value.astype(jnp.bfloat16).astype(jnp.float32)
    rest = value - high
    middle = rest.astype(jnp.bfloat16).astype(jnp.float32)
    low = (rest - middle).astype(jnp.bfloat16).astype(jnp.float32)
    return high, middle, low


def near_kernel(
    part, near_ref, win_ref, out_ref, src_ref, tgt_ref, table_ref, charge_ref,
):
    targets = PAIRS // NEAR_PARTS
    width = targets + 2 * HPAIRS
    base = part * targets
    at = pl.ds(base, width)
    points = [win_ref[c, at, :] for c in range(3)]
    moved = []
    for c in range(3):
        least = jnp.min(points[c], keepdims=True)
        most = jnp.max(points[c], keepdims=True)
        moved.append(points[c] - 0.5 * (least + most))
    norm = moved[0] * moved[0] + moved[1] * moved[1] + moved[2] * moved[2]
    close = jnp.max(norm) <= REACH_SQ

    @pl.when(close)
    def _():
        own = slice(HPAIRS, HPAIRS + targets)
        src_ref[...] = jnp.zeros_like(src_ref)
        tgt_ref[...] = jnp.zeros_like(tgt_ref)
        for c in range(3):
            h, m, l = split3(moved[c])
            for i, feature in enumerate((h, h, m, m, h, l)):
                src_ref[pl.ds(6 * c + i, width, stride=FEAT), :] = feature
            th, tm, tl = [-2.0 * piece[own] for piece in (h, m, l)]
            for i, feature in enumerate((th, tm, th, tm, tl, th)):
                tgt_ref[pl.ds(6 * c + i, targets, stride=FEAT), :] = feature
        ones = jnp.ones((width, 128), jnp.float32)
        for i, feature in enumerate(split3(norm + SOFTENING)):
            src_ref[pl.ds(18 + i, width, stride=FEAT), :] = feature
            tgt_ref[pl.ds(18 + i, targets, stride=FEAT), :] = ones[own]
        for i, feature in enumerate(split3(norm[own])):
            src_ref[pl.ds(21 + i, width, stride=FEAT), :] = ones
            tgt_ref[pl.ds(21 + i, targets, stride=FEAT), :] = feature
        for i, feature in enumerate(split3(win_ref[3, at, :])):
            src_ref[pl.ds(24 + i, width, stride=FEAT), :] = feature

        row = rows_of((128, 256))
        lane = lanes((128, 256))
        spread = []
        for p in range(4):
            local = row - FEAT * p
            same = (lane < 128) & (local < 24) & (local == (lane & (FEAT - 1)))
            charge = (lane >= 128) & (local >= 24) & (local < 27)
            spread.append(jnp.where(same | charge, 1.0, 0.0).astype(jnp.bfloat16))

        def build(g, carry):
            turned = src_ref[pl.ds(pl.multiple_of(g * 128, 128), 128), :].T.astype(jnp.bfloat16)
            for p in range(4):
                both = lax.dot_general(turned, spread[p], NN, preferred_element_type=jnp.float32)
                to = pl.ds(pl.multiple_of((g * 4 + p) * 128, 128), 128)
                table_ref[to, :] = both[:, :128].astype(jnp.bfloat16)
                charge_ref[to, :] = both[:, 128:]
            return carry

        lax.fori_loop(0, width // 4, build, 0)

        lane_w = lanes((FEAT, 128))
        lane_b = lanes((PART, 128))
        low_half = lane_b < PART
        start = 2 * base

        def group(g, carry):
            two = tgt_ref[pl.ds(pl.multiple_of(g * 2 * FEAT, 2 * FEAT), 2 * FEAT), :]
            zero = jnp.zeros((FEAT, 128), jnp.float32)
            left, right = [], []
            for half in range(2):
                one = two[half * FEAT : (half + 1) * FEAT]
                low = jnp.where(lane_w < PART, one, 0.0)
                high = jnp.where(lane_w < PART, 0.0, one)
                left += [low, high] if half == 0 else [zero, zero]
                right += [zero, zero] if half == 0 else [low, high]
            weights = jnp.concatenate(
                [jnp.concatenate(left, axis=0), jnp.concatenate(right, axis=0)], axis=1
            ).astype(jnp.bfloat16)

            def one_entry(k, total):
                spots = []
                for v in range(4):
                    leaf = near_ref[(start + g * 4 + v) * NEAR + k] - start
                    spots.append(pl.ds(pl.multiple_of(leaf * PART, PART), PART))
                rows = [table_ref[spot, :] for spot in spots]
                mixed = jnp.where(
                    lane_b < 2 * FEAT,
                    jnp.where(lane_b < FEAT, rows[0], rows[1]),
                    jnp.where(lane_b < 3 * FEAT, rows[2], rows[3]),
                )
                dist = lax.dot_general(mixed, weights, NN, preferred_element_type=jnp.float32)
                inverse = lax.rsqrt(dist)
                sums = []
                for half in range(2):
                    charge = jnp.where(
                        low_half, charge_ref[spots[2 * half], :], charge_ref[spots[2 * half + 1], :]
                    )
                    term = charge * inverse[:, half * 128 : (half + 1) * 128]
                    sums.append(jnp.sum(term.reshape(8, 8, 128), axis=0))
                return total[0] + sums[0], total[1] + sums[1]

            def entries(k, total):
                for i in range(3):
                    total = one_entry(k * 3 + i, total)
                return total

            zeros = jnp.zeros((8, 128), jnp.float32)
            total = lax.fori_loop(0, NEAR // 3, entries, (zeros, zeros))
            both = jnp.concatenate([jnp.sum(t, axis=0, keepdims=True) for t in total], axis=0)
            out_ref[pl.ds(g * 2, 2), :] = both
            return carry

        lax.fori_loop(0, targets // 2, group, 0)

    @pl.when(jnp.logical_not(close))
    def _():
        lane = lanes((PART, 128))

        def pair(r, carry):
            columns = [
                jnp.broadcast_to(win_ref[c, pl.ds(base + HPAIRS + r, 1), :], (128, 128)).T
                for c in range(3)
            ]
            results = []
            for p in range(2):
                mine = [column[p * PART : (p + 1) * PART] for column in columns]

                def entry(k, total):
                    leaf = near_ref[(2 * (base + r) + p) * NEAR + k]
                    at = pl.ds(leaf // 2, 1)
                    gap = SOFTENING
                    for c in range(3):
                        diff = mine[c] - win_ref[c, at, :]
                        gap = gap + diff * diff
                    half = jnp.where((lane // PART) == leaf % 2, 1.0, 0.0)
                    return total + half * (win_ref[3, at, :] * lax.rsqrt(gap))

                total = lax.fori_loop(0, NEAR, entry, jnp.zeros((PART, 128), jnp.float32))
                results.append(jnp.sum(total, axis=1, keepdims=True))
            wide = jnp.broadcast_to(jnp.concatenate(results, axis=0), (128, 128)).T
            out_ref[pl.ds(r, 1), :] = wide[:1]
            return carry

        lax.fori_loop(0, targets, pair, 0)


def gather_products(codes, m2l_ref, rows_ref):
    total = None
    for code in codes:
        at = pl.ds(code >> CLASS_BITS, 1)
        term = m2l_ref[code & ((1 << CLASS_BITS) - 1)] * rows_ref[at, :][:, :COEF]
        total = term if total is None else total + term
    return total


def leaf_kernel(
    code_ref, m2l_ref, moment_ref, low_ref, high_ref, out_ref,
    rows_ref, d_ref, q_ref, acc_ref, halo_ref,
):
    fill = jnp.zeros((PAIRS - 2 * HPAIRS, 128), jnp.float32)
    for c in range(3):
        d_ref[c] = centred(jnp.concatenate([low_ref[c], high_ref[c], fill], axis=0))
    q_ref[...] = jnp.concatenate([low_ref[3], high_ref[3], fill], axis=0).T
    expand_into(d_ref, q_ref, acc_ref, halo_ref)
    for p in range(2):
        at = p * WPAIRS
        rows_ref[at : at + HPAIRS] = halo_ref[p, :HPAIRS]
        rows_ref[at + HPAIRS : at + HPAIRS + PAIRS] = moment_ref[p]
        rows_ref[at + HPAIRS + PAIRS : at + WPAIRS] = halo_ref[p, HPAIRS : 2 * HPAIRS]
    lane = lanes((COEF, 128))
    for p in range(2):

        def leaf(r, wide):
            spot = (2 * r + p) * LLIST
            total = gather_products([code_ref[spot + k] for k in range(LLIST)], m2l_ref, rows_ref)
            return jnp.where(lane == r, jnp.sum(total, axis=1, keepdims=True), wide)

        out_ref[p] = lax.fori_loop(0, PAIRS, leaf, jnp.zeros((COEF, 128), jnp.float32))


def finish(
    cap, info_ref, code_ref, table_ref, m2l_ref, m2m_ref, top_ref, local_ref, dist_ref,
    near_refs, count_ref, out_ref, field_ref, pot_ref,
):
    first, shift, boxes = info_ref[0], info_ref[1], info_ref[2]
    lane = lanes((COEF, 128))
    spread = [jnp.zeros((PAIRS, COEF), jnp.float32) for _ in range(2)]
    for block in range((cap + 127) // 128):

        def box(b, wide):
            row = block * 128 + b + shift

            def some(i, total):
                codes = [code_ref[row, i * 16 + k] for k in range(16)]
                return total + gather_products(codes, m2l_ref, table_ref)

            total = lax.fori_loop(0, TLIST // 16, some, jnp.zeros((COEF, COEF), jnp.float32))
            return jnp.where(lane == b, jnp.sum(total, axis=1, keepdims=True), wide)

        count = jnp.clip(boxes - block * 128, 0, 128)
        wide = lax.fori_loop(0, count, box, jnp.zeros((COEF, 128), jnp.float32))
        for p in range(2):
            held = lanes((PAIRS, 128)) + block * 128 == top_ref[p * PAIRS : (p + 1) * PAIRS] - first
            spread[p] += dot_f32(jnp.where(held, 1.0, 0.0), wide, NT)
    row = rows_of((PAIRS, COEF))
    for p in range(2):
        lowered = jnp.zeros((PAIRS, COEF), jnp.float32)
        for u in range(4):
            lowered += dot_f32(jnp.where((row & 3) == u, spread[p], 0.0), m2m_ref[2 * u + p])
        full = jnp.concatenate([lowered, jnp.zeros((PAIRS, 128 - COEF), jnp.float32)], axis=1)
        field_ref[p] = full.T[:COEF] + local_ref[p]
    for p in range(2):

        def step(s, carry):
            at = pl.ds(pl.multiple_of(p * PART + s * 16, 16), 16)
            listed = harmonics(dist_ref[0, at, :], dist_ref[1, at, :], dist_ref[2, at, :])
            total = None
            for c, term in enumerate(listed):
                weight = field_ref[p, pl.ds(c, 1), :]
                value = jnp.broadcast_to(weight, (16, 128)) if term is None else term * weight
                total = value if total is None else total + value
            pot_ref[at, :] = total
            return carry

        lax.fori_loop(0, PART // 16, step, 0)
    near = jnp.concatenate([ref[...] for ref in near_refs], axis=0)
    out_ref[...] = (near + pot_ref[...].T) * slot_mask_rows(count_ref)


def last_kernel(
    info_ref, code_ref, mine_ref, other_ref, m2l_ref, m2m_ref, top_ref, local_ref, dist_ref,
    near_a_ref, near_b_ref, count_ref, out_ref, over_ref, table_ref, field_ref, pot_ref,
):
    core, my_y, my_x, my_z = info_ref[3], info_ref[4], info_ref[5], info_ref[6]
    table_ref[0:1, :] = jnp.zeros((1, 128), jnp.float32)
    over_ref[0] = 0

    def assemble(ref, zlo):
        def step(i, carry):
            y, x, zhi = i // 8, (i // 2) % 4, i % 2
            block = ((my_z - (zlo * 2 + zhi)) & 3) * 16 + ((my_x - x) & 3) * 4 + ((my_y - y) & 3)
            at = pl.multiple_of(block * SEND, 8)
            ends = ref[pl.ds(at, 1), :]
            begin = ends[0, 127].astype(jnp.int32)
            end = ends[0, 126].astype(jnp.int32)
            over_ref[0] = jnp.maximum(over_ref[0], end - begin + 1)
            so_far = table_ref[pl.ds(begin, 1), :]
            table_ref[pl.ds(begin, SEND), :] = ref[pl.ds(at, SEND), :]
            table_ref[pl.ds(begin, 1), :] = ends + so_far
            return carry

        lax.fori_loop(0, 32, step, 0)

    for zlo in range(2):
        for side in range(2):

            @pl.when(core == side)
            def _():
                assemble(mine_ref, zlo)

            @pl.when(core != side)
            def _():
                assemble(other_ref, zlo)

    @pl.when(over_ref[0] < SEND)
    def _():
        finish(
            64, info_ref, code_ref, table_ref, m2l_ref, m2m_ref, top_ref, local_ref, dist_ref,
            (near_a_ref, near_b_ref), count_ref, out_ref, field_ref, pot_ref,
        )


def spare_kernel(
    info_ref, code_ref, table_ref, m2l_ref, m2m_ref, top_ref, local_ref, dist_ref,
    near_a_ref, near_b_ref, count_ref, out_ref, field_ref, pot_ref,
):
    finish(
        LEAVES, info_ref, code_ref, table_ref, m2l_ref, m2m_ref, top_ref, local_ref, dist_ref,
        (near_a_ref, near_b_ref), count_ref, out_ref, field_ref, pot_ref,
    )


SMEM = pl.BlockSpec(memory_space=pltpu.SMEM)
VMEM = pl.BlockSpec(memory_space=pltpu.VMEM)
F32 = jnp.float32


def shape(*dims):
    return jax.ShapeDtypeStruct(dims, F32)


def call_first(pts, count, top2, ends, m2m_ops):
    return pl.pallas_call(
        first_kernel,
        out_shape=(
            shape(4, PAIRS, 128), shape(4, HPAIRS, 128), shape(4, HPAIRS, 128),
            shape(3, PAIRS, 128), shape(2, PAIRS, 128), shape(LEAVES, 128),
        ),
        in_specs=[VMEM, VMEM, VMEM, SMEM, VMEM],
        out_specs=(VMEM,) * 6,
        scratch_shapes=[pltpu.VMEM((128, 128), F32), pltpu.VMEM((COEF, 8, 128), F32)],
        compiler_params=pltpu.CompilerParams(vmem_limit_bytes=16 * MIB),
        cost_estimate=pl.CostEstimate(flops=10**9, bytes_accessed=10**7, transcendentals=0),
        name="expand_own",
    )(pts, count, top2, ends, m2m_ops)


def call_near(part, near, window):
    targets = PAIRS // NEAR_PARTS
    width = targets + 2 * HPAIRS
    return pl.pallas_call(
        functools.partial(near_kernel, part),
        out_shape=shape(targets, 128),
        in_specs=[SMEM, VMEM],
        out_specs=VMEM,
        scratch_shapes=[
            pltpu.VMEM((width * FEAT, 128), F32),
            pltpu.VMEM((targets * FEAT, 128), F32),
            pltpu.VMEM((width * 128, 128), jnp.bfloat16),
            pltpu.VMEM((width * 128, 128), F32),
        ],
        compiler_params=pltpu.CompilerParams(vmem_limit_bytes=24 * MIB),
        cost_estimate=pl.CostEstimate(
            flops=10 * targets * 2 * 64 * NEAR * 64, bytes_accessed=3 * 10**7,
            transcendentals=targets * 2 * 64 * NEAR * 64,
        ),
        name="near",
    )(near, window)


def call_leaf(code, m2l_ops, moments, low, high):
    return pl.pallas_call(
        leaf_kernel,
        out_shape=shape(2, COEF, 128),
        in_specs=[SMEM] + [VMEM] * 4,
        out_specs=VMEM,
        scratch_shapes=[
            pltpu.VMEM((2 * WPAIRS, 128), F32),
            pltpu.VMEM((3, 128, 128), F32),
            pltpu.VMEM((128, 128), F32),
            pltpu.VMEM((COEF, 8, 128), F32),
            pltpu.VMEM((2, 128, 128), F32),
        ],
        compiler_params=pltpu.CompilerParams(vmem_limit_bytes=24 * MIB),
        cost_estimate=pl.CostEstimate(
            flops=2 * LEAVES * LLIST * COEF * COEF * 8, bytes_accessed=3 * 10**7, transcendentals=0
        ),
        name="leaf_translate",
    )(code, m2l_ops, moments, low, high)


def call_last(info, code, mine, other, *rest):
    return pl.pallas_call(
        last_kernel,
        out_shape=(shape(PAIRS, 128), jax.ShapeDtypeStruct((1,), jnp.int32)),
        in_specs=[SMEM, SMEM] + [VMEM] * 10,
        out_specs=(VMEM, SMEM),
        scratch_shapes=[
            pltpu.VMEM((TOPBOX + SEND, 128), F32),
            pltpu.VMEM((2, COEF, 128), F32),
            pltpu.VMEM((128, 128), F32),
        ],
        compiler_params=pltpu.CompilerParams(vmem_limit_bytes=32 * MIB),
        name="finish",
    )(info, code, mine, other, *rest)


def call_spare(info, code, table, *rest):
    return pl.pallas_call(
        spare_kernel,
        out_shape=shape(PAIRS, 128),
        in_specs=[SMEM, SMEM] + [VMEM] * 9,
        out_specs=VMEM,
        scratch_shapes=[pltpu.VMEM((2, COEF, 128), F32), pltpu.VMEM((128, 128), F32)],
        compiler_params=pltpu.CompilerParams(vmem_limit_bytes=32 * MIB),
        name="finish_spare",
    )(info, code, table, *rest)


def spread_over(block, axis, count):
    pieces = [block]
    for s in range(1, count):
        pieces.append(lax.ppermute(block, axis, [(i, (i + s) % count) for i in range(count)]))
    return jnp.concatenate(pieces, axis=0)


def prepare(particles, counts, leaf_top, near_list, leaf_list, leaf_class, my_index):
    pts = particles.reshape(4, PAIRS, 128)
    count = counts.reshape(PAIRS, 2)
    top2 = leaf_top.reshape(PAIRS, 2).T
    ends = jnp.stack([leaf_top[0], leaf_top[LEAVES - 1]])
    before = my_index * LEAVES - HALO
    near = (near_list - before).reshape(-1)
    spot = leaf_list - before
    code = ((((spot & 1) * WPAIRS + (spot >> 1)) << CLASS_BITS) | leaf_class).reshape(-1)
    return pts, count, top2, ends, near, code


def top_codes(top_list, top_class, first, cap):
    start = jnp.minimum(first, TOPBOX - cap)
    rows = lax.dynamic_slice_in_dim(top_list, start, cap, axis=0)
    classes = lax.dynamic_slice_in_dim(top_class, start, cap, axis=0)
    return (rows << CLASS_BITS) | classes, first - start


def body(
    particles, counts, leaf_top, near_list, leaf_list, leaf_class, top_list, top_class,
    m2l_ops, m2m_ops,
):
    my_index = lax.axis_index(AXES)
    pts, count, top2, ends, near, code = prepare(
        particles, counts, leaf_top, near_list, leaf_list, leaf_class, my_index
    )
    own, low, high, dist, moments, partial = call_first(pts, count, top2, ends, m2m_ops)
    devices = lax.axis_size(AXES)
    up = [(i, i + 1) for i in range(devices - 1)]
    down = [(j, i) for i, j in up]
    before = lax.ppermute(high, AXES, up)
    after = lax.ppermute(low, AXES, down)
    window = jnp.concatenate([before, own, after], axis=1)

    gathered = spread_over(partial[:SEND], "y", 4)
    near_a = call_near(0, near, window)
    gathered, window = lax.optimization_barrier((gathered, window))
    gathered = spread_over(gathered, "x", 4)
    near_b = call_near(1, near, window)
    gathered = spread_over(gathered, ("zlo", "zhi"), 4)
    local = call_leaf(code, m2l_ops, moments, before, after)
    other = lax.ppermute(gathered, "core", [(0, 1), (1, 0)])

    first, boxes = ends[0], ends[1] - ends[0] + 1
    place = [
        lax.axis_index("core"), lax.axis_index("y"), lax.axis_index("x"),
        lax.axis_index(("zlo", "zhi")),
    ]

    def info_of(shift):
        return jnp.stack([first, shift, boxes, *place]).astype(jnp.int32)

    top_column = top2.reshape(LEAVES, 1)
    rest = (m2l_ops, m2m_ops, top_column, local, dist, near_a, near_b, count)
    top_code, shift = top_codes(top_list, top_class, first, 64)
    result, over = call_last(info_of(shift), top_code, gathered, other, *rest)

    def spare():
        table = lax.dynamic_update_slice(
            jnp.zeros((TOPBOX + LEAVES, 128), F32), partial, (first, 0)
        )
        table = lax.psum(table, AXES)
        wide_code, wide_shift = top_codes(top_list, top_class, first, LEAVES)
        return call_spare(info_of(wide_shift), wide_code, table, *rest)

    result = lax.cond(over[0] >= SEND, spare, lambda: result)
    return result.reshape(-1)


def solution(mesh):
    fine = Mesh(mesh.devices.reshape(2, 2, 4, 4, 2), AXES)
    return jax.shard_map(
        body,
        mesh=fine,
        in_specs=(
            P(None, AXES), P(AXES), P(AXES), P(AXES, None), P(AXES, None), P(AXES, None),
            P(), P(), P(), P(),
        ),
        out_specs=P(AXES),
        check_vma=False,
    )
```

```python
import functools

import jax
import jax.numpy as jnp
from jax import lax
from jax.experimental import pallas as pl
from jax.experimental.pallas import tpu as pltpu
from jax.sharding import Mesh, PartitionSpec as P

ORDER = 8
COEF = 81
PART = 64
LEAVES = 256
PAIRS = 128
HALO = 32
HPAIRS = 16
WPAIRS = PAIRS + 2 * HPAIRS
NEAR = 27
LLIST = 16
TLIST = 64
TOPBOX = 4096
ROW_BITS = 12
CLASSES = 316
OPROWS = 88
SOFTENING = 0.01
SEND = 56
REACH_SQ = 16.0
FEAT = 32
LEAF_STEP = 4
TURN_STEP = 3
TOP_WINDOW = 256

HIGH = lax.Precision.HIGHEST
MIB = 1 << 20
AXES = ("zlo", "core", "y", "x", "zhi")

NN = (((1,), (0,)), ((), ()))
NT = (((1,), (1,)), ((), ()))


def dot_f32(left, right, dims=NN):
    return lax.dot_general(left, right, dims, precision=HIGH, preferred_element_type=jnp.float32)


def lanes(shape):
    return lax.broadcasted_iota(jnp.int32, shape, len(shape) - 1)


def rows_of(shape):
    return lax.broadcasted_iota(jnp.int32, shape, len(shape) - 2)


def harmonics(coord_x, coord_y, coord_z):
    radius_sq = coord_x * coord_x + coord_y * coord_y + coord_z * coord_z
    terms = {(0, 0): (None, None)}
    for m in range(1, ORDER + 1):
        if m == 1:
            terms[1, 1] = (coord_x * 0.5, coord_y * 0.5)
            continue
        re, im = terms[m - 1, m - 1]
        scale = 1.0 / (2.0 * m)
        terms[m, m] = (
            (coord_x * re - coord_y * im) * scale,
            (coord_x * im + coord_y * re) * scale,
        )
    for m in range(ORDER):
        re, im = terms[m, m]
        terms[m + 1, m] = (coord_z, None) if m == 0 else (coord_z * re, coord_z * im)
    for m in range(ORDER - 1):
        for n in range(m + 2, ORDER + 1):
            one = (2.0 * n - 1.0) / ((n - m) * (n + m))
            two = 1.0 / ((n - m) * (n + m))
            z_one = coord_z * one
            r_two = radius_sq * two
            upper, lower = terms[n - 1, m], terms[n - 2, m]
            re = z_one * upper[0] - (r_two if lower[0] is None else r_two * lower[0])
            im = None if m == 0 else z_one * upper[1] - r_two * lower[1]
            terms[n, m] = (re, im)
    listed = []
    for n in range(ORDER + 1):
        listed.append(terms[n, 0][0])
        for m in range(1, n + 1):
            listed.extend(terms[n, m])
    return listed


def centred(block):
    turned = block.T
    halves = []
    for p in range(2):
        half = turned[p * PART : (p + 1) * PART]
        halves.append(half - jnp.sum(half, axis=0, keepdims=True) * (1.0 / PART))
    return jnp.concatenate(halves, axis=0)


def expand_into(d_ref, q_ref, acc_ref, out_ref):
    for p in range(2):
        acc_ref[...] = jnp.zeros_like(acc_ref)

        def step(s, carry):
            at = pl.ds(pl.multiple_of(p * PART + s * 16, 16), 16)
            charge = q_ref[at, :]
            listed = harmonics(d_ref[0, at, :], d_ref[1, at, :], d_ref[2, at, :])
            for c, term in enumerate(listed):
                value = charge if term is None else charge * term
                acc_ref[c] += value[:8] + value[8:]
            return carry

        lax.fori_loop(0, PART // 16, step, 0)
        sums = jnp.sum(acc_ref[...], axis=1)
        full = jnp.concatenate([sums, jnp.zeros((128 - COEF, 128), jnp.float32)], axis=0)
        out_ref[pl.ds(p, PAIRS, stride=2), :] = full.T


def widen(block):
    return jnp.concatenate(
        [block, jnp.zeros((block.shape[0], 128 - block.shape[1]), jnp.float32)], axis=1
    )


def first_kernel(
    pts_ref, count_ref, top_ref, tops_ref, m2m_ref,
    own_ref, low_ref, high_ref, dist_ref, moment_ref, send_ref, part_ref, mask_ref,
    q_ref, acc_ref, lift_ref,
):
    lane = lanes((1, 128))

    def hold(i, carry):
        for u in range(8):
            r = i * 8 + u
            held = jnp.where(lane < PART, count_ref[2 * r], count_ref[2 * r + 1])
            mask_ref[pl.ds(r, 1), :] = jnp.where((lane & (PART - 1)) < held, 1.0, 0.0)
        return carry

    lax.fori_loop(0, PAIRS // 8, hold, 0)
    charge = pts_ref[pl.ds(3, PAIRS, stride=4), :] * mask_ref[...]
    own_ref[...] = pts_ref[...]
    own_ref[pl.ds(3, PAIRS, stride=4), :] = charge
    low_ref[...] = own_ref[: 4 * HPAIRS]
    high_ref[...] = own_ref[4 * (PAIRS - HPAIRS) :]
    for c in range(3):
        dist_ref[c] = centred(pts_ref[pl.ds(c, PAIRS, stride=4), :])
    q_ref[...] = charge.T
    expand_into(dist_ref, q_ref, acc_ref, moment_ref)
    first, last = top_ref[0], top_ref[LEAVES - 1]
    for a in range(8):
        at = pl.ds(a, LEAVES // 8, stride=8)
        lift_ref[at, :] = widen(dot_f32(moment_ref[at, :][:, :COEF], m2m_ref[:, a, :], NT))
    held = jnp.where(rows_of((LEAVES, LEAVES)) == tops_ref[...] - first, 1.0, 0.0)
    wide = dot_f32(held, lift_ref[...])
    lane = lanes((LEAVES, 128))
    wide = jnp.where(lane == 127, first.astype(jnp.float32), wide)
    wide = jnp.where(lane == 126, last.astype(jnp.float32), wide)
    part_ref[...] = wide
    send_ref[...] = wide[:SEND]


def turn_kernel(in_ref, after_ref, out_ref):
    del after_ref

    def step(i, carry):
        for u in range(TURN_STEP):
            one = in_ref[i * TURN_STEP + u]
            for begin in range(0, CLASSES, 128):
                count = min(128, CLASSES - begin)
                at = pl.ds(begin * OPROWS + i * TURN_STEP + u, count, stride=OPROWS)
                out_ref[at, :] = widen(one[:, begin : begin + count].T)
        return carry

    lax.fori_loop(0, COEF // TURN_STEP, step, 0)


def join_kernel(*refs):
    out_ref = refs[-1]
    rows = refs[0].shape[0]
    for i, ref in enumerate(refs[:4]):
        out_ref[i * rows : (i + 1) * rows] = ref[...]


def split3(value):
    high = value.astype(jnp.bfloat16).astype(jnp.float32)
    rest = value - high
    middle = rest.astype(jnp.bfloat16).astype(jnp.float32)
    low = (rest - middle).astype(jnp.bfloat16).astype(jnp.float32)
    return high, middle, low


def near_kernel(
    near_ref, own_ref, before_ref, behind_ref, after_ref, out_ref,
    win_ref, src_ref, tgt_ref, table_ref, charge_ref,
):
    del after_ref
    targets, width = PAIRS, WPAIRS
    edge = 4 * HPAIRS
    win_ref[:edge] = before_ref[...]
    win_ref[edge : edge + 4 * PAIRS] = own_ref[...]
    win_ref[edge + 4 * PAIRS :] = behind_ref[...]
    shift = lax.axis_index(AXES) * LEAVES - HALO

    def component(c):
        return win_ref[pl.ds(c, width, stride=4), :]

    points = [component(c) for c in range(3)]
    moved = []
    for c in range(3):
        least = jnp.min(points[c], keepdims=True)
        most = jnp.max(points[c], keepdims=True)
        moved.append(points[c] - 0.5 * (least + most))
    norm = moved[0] * moved[0] + moved[1] * moved[1] + moved[2] * moved[2]
    close = jnp.max(norm) <= REACH_SQ

    @pl.when(close)
    def _():
        own = slice(HPAIRS, HPAIRS + targets)
        src_ref[...] = jnp.zeros_like(src_ref)
        tgt_ref[...] = jnp.zeros_like(tgt_ref)
        for c in range(3):
            h, m, l = split3(moved[c])
            for i, feature in enumerate((h, h, m, m, h, l)):
                src_ref[pl.ds(6 * c + i, width, stride=FEAT), :] = feature
            th, tm, tl = [-2.0 * piece[own] for piece in (h, m, l)]
            for i, feature in enumerate((th, tm, th, tm, tl, th)):
                tgt_ref[pl.ds(6 * c + i, targets, stride=FEAT), :] = feature
        ones = jnp.ones((width, 128), jnp.float32)
        for i, feature in enumerate(split3(norm + SOFTENING)):
            src_ref[pl.ds(18 + i, width, stride=FEAT), :] = feature
            tgt_ref[pl.ds(18 + i, targets, stride=FEAT), :] = ones[own]
        for i, feature in enumerate(split3(norm[own])):
            src_ref[pl.ds(21 + i, width, stride=FEAT), :] = ones
            tgt_ref[pl.ds(21 + i, targets, stride=FEAT), :] = feature
        for i, feature in enumerate(split3(component(3))):
            src_ref[pl.ds(24 + i, width, stride=FEAT), :] = feature

        row = rows_of((128, 256))
        lane = lanes((128, 256))
        spread = []
        for p in range(4):
            local = row - FEAT * p
            same = (lane < 128) & (local < 24) & (local == (lane & (FEAT - 1)))
            charge = (lane >= 128) & (local >= 24) & (local < 27)
            spread.append(jnp.where(same | charge, 1.0, 0.0).astype(jnp.bfloat16))

        def build(i, carry):
            for g in (2 * i, 2 * i + 1):
                block = src_ref[pl.ds(pl.multiple_of(g * 128, 128), 128), :]
                turned = block.T.astype(jnp.bfloat16)
                for p in range(4):
                    both = lax.dot_general(
                        turned, spread[p], NN, preferred_element_type=jnp.float32
                    )
                    to = pl.ds(pl.multiple_of((g * 4 + p) * 128, 128), 128)
                    table_ref[to, :] = both[:, :128].astype(jnp.bfloat16)
                    charge_ref[to, :] = both[:, 128:]
            return carry

        lax.fori_loop(0, width // 8, build, 0)

        lane_w = lanes((FEAT, 128))
        lane_b = lanes((PART, 128))
        low_half = lane_b < PART
        def group(g, carry):
            two = tgt_ref[pl.ds(pl.multiple_of(g * 2 * FEAT, 2 * FEAT), 2 * FEAT), :]
            zero = jnp.zeros((FEAT, 128), jnp.float32)
            left, right = [], []
            for half in range(2):
                one = two[half * FEAT : (half + 1) * FEAT]
                low = jnp.where(lane_w < PART, one, 0.0)
                high = jnp.where(lane_w < PART, 0.0, one)
                left += [low, high] if half == 0 else [zero, zero]
                right += [zero, zero] if half == 0 else [low, high]
            weights = jnp.concatenate(
                [jnp.concatenate(left, axis=0), jnp.concatenate(right, axis=0)], axis=1
            ).astype(jnp.bfloat16)
            mixed, spots = [], []
            for k in range(NEAR):
                four = []
                for v in range(4):
                    leaf = near_ref[k, g * 4 + v] - shift
                    four.append(pl.ds(pl.multiple_of(leaf * PART, PART), PART))
                rows = [table_ref[spot, :] for spot in four]
                mixed.append(
                    jnp.where(
                        lane_b < 2 * FEAT,
                        jnp.where(lane_b < FEAT, rows[0], rows[1]),
                        jnp.where(lane_b < 3 * FEAT, rows[2], rows[3]),
                    )
                )
                spots.append(four)
            total = [jnp.zeros((8, 128), jnp.float32)] * 2
            for some in range(0, NEAR, 14):
                count = min(14, NEAR - some)
                dist = lax.dot_general(
                    jnp.concatenate(mixed[some : some + count], axis=0), weights, NN,
                    preferred_element_type=jnp.float32,
                )
                for k in range(count):
                    inverse = lax.rsqrt(dist[k * PART : (k + 1) * PART])
                    for half in range(2):
                        low, high = spots[some + k][2 * half : 2 * half + 2]
                        charge = jnp.where(low_half, charge_ref[low, :], charge_ref[high, :])
                        term = charge * inverse[:, half * 128 : (half + 1) * 128]
                        total[half] += jnp.sum(term.reshape(8, 8, 128), axis=0)
            both = jnp.concatenate([jnp.sum(t, axis=0, keepdims=True) for t in total], axis=0)
            out_ref[pl.ds(g * 2, 2), :] = both
            return carry

        lax.fori_loop(0, targets // 2, group, 0)

    @pl.when(jnp.logical_not(close))
    def _():
        lane = lanes((PART, 128))

        def pair(r, carry):
            columns = [
                jnp.broadcast_to(
                    win_ref[pl.ds(4 * (HPAIRS + r) + c, 1), :], (128, 128)
                ).T
                for c in range(3)
            ]
            results = []
            for p in range(2):
                mine = [column[p * PART : (p + 1) * PART] for column in columns]

                def entry(k, total):
                    leaf = near_ref[k, 2 * r + p] - shift
                    at = 4 * (leaf // 2)
                    gap = SOFTENING
                    for c in range(3):
                        diff = mine[c] - win_ref[pl.ds(at + c, 1), :]
                        gap = gap + diff * diff
                    half = jnp.where((lane // PART) == leaf % 2, 1.0, 0.0)
                    return total + half * (win_ref[pl.ds(at + 3, 1), :] * lax.rsqrt(gap))

                total = lax.fori_loop(0, NEAR, entry, jnp.zeros((PART, 128), jnp.float32))
                results.append(jnp.sum(total, axis=1, keepdims=True))
            wide = jnp.broadcast_to(jnp.concatenate(results, axis=0), (128, 128)).T
            out_ref[pl.ds(r, 1), :] = wide[:1]
            return carry

        lax.fori_loop(0, targets, pair, 0)


def gather_products(codes, ops_ref, rows_ref):
    total = None
    for code in codes:
        at = pl.ds(pl.multiple_of(code >> ROW_BITS, 8), OPROWS)
        row = rows_ref[pl.ds(code & ((1 << ROW_BITS) - 1), 1), :]
        term = ops_ref[at, :] * row
        total = term if total is None else total + term
    return total


def pack_codes(kinds, rows):
    return ((kinds * OPROWS) << ROW_BITS) | rows


def put_sums(total_ref, out_ref, lane):
    sums = jnp.sum(total_ref[...], axis=1, keepdims=True)
    out_ref[...] = jnp.where(lanes((OPROWS, 128)) == lane, sums, out_ref[...])


def halo_kernel(
    list_ref, class_ref, moment_ref, before_ref, behind_ref, code_ref, rows_ref,
    d_ref, q_ref, acc_ref, halo_ref,
):
    shift = lax.axis_index(AXES) * LEAVES - HALO
    code_ref[...] = pack_codes(class_ref[...], list_ref[...] - shift)
    fill = jnp.zeros((PAIRS - 2 * HPAIRS, 128), jnp.float32)

    def component(c):
        at = pl.ds(c, HPAIRS, stride=4)
        return jnp.concatenate([before_ref[at, :], behind_ref[at, :], fill], axis=0)

    for c in range(3):
        d_ref[c] = centred(component(c))
    q_ref[...] = component(3).T
    expand_into(d_ref, q_ref, acc_ref, halo_ref)
    rows_ref[:HALO] = halo_ref[:HALO]
    rows_ref[HALO : HALO + LEAVES] = moment_ref[...]
    rows_ref[HALO + LEAVES :] = halo_ref[HALO : 2 * HALO]


def leaf_kernel(part, code_ref, ops_ref, rows_ref, after_ref, out_ref, total_ref):
    del after_ref
    begin = part * (PAIRS // 2)

    def reduce(i):
        for v in range(LEAF_STEP):
            put_sums(total_ref.at[v], out_ref.at[v & 1], begin + 2 * i + (v >> 1))

    def step(i, carry):
        reduce(i - 1)
        for v in range(LEAF_STEP):
            leaf = 2 * begin + i * LEAF_STEP + v
            total_ref[v] = gather_products(
                [code_ref[k, leaf] for k in range(LLIST)], ops_ref, rows_ref
            )
        return carry

    total_ref[...] = jnp.zeros_like(total_ref)
    out_ref[...] = jnp.zeros_like(out_ref)
    steps = LEAVES // 2 // LEAF_STEP
    lax.fori_loop(0, steps, step, 0)
    reduce(steps - 1)


def fetch_kernel(top_ref, list_ref, class_ref, code_ref, list_vmem, class_vmem, sems):
    at = pl.ds(pl.multiple_of(window_start(top_ref), 128), TOP_WINDOW)
    copies = [
        pltpu.make_async_copy(list_ref.at[:, at], list_vmem, sems.at[0]),
        pltpu.make_async_copy(class_ref.at[:, at], class_vmem, sems.at[1]),
    ]
    for copy in copies:
        copy.start()
    for copy in copies:
        copy.wait()
    code_ref[...] = pack_codes(class_vmem[...], list_vmem[...])


def window_start(top_ref):
    return jnp.minimum(top_ref[0] // 128 * 128, TOPBOX - TOP_WINDOW)


def finish(
    cap, begin, top_ref, code_ref, table_ref, ops_ref, m2m_ref, tops_ref, local_refs, dist_ref,
    near_ref, mask_ref, out_ref, field_ref, pot_ref, total_ref, wide_ref, rows_ref,
):
    first = top_ref[0]
    boxes = top_ref[LEAVES - 1] - first + 1
    spread = jnp.zeros((OPROWS, LEAVES), jnp.float32)
    width = min(cap, 128)
    for block in range(cap // width):
        total_ref[...] = jnp.zeros_like(total_ref)
        wide_ref[...] = jnp.zeros_like(wide_ref)

        def step(b, carry):
            put_sums(total_ref, wide_ref, b - 1)
            column = first - begin + block * width + b
            total_ref[...] = gather_products(
                [code_ref[k, column] for k in range(TLIST)], ops_ref, table_ref
            )
            return carry

        count = jnp.clip(boxes - block * width, 0, width)
        lax.fori_loop(0, count, step, 0)
        put_sums(total_ref, wide_ref, count - 1)
        place = rows_of((128, LEAVES)) + block * width
        held = jnp.where(place == tops_ref[...] - first, 1.0, 0.0)
        spread += dot_f32(wide_ref[...], held)
    full = jnp.concatenate([spread, jnp.zeros((128 - OPROWS, LEAVES), jnp.float32)], axis=0)
    rows_ref[...] = full.T
    for a in range(8):
        at = pl.ds(a, LEAVES // 8, stride=8)
        rows_ref[at, :] = widen(dot_f32(rows_ref[at, :][:, :COEF], m2m_ref[:, a, :]))
    for p in range(2):
        field_ref[p] = (
            rows_ref[pl.ds(p, PAIRS, stride=2), :].T[:OPROWS]
            + local_refs[0][p] + local_refs[1][p]
        )
    for p in range(2):

        def step(s, carry):
            at = pl.ds(pl.multiple_of(p * PART + s * 16, 16), 16)
            listed = harmonics(dist_ref[0, at, :], dist_ref[1, at, :], dist_ref[2, at, :])
            total = None
            for c, term in enumerate(listed):
                weight = field_ref[p, pl.ds(c, 1), :]
                value = jnp.broadcast_to(weight, (16, 128)) if term is None else term * weight
                total = value if total is None else total + value
            pot_ref[at, :] = total
            return carry

        lax.fori_loop(0, PART // 16, step, 0)
    out_ref[...] = (near_ref[...] + pot_ref[...].T) * mask_ref[...]


def last_kernel(
    top_ref, code_ref, mine_ref, other_ref, ops_ref, m2m_ref, tops_ref, local_a_ref, local_b_ref,
    dist_ref, near_ref, mask_ref, out_ref, over_ref, table_ref, *scratch,
):
    core, my_y, my_x = lax.axis_index("core"), lax.axis_index("y"), lax.axis_index("x")
    my_z = lax.axis_index(("zlo", "zhi"))
    table_ref[0:1, :] = jnp.zeros((1, 128), jnp.float32)
    over_ref[0] = 0

    def assemble(ref, zlo):
        def step(i, carry):
            y, x, zhi = i // 8, (i // 2) % 4, i % 2
            block = ((my_z - (zlo * 2 + zhi)) & 3) * 16 + ((my_x - x) & 3) * 4 + ((my_y - y) & 3)
            at = pl.multiple_of(block * SEND, 8)
            ends = ref[pl.ds(at, 1), :]
            begin = ends[0, 127].astype(jnp.int32)
            end = ends[0, 126].astype(jnp.int32)
            over_ref[0] = jnp.maximum(over_ref[0], end - begin + 1)
            so_far = table_ref[pl.ds(begin, 1), :]
            table_ref[pl.ds(begin, SEND), :] = ref[pl.ds(at, SEND), :]
            table_ref[pl.ds(begin, 1), :] = ends + so_far
            return carry

        lax.fori_loop(0, 32, step, 0)

    for zlo in range(2):
        for side in range(2):

            @pl.when(core == side)
            def _():
                assemble(mine_ref, zlo)

            @pl.when(core != side)
            def _():
                assemble(other_ref, zlo)

    @pl.when(over_ref[0] < SEND)
    def _():
        finish(
            64, window_start(top_ref), top_ref, code_ref, table_ref, ops_ref, m2m_ref, tops_ref,
            (local_a_ref, local_b_ref), dist_ref, near_ref, mask_ref, out_ref, *scratch,
        )


def spare_kernel(
    top_ref, code_ref, table_ref, ops_ref, m2m_ref, tops_ref, local_a_ref, local_b_ref,
    dist_ref, near_ref, mask_ref, out_ref, *scratch,
):
    finish(
        LEAVES, jnp.minimum(top_ref[0], TOPBOX - LEAVES), top_ref, code_ref, table_ref, ops_ref, m2m_ref, tops_ref,
        (local_a_ref, local_b_ref), dist_ref, near_ref, mask_ref, out_ref, *scratch,
    )


SMEM = pl.BlockSpec(memory_space=pltpu.SMEM)
VMEM = pl.BlockSpec(memory_space=pltpu.VMEM)
F32 = jnp.float32


def shape(*dims):
    return jax.ShapeDtypeStruct(dims, F32)


ANY = pl.BlockSpec(memory_space=pl.ANY)
FINISH_SCRATCH = [
    pltpu.VMEM((2, OPROWS, 128), F32),
    pltpu.VMEM((128, 128), F32),
    pltpu.VMEM((OPROWS, 128), F32),
    pltpu.VMEM((OPROWS, 128), F32),
    pltpu.VMEM((LEAVES, 128), F32),
]


def cost(flops, bytes_accessed):
    return pl.CostEstimate(flops=flops, bytes_accessed=bytes_accessed, transcendentals=0)


def call_first(pts, counts, leaf_top, tops, m2m):
    return pl.pallas_call(
        first_kernel,
        out_shape=(
            shape(4 * PAIRS, 128), shape(4 * HPAIRS, 128), shape(4 * HPAIRS, 128),
            shape(3, PAIRS, 128), shape(LEAVES, 128), shape(SEND, 128), shape(LEAVES, 128),
            shape(PAIRS, 128),
        ),
        in_specs=[VMEM, SMEM, SMEM, VMEM, VMEM],
        out_specs=(VMEM,) * 8,
        scratch_shapes=[
            pltpu.VMEM((128, 128), F32), pltpu.VMEM((COEF, 8, 128), F32),
            pltpu.VMEM((LEAVES, 128), F32),
        ],
        compiler_params=pltpu.CompilerParams(vmem_limit_bytes=16 * MIB),
        cost_estimate=cost(10**9, 10**7),
        name="expand_own",
    )(pts, counts, leaf_top, tops, m2m)


def call_turn(ops, after):
    return pl.pallas_call(
        turn_kernel,
        out_shape=shape(CLASSES * OPROWS, 128),
        in_specs=[VMEM, ANY],
        out_specs=VMEM,
        compiler_params=pltpu.CompilerParams(vmem_limit_bytes=30 * MIB),
        cost_estimate=cost(10**7, 3 * 10**7),
        name="turn_operators",
    )(ops, after)


def call_join(pieces, *after):
    rows = pieces[0].shape[0]
    return pl.pallas_call(
        join_kernel,
        out_shape=shape(4 * rows, 128),
        in_specs=[VMEM] * 4 + [ANY] * len(after),
        out_specs=VMEM,
        compiler_params=pltpu.CompilerParams(vmem_limit_bytes=8 * MIB),
        cost_estimate=cost(10**5, 8 * rows * 512),
        name="join",
    )(*pieces, *after)


def call_near(near, own, before, behind, after):
    targets, width = PAIRS, WPAIRS
    return pl.pallas_call(
        near_kernel,
        out_shape=shape(targets, 128),
        in_specs=[SMEM, VMEM, VMEM, VMEM, ANY],
        out_specs=VMEM,
        scratch_shapes=[
            pltpu.VMEM((4 * WPAIRS, 128), F32),
            pltpu.VMEM((width * FEAT, 128), F32),
            pltpu.VMEM((targets * FEAT, 128), F32),
            pltpu.VMEM((width * 128, 128), jnp.bfloat16),
            pltpu.VMEM((width * 128, 128), F32),
        ],
        compiler_params=pltpu.CompilerParams(vmem_limit_bytes=30 * MIB),
        cost_estimate=cost(10 * targets * 2 * 64 * NEAR * 64, 3 * 10**7),
        name="near",
    )(near, own, before, behind, after)


def call_halo(lists, classes, moments, before, behind):
    return pl.pallas_call(
        halo_kernel,
        out_shape=(jax.ShapeDtypeStruct((LLIST, LEAVES), jnp.int32), shape(2 * WPAIRS, 128)),
        in_specs=[VMEM] * 5,
        out_specs=(VMEM, VMEM),
        scratch_shapes=[
            pltpu.VMEM((3, 128, 128), F32),
            pltpu.VMEM((128, 128), F32),
            pltpu.VMEM((COEF, 8, 128), F32),
            pltpu.VMEM((LEAVES, 128), F32),
        ],
        compiler_params=pltpu.CompilerParams(vmem_limit_bytes=16 * MIB),
        cost_estimate=cost(10**8, 10**6),
        name="expand_halo",
    )(lists, classes, moments, before, behind)


def call_leaf(part, code, ops, rows, after):
    return pl.pallas_call(
        functools.partial(leaf_kernel, part),
        out_shape=shape(2, OPROWS, 128),
        in_specs=[SMEM, VMEM, VMEM, ANY],
        out_specs=VMEM,
        scratch_shapes=[pltpu.VMEM((LEAF_STEP, OPROWS, 128), F32)],
        compiler_params=pltpu.CompilerParams(vmem_limit_bytes=24 * MIB),
        cost_estimate=cost(LEAVES * LLIST * COEF * COEF * 8, 2 * 10**7),
        name="leaf_translate",
    )(code, ops, rows, after)


def call_fetch(leaf_top, lists, classes):
    window = (TLIST, TOP_WINDOW)
    return pl.pallas_call(
        fetch_kernel,
        out_shape=jax.ShapeDtypeStruct(window, jnp.int32),
        in_specs=[SMEM, ANY, ANY],
        out_specs=VMEM,
        scratch_shapes=[
            pltpu.VMEM(window, jnp.int32), pltpu.VMEM(window, jnp.int32),
            pltpu.SemaphoreType.DMA((2,)),
        ],
        compiler_params=pltpu.CompilerParams(vmem_limit_bytes=8 * MIB),
        cost_estimate=cost(10**5, 10**5),
        name="fetch_lists",
    )(leaf_top, lists, classes)


def call_last(leaf_top, code, mine, other, *rest):
    return pl.pallas_call(
        last_kernel,
        out_shape=(shape(PAIRS, 128), jax.ShapeDtypeStruct((1,), jnp.int32)),
        in_specs=[SMEM, SMEM] + [VMEM] * 10,
        out_specs=(VMEM, SMEM),
        scratch_shapes=[pltpu.VMEM((TOPBOX + SEND, 128), F32)] + FINISH_SCRATCH,
        compiler_params=pltpu.CompilerParams(vmem_limit_bytes=32 * MIB),
        name="finish",
    )(leaf_top, code, mine, other, *rest)


def call_spare(leaf_top, code, table, *rest):
    return pl.pallas_call(
        spare_kernel,
        out_shape=shape(PAIRS, 128),
        in_specs=[SMEM, SMEM] + [VMEM] * 9,
        out_specs=VMEM,
        scratch_shapes=FINISH_SCRATCH,
        compiler_params=pltpu.CompilerParams(vmem_limit_bytes=32 * MIB),
        name="finish_spare",
    )(leaf_top, code, table, *rest)


def sent_over(block, axis, count):
    return [block] + [
        lax.ppermute(block, axis, [(i, (i + s) % count) for i in range(count)])
        for s in range(1, count)
    ]


def body(
    particles, counts, leaf_top, near_list, leaf_list, leaf_class, top_list, top_class,
    m2l_ops, m2m_ops,
):
    pts = particles.reshape(4, PAIRS, 128).transpose(1, 0, 2).reshape(4 * PAIRS, 128)
    tops = leaf_top.reshape(1, LEAVES)
    m2m = m2m_ops.transpose(1, 0, 2)
    own, low, high, dist, moments, send, partial, mask = call_first(
        pts, counts, leaf_top, tops, m2m
    )
    devices = lax.axis_size(AXES)
    up = [(i, (i + 1) % devices) for i in range(devices)]
    down = [(j, i) for i, j in up]
    over_y = sent_over(send, "y", 4)
    before = lax.ppermute(high, AXES, up)
    behind = lax.ppermute(low, AXES, down)
    ops = call_turn(m2l_ops.transpose(1, 2, 0), send)
    by_y = call_join(over_y, ops, before, behind)
    over_x = sent_over(by_y, "x", 4)
    near = call_near(near_list.T, own, before, behind, by_y)
    by_x = call_join(over_x, near)
    over_z = sent_over(by_x, ("zlo", "zhi"), 4)
    code, rows = call_halo(leaf_list.T, leaf_class.T, moments, before, behind)
    local_a = call_leaf(0, code, ops, rows, by_x)
    mine = call_join(over_z, local_a)
    other = lax.ppermute(mine, "core", [(0, 1), (1, 0)])
    local_b = call_leaf(1, code, ops, rows, mine)
    top_code = call_fetch(leaf_top, top_list.T, top_class.T)
    rest = (ops, m2m, tops, local_a, local_b, dist, near, mask)
    result, over = call_last(leaf_top, top_code, mine, other, *rest)

    def spare():
        table = lax.dynamic_update_slice(
            jnp.zeros((TOPBOX + LEAVES, 128), F32), partial, (leaf_top[0], 0)
        )
        for k in range(7):
            swap = [(i, i ^ (1 << k)) for i in range(devices)]
            table = table + lax.ppermute(table, AXES, swap)
        start = jnp.minimum(leaf_top[0], TOPBOX - LEAVES)
        lists, classes = (
            lax.dynamic_slice_in_dim(x, start, LEAVES, axis=0).T for x in (top_list, top_class)
        )
        return call_spare(leaf_top, pack_codes(classes, lists), table, *rest)

    result = lax.cond(over[0] >= SEND, spare, lambda: result)
    return result.reshape(-1)


def solution(mesh):
    fine = Mesh(mesh.devices.reshape(2, 2, 4, 4, 2), AXES)
    return jax.shard_map(
        body,
        mesh=fine,
        in_specs=(
            P(None, AXES), P(AXES), P(AXES), P(AXES, None), P(AXES, None), P(AXES, None),
            P(), P(), P(), P(),
        ),
        out_specs=P(AXES),
        check_vma=False,
    )
```

```python
import functools

import jax
import jax.numpy as jnp
from jax import lax
from jax.experimental import pallas as pl
from jax.experimental.pallas import tpu as pltpu
from jax.sharding import Mesh, PartitionSpec as P

ORDER = 8
COEF = 81
PART = 64
LEAVES = 256
PAIRS = 128
HALO = 32
HPAIRS = 16
WPAIRS = PAIRS + 2 * HPAIRS
NEAR = 27
LLIST = 16
TLIST = 64
TOPBOX = 4096
ROW_BITS = 13
CLASSES = 316
OPROWS = 88
SOFTENING = 0.01
SEND = 56
REACH_SQ = 16.0
FEAT = 32
LEAF_STEP = 4
TURN_STEP = 3
TOP_WINDOW = 256

HIGH = lax.Precision.HIGHEST
MIB = 1 << 20
AXES = ("zlo", "core", "y", "x", "zhi")

NN = (((1,), (0,)), ((), ()))
NT = (((1,), (1,)), ((), ()))


def dot_f32(left, right, dims=NN):
    return lax.dot_general(left, right, dims, precision=HIGH, preferred_element_type=jnp.float32)


def lanes(shape):
    return lax.broadcasted_iota(jnp.int32, shape, len(shape) - 1)


def rows_of(shape):
    return lax.broadcasted_iota(jnp.int32, shape, len(shape) - 2)


def harmonics(coord_x, coord_y, coord_z):
    radius_sq = coord_x * coord_x + coord_y * coord_y + coord_z * coord_z
    terms = {(0, 0): (None, None)}
    for m in range(1, ORDER + 1):
        if m == 1:
            terms[1, 1] = (coord_x * 0.5, coord_y * 0.5)
            continue
        re, im = terms[m - 1, m - 1]
        scale = 1.0 / (2.0 * m)
        terms[m, m] = (
            (coord_x * re - coord_y * im) * scale,
            (coord_x * im + coord_y * re) * scale,
        )
    for m in range(ORDER):
        re, im = terms[m, m]
        terms[m + 1, m] = (coord_z, None) if m == 0 else (coord_z * re, coord_z * im)
    for m in range(ORDER - 1):
        for n in range(m + 2, ORDER + 1):
            one = (2.0 * n - 1.0) / ((n - m) * (n + m))
            two = 1.0 / ((n - m) * (n + m))
            z_one = coord_z * one
            r_two = radius_sq * two
            upper, lower = terms[n - 1, m], terms[n - 2, m]
            re = z_one * upper[0] - (r_two if lower[0] is None else r_two * lower[0])
            im = None if m == 0 else z_one * upper[1] - r_two * lower[1]
            terms[n, m] = (re, im)
    listed = []
    for n in range(ORDER + 1):
        listed.append(terms[n, 0][0])
        for m in range(1, n + 1):
            listed.extend(terms[n, m])
    return listed


def centred(block):
    turned = block.T
    halves = []
    for p in range(2):
        half = turned[p * PART : (p + 1) * PART]
        halves.append(half - jnp.sum(half, axis=0, keepdims=True) * (1.0 / PART))
    return jnp.concatenate(halves, axis=0)


def expand_into(d_ref, q_ref, acc_ref, out_ref):
    for p in range(2):
        acc_ref[...] = jnp.zeros_like(acc_ref)

        def step(s, carry):
            at = pl.ds(pl.multiple_of(p * PART + s * 16, 16), 16)
            charge = q_ref[at, :]
            listed = harmonics(d_ref[0, at, :], d_ref[1, at, :], d_ref[2, at, :])
            for c, term in enumerate(listed):
                value = charge if term is None else charge * term
                acc_ref[c] += value[:8] + value[8:]
            return carry

        lax.fori_loop(0, PART // 16, step, 0)
        sums = jnp.sum(acc_ref[...], axis=1)
        full = jnp.concatenate([sums, jnp.zeros((128 - COEF, 128), jnp.float32)], axis=0)
        out_ref[pl.ds(p, PAIRS, stride=2), :] = full.T


def widen(block):
    return jnp.concatenate(
        [block, jnp.zeros((block.shape[0], 128 - block.shape[1]), jnp.float32)], axis=1
    )


def first_kernel(
    pts_ref, count_ref, top_ref, tops_ref, m2m_ref,
    own_ref, low_ref, high_ref, dist_ref, moment_ref, send_ref, part_ref, mask_ref,
    q_ref, acc_ref, lift_ref,
):
    lane = lanes((1, 128))

    def hold(i, carry):
        for u in range(8):
            r = i * 8 + u
            held = jnp.where(lane < PART, count_ref[2 * r], count_ref[2 * r + 1])
            mask_ref[pl.ds(r, 1), :] = jnp.where((lane & (PART - 1)) < held, 1.0, 0.0)
        return carry

    lax.fori_loop(0, PAIRS // 8, hold, 0)
    charge = pts_ref[pl.ds(3, PAIRS, stride=4), :] * mask_ref[...]
    own_ref[...] = pts_ref[...]
    own_ref[pl.ds(3, PAIRS, stride=4), :] = charge
    low_ref[...] = own_ref[: 4 * HPAIRS]
    high_ref[...] = own_ref[4 * (PAIRS - HPAIRS) :]
    for c in range(3):
        dist_ref[c] = centred(pts_ref[pl.ds(c, PAIRS, stride=4), :])
    q_ref[...] = charge.T
    expand_into(dist_ref, q_ref, acc_ref, moment_ref)
    first, last = top_ref[0], top_ref[LEAVES - 1]
    for a in range(8):
        at = pl.ds(a, LEAVES // 8, stride=8)
        lift_ref[at, :] = widen(dot_f32(moment_ref[at, :][:, :COEF], m2m_ref[:, a, :], NT))
    held = jnp.where(rows_of((LEAVES, LEAVES)) == tops_ref[...] - first, 1.0, 0.0)
    wide = dot_f32(held, lift_ref[...])
    lane = lanes((LEAVES, 128))
    wide = jnp.where(lane == 127, first.astype(jnp.float32), wide)
    wide = jnp.where(lane == 126, last.astype(jnp.float32), wide)
    part_ref[...] = wide
    send_ref[...] = wide[:SEND]


def turn_kernel(in_ref, after_ref, out_ref):
    del after_ref

    def step(i, carry):
        for u in range(TURN_STEP):
            one = in_ref[i * TURN_STEP + u]
            for begin in range(0, CLASSES, 128):
                count = min(128, CLASSES - begin)
                at = pl.ds(begin * OPROWS + i * TURN_STEP + u, count, stride=OPROWS)
                out_ref[at, :] = widen(one[:, begin : begin + count].T)
        return carry

    lax.fori_loop(0, COEF // TURN_STEP, step, 0)


def join_kernel(*refs):
    out_ref = refs[-1]
    rows = refs[0].shape[0]
    for i, ref in enumerate(refs[:4]):
        out_ref[i * rows : (i + 1) * rows] = ref[...]


def split3(value):
    high = value.astype(jnp.bfloat16).astype(jnp.float32)
    rest = value - high
    middle = rest.astype(jnp.bfloat16).astype(jnp.float32)
    low = (rest - middle).astype(jnp.bfloat16).astype(jnp.float32)
    return high, middle, low


def near_kernel(
    near_ref, own_ref, before_ref, behind_ref, after_ref, out_ref,
    win_ref, src_ref, tgt_ref, table_ref, charge_ref,
):
    del after_ref
    targets, width = PAIRS, WPAIRS
    edge = 4 * HPAIRS
    win_ref[:edge] = before_ref[...]
    win_ref[edge : edge + 4 * PAIRS] = own_ref[...]
    win_ref[edge + 4 * PAIRS :] = behind_ref[...]
    shift = lax.axis_index(AXES) * LEAVES - HALO

    def component(c):
        return win_ref[pl.ds(c, width, stride=4), :]

    points = [component(c) for c in range(3)]
    moved = []
    for c in range(3):
        least = jnp.min(points[c], keepdims=True)
        most = jnp.max(points[c], keepdims=True)
        moved.append(points[c] - 0.5 * (least + most))
    norm = moved[0] * moved[0] + moved[1] * moved[1] + moved[2] * moved[2]
    close = jnp.max(norm) <= REACH_SQ

    @pl.when(close)
    def _():
        own = slice(HPAIRS, HPAIRS + targets)
        src_ref[...] = jnp.zeros_like(src_ref)
        tgt_ref[...] = jnp.zeros_like(tgt_ref)
        for c in range(3):
            h, m, l = split3(moved[c])
            for i, feature in enumerate((h, h, m, m, h, l)):
                src_ref[pl.ds(6 * c + i, width, stride=FEAT), :] = feature
            th, tm, tl = [-2.0 * piece[own] for piece in (h, m, l)]
            for i, feature in enumerate((th, tm, th, tm, tl, th)):
                tgt_ref[pl.ds(6 * c + i, targets, stride=FEAT), :] = feature
        ones = jnp.ones((width, 128), jnp.float32)
        for i, feature in enumerate(split3(norm + SOFTENING)):
            src_ref[pl.ds(18 + i, width, stride=FEAT), :] = feature
            tgt_ref[pl.ds(18 + i, targets, stride=FEAT), :] = ones[own]
        for i, feature in enumerate(split3(norm[own])):
            src_ref[pl.ds(21 + i, width, stride=FEAT), :] = ones
            tgt_ref[pl.ds(21 + i, targets, stride=FEAT), :] = feature
        for i, feature in enumerate(split3(component(3))):
            src_ref[pl.ds(24 + i, width, stride=FEAT), :] = feature

        row = rows_of((128, 256))
        lane = lanes((128, 256))
        spread = []
        for p in range(4):
            local = row - FEAT * p
            same = (lane < 128) & (local < 24) & (local == (lane & (FEAT - 1)))
            charge = (lane >= 128) & (local >= 24) & (local < 27)
            spread.append(jnp.where(same | charge, 1.0, 0.0).astype(jnp.bfloat16))

        def build(i, carry):
            for g in (2 * i, 2 * i + 1):
                block = src_ref[pl.ds(pl.multiple_of(g * 128, 128), 128), :]
                turned = block.T.astype(jnp.bfloat16)
                for p in range(4):
                    both = lax.dot_general(
                        turned, spread[p], NN, preferred_element_type=jnp.float32
                    )
                    to = pl.ds(pl.multiple_of((g * 4 + p) * 128, 128), 128)
                    table_ref[to, :] = both[:, :128].astype(jnp.bfloat16)
                    charge_ref[to, :] = both[:, 128:]
            return carry

        lax.fori_loop(0, width // 8, build, 0)

        lane_w = lanes((FEAT, 128))
        lane_b = lanes((PART, 128))
        low_half = lane_b < PART
        def group(g, carry):
            two = tgt_ref[pl.ds(pl.multiple_of(g * 2 * FEAT, 2 * FEAT), 2 * FEAT), :]
            zero = jnp.zeros((FEAT, 128), jnp.float32)
            left, right = [], []
            for half in range(2):
                one = two[half * FEAT : (half + 1) * FEAT]
                low = jnp.where(lane_w < PART, one, 0.0)
                high = jnp.where(lane_w < PART, 0.0, one)
                left += [low, high] if half == 0 else [zero, zero]
                right += [zero, zero] if half == 0 else [low, high]
            weights = jnp.concatenate(
                [jnp.concatenate(left, axis=0), jnp.concatenate(right, axis=0)], axis=1
            ).astype(jnp.bfloat16)
            mixed, spots = [], []
            for k in range(NEAR):
                four = []
                for v in range(4):
                    leaf = near_ref[k, g * 4 + v] - shift
                    four.append(pl.ds(pl.multiple_of(leaf * PART, PART), PART))
                rows = [table_ref[spot, :] for spot in four]
                mixed.append(
                    jnp.where(
                        lane_b < 2 * FEAT,
                        jnp.where(lane_b < FEAT, rows[0], rows[1]),
                        jnp.where(lane_b < 3 * FEAT, rows[2], rows[3]),
                    )
                )
                spots.append(four)
            total = [jnp.zeros((8, 128), jnp.float32)] * 2
            for some in range(0, NEAR, 14):
                count = min(14, NEAR - some)
                dist = lax.dot_general(
                    jnp.concatenate(mixed[some : some + count], axis=0), weights, NN,
                    preferred_element_type=jnp.float32,
                )
                for k in range(count):
                    inverse = lax.rsqrt(dist[k * PART : (k + 1) * PART])
                    for half in range(2):
                        low, high = spots[some + k][2 * half : 2 * half + 2]
                        charge = jnp.where(low_half, charge_ref[low, :], charge_ref[high, :])
                        term = charge * inverse[:, half * 128 : (half + 1) * 128]
                        total[half] += jnp.sum(term.reshape(8, 8, 128), axis=0)
            both = jnp.concatenate([jnp.sum(t, axis=0, keepdims=True) for t in total], axis=0)
            out_ref[pl.ds(g * 2, 2), :] = both
            return carry

        lax.fori_loop(0, targets // 2, group, 0)

    @pl.when(jnp.logical_not(close))
    def _():
        lane = lanes((PART, 128))

        def pair(r, carry):
            columns = [
                jnp.broadcast_to(
                    win_ref[pl.ds(4 * (HPAIRS + r) + c, 1), :], (128, 128)
                ).T
                for c in range(3)
            ]
            results = []
            for p in range(2):
                mine = [column[p * PART : (p + 1) * PART] for column in columns]

                def entry(k, total):
                    leaf = near_ref[k, 2 * r + p] - shift
                    at = 4 * (leaf // 2)
                    gap = SOFTENING
                    for c in range(3):
                        diff = mine[c] - win_ref[pl.ds(at + c, 1), :]
                        gap = gap + diff * diff
                    half = jnp.where((lane // PART) == leaf % 2, 1.0, 0.0)
                    return total + half * (win_ref[pl.ds(at + 3, 1), :] * lax.rsqrt(gap))

                total = lax.fori_loop(0, NEAR, entry, jnp.zeros((PART, 128), jnp.float32))
                results.append(jnp.sum(total, axis=1, keepdims=True))
            wide = jnp.broadcast_to(jnp.concatenate(results, axis=0), (128, 128)).T
            out_ref[pl.ds(r, 1), :] = wide[:1]
            return carry

        lax.fori_loop(0, targets, pair, 0)


def gather_products(codes, ops_ref, rows_ref):
    total = None
    for code in codes:
        at = pl.ds(pl.multiple_of(code >> ROW_BITS, 8), OPROWS)
        row = rows_ref[pl.ds(code & ((1 << ROW_BITS) - 1), 1), :]
        term = ops_ref[at, :] * row
        total = term if total is None else total + term
    return total


def pack_codes(kinds, rows):
    return ((kinds * OPROWS) << ROW_BITS) | rows


def put_sums(total_ref, out_ref, lane):
    sums = jnp.sum(total_ref[...], axis=1, keepdims=True)
    out_ref[...] = jnp.where(lanes((OPROWS, 128)) == lane, sums, out_ref[...])


def halo_kernel(
    list_ref, class_ref, moment_ref, before_ref, behind_ref, code_ref, rows_ref,
    d_ref, q_ref, acc_ref, halo_ref,
):
    shift = lax.axis_index(AXES) * LEAVES - HALO
    code_ref[...] = pack_codes(class_ref[...], list_ref[...] - shift)
    fill = jnp.zeros((PAIRS - 2 * HPAIRS, 128), jnp.float32)

    def component(c):
        at = pl.ds(c, HPAIRS, stride=4)
        return jnp.concatenate([before_ref[at, :], behind_ref[at, :], fill], axis=0)

    for c in range(3):
        d_ref[c] = centred(component(c))
    q_ref[...] = component(3).T
    expand_into(d_ref, q_ref, acc_ref, halo_ref)
    rows_ref[:HALO] = halo_ref[:HALO]
    rows_ref[HALO : HALO + LEAVES] = moment_ref[...]
    rows_ref[HALO + LEAVES :] = halo_ref[HALO : 2 * HALO]


def leaf_kernel(part, code_ref, ops_ref, rows_ref, after_ref, out_ref, total_ref):
    del after_ref
    begin = part * (PAIRS // 2)

    def reduce(i):
        for v in range(LEAF_STEP):
            put_sums(total_ref.at[v], out_ref.at[v & 1], begin + 2 * i + (v >> 1))

    def step(i, carry):
        reduce(i - 1)
        for v in range(LEAF_STEP):
            leaf = 2 * begin + i * LEAF_STEP + v
            total_ref[v] = gather_products(
                [code_ref[k, leaf] for k in range(LLIST)], ops_ref, rows_ref
            )
        return carry

    total_ref[...] = jnp.zeros_like(total_ref)
    out_ref[...] = jnp.zeros_like(out_ref)
    steps = LEAVES // 2 // LEAF_STEP
    lax.fori_loop(0, steps, step, 0)
    reduce(steps - 1)


def fetch_kernel(top_ref, list_ref, class_ref, code_ref, list_vmem, class_vmem, sems):
    at = pl.ds(pl.multiple_of(window_start(top_ref), 128), TOP_WINDOW)
    copies = [
        pltpu.make_async_copy(list_ref.at[:, at], list_vmem, sems.at[0]),
        pltpu.make_async_copy(class_ref.at[:, at], class_vmem, sems.at[1]),
    ]
    for copy in copies:
        copy.start()
    for copy in copies:
        copy.wait()
    codes = pack_codes(class_vmem[...], list_vmem[...])
    shift = top_ref[0] - window_start(top_ref)
    code_ref[...] = pltpu.roll(codes, (TOP_WINDOW - shift) % TOP_WINDOW, 1)[:, :128]


def window_start(top_ref):
    return jnp.minimum(top_ref[0] // 128 * 128, TOPBOX - TOP_WINDOW)


def finish(
    cap, shift, top_ref, code_ref, table_ref, ops_ref, m2m_ref, tops_ref, local_refs, dist_ref,
    near_ref, mask_ref, out_ref, field_ref, pot_ref, total_ref, wide_ref, rows_ref,
):
    first = top_ref[0]
    boxes = top_ref[LEAVES - 1] - first + 1
    spread = jnp.zeros((OPROWS, LEAVES), jnp.float32)
    width = min(cap, 128)
    for block in range(cap // width):
        total_ref[...] = jnp.zeros_like(total_ref)
        wide_ref[...] = jnp.zeros_like(wide_ref)

        def step(b, carry):
            put_sums(total_ref, wide_ref, b - 1)
            column = shift + block * width + b
            total_ref[...] = gather_products(
                [code_ref[k, column] for k in range(TLIST)], ops_ref, table_ref
            )
            return carry

        count = jnp.clip(boxes - block * width, 0, width)
        lax.fori_loop(0, count, step, 0)
        put_sums(total_ref, wide_ref, count - 1)
        place = rows_of((128, LEAVES)) + block * width
        held = jnp.where(place == tops_ref[...] - first, 1.0, 0.0)
        spread += dot_f32(wide_ref[...], held)
    full = jnp.concatenate([spread, jnp.zeros((128 - OPROWS, LEAVES), jnp.float32)], axis=0)
    rows_ref[...] = full.T
    for a in range(8):
        at = pl.ds(a, LEAVES // 8, stride=8)
        rows_ref[at, :] = widen(dot_f32(rows_ref[at, :][:, :COEF], m2m_ref[:, a, :]))
    for p in range(2):
        field_ref[p] = (
            rows_ref[pl.ds(p, PAIRS, stride=2), :].T[:OPROWS]
            + local_refs[0][p] + local_refs[1][p]
        )
    for p in range(2):

        def step(s, carry):
            at = pl.ds(pl.multiple_of(p * PART + s * 16, 16), 16)
            listed = harmonics(dist_ref[0, at, :], dist_ref[1, at, :], dist_ref[2, at, :])
            total = None
            for c, term in enumerate(listed):
                weight = field_ref[p, pl.ds(c, 1), :]
                value = jnp.broadcast_to(weight, (16, 128)) if term is None else term * weight
                total = value if total is None else total + value
            pot_ref[at, :] = total
            return carry

        lax.fori_loop(0, PART // 16, step, 0)
    out_ref[...] = (near_ref[...] + pot_ref[...].T) * mask_ref[...]


def last_kernel(
    top_ref, code_ref, mine_ref, other_ref, ops_ref, m2m_ref, tops_ref, local_a_ref, local_b_ref,
    dist_ref, near_ref, mask_ref, out_ref, over_ref,
    table_ref, rest_ref, meta_ref, ends_ref, packed_ref, scalar_ref, sems, *scratch,
):
    half = mine_ref.shape[0]
    blocks = half // SEND
    table_ref[:half] = mine_ref[...]
    table_ref[half:] = other_ref[...]
    heads = pl.ds(0, 2 * blocks, stride=SEND)
    turned = table_ref[heads, :].T[120:]
    meta_ref[...] = turned.astype(jnp.int32)
    copy = pltpu.make_async_copy(meta_ref, ends_ref, sems.at[0])
    copy.start()
    most = jnp.max(turned[6:7] - turned[7:8]).astype(jnp.int32) + 1
    over_ref[0] = most
    core, my_y, my_x = lax.axis_index("core"), lax.axis_index("y"), lax.axis_index("x")
    my_z = lax.axis_index(("zlo", "zhi"))
    by_z = [((my_z - z) & 3) * 16 for z in range(4)]
    by_x = [((my_x - x) & 3) * 4 for x in range(4)]
    by_y = [(my_y - y) & 3 for y in range(4)]
    by_core = [blocks * (core ^ side) for side in range(2)]
    order = [
        by_z[zlo * 2 + zhi] + by_x[x] + by_y[y] + by_core[side]
        for zlo in range(2) for side in range(2) for y in range(4) for x in range(4)
        for zhi in range(2)
    ]
    copy.wait()

    @pl.when(most < SEND)
    def _():
        code = code_ref[...]
        box = code & ((1 << ROW_BITS) - 1)
        row = code
        last, last_begin = 0, 0
        rest_ref[pl.ds(order[0], 1), :] = jnp.zeros((1, 128), jnp.float32)
        for d, block in enumerate(order):
            begin = ends_ref[7, block]
            base = block * SEND
            if d:
                rest_ref[pl.ds(block, 1), :] = table_ref[pl.ds(last + begin - last_begin, 1), :]
                row += jnp.where(box >= begin, base - begin - last + last_begin, 0)
            else:
                row += base - begin
            last, last_begin = base, begin
        packed_ref[...] = row
        copy = pltpu.make_async_copy(packed_ref, scalar_ref, sems.at[1])
        copy.start()
        table_ref[heads, :] += rest_ref[...]
        copy.wait()
        finish(
            64, 0, top_ref, scalar_ref, table_ref, ops_ref, m2m_ref, tops_ref,
            (local_a_ref, local_b_ref), dist_ref, near_ref, mask_ref, out_ref, *scratch,
        )


def spare_kernel(
    top_ref, code_ref, table_ref, ops_ref, m2m_ref, tops_ref, local_a_ref, local_b_ref,
    dist_ref, near_ref, mask_ref, out_ref, *scratch,
):
    finish(
        LEAVES, top_ref[0] - jnp.minimum(top_ref[0], TOPBOX - LEAVES), top_ref, code_ref, table_ref, ops_ref, m2m_ref, tops_ref,
        (local_a_ref, local_b_ref), dist_ref, near_ref, mask_ref, out_ref, *scratch,
    )


SMEM = pl.BlockSpec(memory_space=pltpu.SMEM)
VMEM = pl.BlockSpec(memory_space=pltpu.VMEM)
F32 = jnp.float32


def shape(*dims):
    return jax.ShapeDtypeStruct(dims, F32)


ANY = pl.BlockSpec(memory_space=pl.ANY)
FINISH_SCRATCH = [
    pltpu.VMEM((2, OPROWS, 128), F32),
    pltpu.VMEM((128, 128), F32),
    pltpu.VMEM((OPROWS, 128), F32),
    pltpu.VMEM((OPROWS, 128), F32),
    pltpu.VMEM((LEAVES, 128), F32),
]


def cost(flops, bytes_accessed):
    return pl.CostEstimate(flops=flops, bytes_accessed=bytes_accessed, transcendentals=0)


def call_first(pts, counts, leaf_top, tops, m2m):
    return pl.pallas_call(
        first_kernel,
        out_shape=(
            shape(4 * PAIRS, 128), shape(4 * HPAIRS, 128), shape(4 * HPAIRS, 128),
            shape(3, PAIRS, 128), shape(LEAVES, 128), shape(SEND, 128), shape(LEAVES, 128),
            shape(PAIRS, 128),
        ),
        in_specs=[VMEM, SMEM, SMEM, VMEM, VMEM],
        out_specs=(VMEM,) * 8,
        scratch_shapes=[
            pltpu.VMEM((128, 128), F32), pltpu.VMEM((COEF, 8, 128), F32),
            pltpu.VMEM((LEAVES, 128), F32),
        ],
        compiler_params=pltpu.CompilerParams(vmem_limit_bytes=16 * MIB),
        cost_estimate=cost(10**9, 10**7),
        name="expand_own",
    )(pts, counts, leaf_top, tops, m2m)


def call_turn(ops, after):
    return pl.pallas_call(
        turn_kernel,
        out_shape=shape(CLASSES * OPROWS, 128),
        in_specs=[VMEM, ANY],
        out_specs=VMEM,
        compiler_params=pltpu.CompilerParams(vmem_limit_bytes=26 * MIB),
        cost_estimate=cost(10**7, 3 * 10**7),
        name="turn_operators",
    )(ops, after)


def call_join(pieces, *after):
    rows = pieces[0].shape[0]
    return pl.pallas_call(
        join_kernel,
        out_shape=shape(4 * rows, 128),
        in_specs=[VMEM] * 4 + [ANY] * len(after),
        out_specs=VMEM,
        compiler_params=pltpu.CompilerParams(vmem_limit_bytes=8 * MIB),
        cost_estimate=cost(10**5, 8 * rows * 512),
        name="join",
    )(*pieces, *after)


def call_near(near, own, before, behind, after):
    targets, width = PAIRS, WPAIRS
    return pl.pallas_call(
        near_kernel,
        out_shape=shape(targets, 128),
        in_specs=[SMEM, VMEM, VMEM, VMEM, ANY],
        out_specs=VMEM,
        scratch_shapes=[
            pltpu.VMEM((4 * WPAIRS, 128), F32),
            pltpu.VMEM((width * FEAT, 128), F32),
            pltpu.VMEM((targets * FEAT, 128), F32),
            pltpu.VMEM((width * 128, 128), jnp.bfloat16),
            pltpu.VMEM((width * 128, 128), F32),
        ],
        compiler_params=pltpu.CompilerParams(vmem_limit_bytes=24 * MIB),
        cost_estimate=cost(10 * targets * 2 * 64 * NEAR * 64, 3 * 10**7),
        name="near",
    )(near, own, before, behind, after)


def call_halo(lists, classes, moments, before, behind):
    return pl.pallas_call(
        halo_kernel,
        out_shape=(jax.ShapeDtypeStruct((LLIST, LEAVES), jnp.int32), shape(2 * WPAIRS, 128)),
        in_specs=[VMEM] * 5,
        out_specs=(VMEM, VMEM),
        scratch_shapes=[
            pltpu.VMEM((3, 128, 128), F32),
            pltpu.VMEM((128, 128), F32),
            pltpu.VMEM((COEF, 8, 128), F32),
            pltpu.VMEM((LEAVES, 128), F32),
        ],
        compiler_params=pltpu.CompilerParams(vmem_limit_bytes=16 * MIB),
        cost_estimate=cost(10**8, 10**6),
        name="expand_halo",
    )(lists, classes, moments, before, behind)


def call_leaf(part, code, ops, rows, after):
    return pl.pallas_call(
        functools.partial(leaf_kernel, part),
        out_shape=shape(2, OPROWS, 128),
        in_specs=[SMEM, VMEM, VMEM, ANY],
        out_specs=VMEM,
        scratch_shapes=[pltpu.VMEM((LEAF_STEP, OPROWS, 128), F32)],
        compiler_params=pltpu.CompilerParams(vmem_limit_bytes=17 * MIB),
        cost_estimate=cost(LEAVES * LLIST * COEF * COEF * 8, 2 * 10**7),
        name="leaf_translate",
    )(code, ops, rows, after)


def call_fetch(leaf_top, lists, classes):
    window = (TLIST, TOP_WINDOW)
    return pl.pallas_call(
        fetch_kernel,
        out_shape=jax.ShapeDtypeStruct((TLIST, 128), jnp.int32),
        in_specs=[SMEM, ANY, ANY],
        out_specs=VMEM,
        scratch_shapes=[
            pltpu.VMEM(window, jnp.int32), pltpu.VMEM(window, jnp.int32),
            pltpu.SemaphoreType.DMA((2,)),
        ],
        compiler_params=pltpu.CompilerParams(vmem_limit_bytes=8 * MIB),
        cost_estimate=cost(10**5, 10**5),
        name="fetch_lists",
    )(leaf_top, lists, classes)


def call_last(leaf_top, code, mine, other, *rest):
    return pl.pallas_call(
        last_kernel,
        out_shape=(shape(PAIRS, 128), jax.ShapeDtypeStruct((1,), jnp.int32)),
        in_specs=[SMEM] + [VMEM] * 11,
        out_specs=(VMEM, SMEM),
        scratch_shapes=[
            pltpu.VMEM((2 * mine.shape[0], 128), F32),
            pltpu.VMEM((2 * mine.shape[0] // SEND, 128), F32),
            pltpu.VMEM((8, 128), jnp.int32),
            pltpu.SMEM((8, 128), jnp.int32),
            pltpu.VMEM((TLIST, 128), jnp.int32),
            pltpu.SMEM((TLIST, 128), jnp.int32),
            pltpu.SemaphoreType.DMA((2,)),
        ] + FINISH_SCRATCH,
        compiler_params=pltpu.CompilerParams(vmem_limit_bytes=24 * MIB),
        name="finish",
    )(leaf_top, code, mine, other, *rest)


def call_spare(leaf_top, code, table, *rest):
    return pl.pallas_call(
        spare_kernel,
        out_shape=shape(PAIRS, 128),
        in_specs=[SMEM, SMEM] + [VMEM] * 9,
        out_specs=VMEM,
        scratch_shapes=FINISH_SCRATCH,
        compiler_params=pltpu.CompilerParams(vmem_limit_bytes=24 * MIB),
        name="finish_spare",
    )(leaf_top, code, table, *rest)


def sent_over(block, axis, count):
    return [block] + [
        lax.ppermute(block, axis, [(i, (i + s) % count) for i in range(count)])
        for s in range(1, count)
    ]


def body(
    particles, counts, leaf_top, near_list, leaf_list, leaf_class, top_list, top_class,
    m2l_ops, m2m_ops,
):
    pts = particles.reshape(4, PAIRS, 128).transpose(1, 0, 2).reshape(4 * PAIRS, 128)
    tops = leaf_top.reshape(1, LEAVES)
    m2m = m2m_ops.transpose(1, 0, 2)
    own, low, high, dist, moments, send, partial, mask = call_first(
        pts, counts, leaf_top, tops, m2m
    )
    devices = lax.axis_size(AXES)
    up = [(i, (i + 1) % devices) for i in range(devices)]
    down = [(j, i) for i, j in up]
    over_y = sent_over(send, "y", 4)
    before = lax.ppermute(high, AXES, up)
    behind = lax.ppermute(low, AXES, down)
    ops = call_turn(m2l_ops.transpose(1, 2, 0), send)
    by_y = call_join(over_y, ops, before, behind)
    over_x = sent_over(by_y, "x", 4)
    code, rows = call_halo(leaf_list.T, leaf_class.T, moments, before, behind)
    local_a = call_leaf(0, code, ops, rows, by_y)
    by_x = call_join(over_x, local_a)
    over_z = sent_over(by_x, ("zlo", "zhi"), 4)
    near = call_near(near_list.T, own, before, behind, by_x)
    mine = call_join(over_z, near)
    other = lax.ppermute(mine, "core", [(0, 1), (1, 0)])
    local_b = call_leaf(1, code, ops, rows, mine)
    top_code = call_fetch(leaf_top, top_list.T, top_class.T)
    rest = (ops, m2m, tops, local_a, local_b, dist, near, mask)
    result, over = call_last(leaf_top, top_code, mine, other, *rest)

    def spare():
        table = lax.dynamic_update_slice(
            jnp.zeros((TOPBOX + LEAVES, 128), F32), partial, (leaf_top[0], 0)
        )
        for k in range(7):
            swap = [(i, i ^ (1 << k)) for i in range(devices)]
            table = table + lax.ppermute(table, AXES, swap)
        start = jnp.minimum(leaf_top[0], TOPBOX - LEAVES)
        lists, classes = (
            lax.dynamic_slice_in_dim(x, start, LEAVES, axis=0).T for x in (top_list, top_class)
        )
        again = call_turn(m2l_ops.transpose(1, 2, 0), table)
        return call_spare(leaf_top, pack_codes(classes, lists), table, again, *rest[1:])

    result = lax.cond(over[0] >= SEND, spare, lambda: result)
    return result.reshape(-1)


def solution(mesh):
    fine = Mesh(mesh.devices.reshape(2, 2, 4, 4, 2), AXES)
    return jax.shard_map(
        body,
        mesh=fine,
        in_specs=(
            P(None, AXES), P(AXES), P(AXES), P(AXES, None), P(AXES, None), P(AXES, None),
            P(), P(), P(), P(),
        ),
        out_specs=P(AXES),
        check_vma=False,
    )
```

```python
import functools

import jax
import jax.numpy as jnp
from jax import lax
from jax.experimental import pallas as pl
from jax.experimental.pallas import tpu as pltpu
from jax.sharding import Mesh, PartitionSpec as P

ORDER = 8
COEF = 81
PART = 64
LEAVES = 256
PAIRS = 128
HALO = 32
HPAIRS = 16
WPAIRS = PAIRS + 2 * HPAIRS
NEAR = 27
LLIST = 16
TLIST = 64
TOPBOX = 4096
ROW_BITS = 13
CLASSES = 316
OPROWS = 88
SOFTENING = 0.01
SEND = 56
REACH_SQ = 16.0
FEAT = 32
FEATS = 24
LEAF_STEP = 4
TURN_STEP = 3
TOP_WINDOW = 256
BUILD_STEP = 16
NEAR_STEP = 32

HIGH = lax.Precision.HIGHEST
MIB = 1 << 20
AXES = ("zlo", "core", "y", "x", "zhi")

NN = (((1,), (0,)), ((), ()))
NT = (((1,), (1,)), ((), ()))


def dot_f32(left, right, dims=NN):
    return lax.dot_general(left, right, dims, precision=HIGH, preferred_element_type=jnp.float32)


def lanes(shape):
    return lax.broadcasted_iota(jnp.int32, shape, len(shape) - 1)


def rows_of(shape):
    return lax.broadcasted_iota(jnp.int32, shape, len(shape) - 2)


def harmonics(coord_x, coord_y, coord_z):
    radius_sq = coord_x * coord_x + coord_y * coord_y + coord_z * coord_z
    terms = {(0, 0): (None, None)}
    for m in range(1, ORDER + 1):
        if m == 1:
            terms[1, 1] = (coord_x * 0.5, coord_y * 0.5)
            continue
        re, im = terms[m - 1, m - 1]
        scale = 1.0 / (2.0 * m)
        terms[m, m] = (
            (coord_x * re - coord_y * im) * scale,
            (coord_x * im + coord_y * re) * scale,
        )
    for m in range(ORDER):
        re, im = terms[m, m]
        terms[m + 1, m] = (coord_z, None) if m == 0 else (coord_z * re, coord_z * im)
    for m in range(ORDER - 1):
        for n in range(m + 2, ORDER + 1):
            one = (2.0 * n - 1.0) / ((n - m) * (n + m))
            two = 1.0 / ((n - m) * (n + m))
            z_one = coord_z * one
            r_two = radius_sq * two
            upper, lower = terms[n - 1, m], terms[n - 2, m]
            re = z_one * upper[0] - (r_two if lower[0] is None else r_two * lower[0])
            im = None if m == 0 else z_one * upper[1] - r_two * lower[1]
            terms[n, m] = (re, im)
    listed = []
    for n in range(ORDER + 1):
        listed.append(terms[n, 0][0])
        for m in range(1, n + 1):
            listed.extend(terms[n, m])
    return listed


def centred(block):
    turned = block.T
    halves = []
    for p in range(2):
        half = turned[p * PART : (p + 1) * PART]
        halves.append(half - jnp.sum(half, axis=0, keepdims=True) * (1.0 / PART))
    return jnp.concatenate(halves, axis=0)


def expand_into(d_ref, q_ref, acc_ref, out_ref):
    for p in range(2):
        acc_ref[...] = jnp.zeros_like(acc_ref)

        def step(s, carry):
            at = pl.ds(pl.multiple_of(p * PART + s * 16, 16), 16)
            charge = q_ref[at, :]
            listed = harmonics(d_ref[0, at, :], d_ref[1, at, :], d_ref[2, at, :])
            for c, term in enumerate(listed):
                value = charge if term is None else charge * term
                acc_ref[c] += value[:8] + value[8:]
            return carry

        lax.fori_loop(0, PART // 16, step, 0)
        sums = jnp.sum(acc_ref[...], axis=1)
        full = jnp.concatenate([sums, jnp.zeros((128 - COEF, 128), jnp.float32)], axis=0)
        out_ref[pl.ds(p, PAIRS, stride=2), :] = full.T


def widen(block):
    return jnp.concatenate(
        [block, jnp.zeros((block.shape[0], 128 - block.shape[1]), jnp.float32)], axis=1
    )


def first_kernel(
    pts_ref, count_ref, top_ref, tops_ref, m2m_ref,
    own_ref, low_ref, high_ref, dist_ref, moment_ref, send_ref, part_ref, mask_ref,
    q_ref, acc_ref, lift_ref,
):
    lane = lanes((1, 128))

    def hold(i, carry):
        for u in range(8):
            r = i * 8 + u
            held = jnp.where(lane < PART, count_ref[2 * r], count_ref[2 * r + 1])
            mask_ref[pl.ds(r, 1), :] = jnp.where((lane & (PART - 1)) < held, 1.0, 0.0)
        return carry

    lax.fori_loop(0, PAIRS // 8, hold, 0)
    charge = pts_ref[pl.ds(3, PAIRS, stride=4), :] * mask_ref[...]
    own_ref[...] = pts_ref[...]
    own_ref[pl.ds(3, PAIRS, stride=4), :] = charge
    low_ref[...] = own_ref[: 4 * HPAIRS]
    high_ref[...] = own_ref[4 * (PAIRS - HPAIRS) :]
    for c in range(3):
        dist_ref[c] = centred(pts_ref[pl.ds(c, PAIRS, stride=4), :])
    q_ref[...] = charge.T
    expand_into(dist_ref, q_ref, acc_ref, moment_ref)
    first, last = top_ref[0], top_ref[LEAVES - 1]
    for a in range(8):
        at = pl.ds(a, LEAVES // 8, stride=8)
        lift_ref[at, :] = widen(dot_f32(moment_ref[at, :][:, :COEF], m2m_ref[:, a, :], NT))
    held = jnp.where(rows_of((LEAVES, LEAVES)) == tops_ref[...] - first, 1.0, 0.0)
    wide = dot_f32(held, lift_ref[...])
    lane = lanes((LEAVES, 128))
    wide = jnp.where(lane == 127, first.astype(jnp.float32), wide)
    wide = jnp.where(lane == 126, last.astype(jnp.float32), wide)
    part_ref[...] = wide
    send_ref[...] = wide[:SEND]


def turn_kernel(in_ref, after_ref, out_ref):
    del after_ref

    def step(i, carry):
        for u in range(TURN_STEP):
            one = in_ref[i * TURN_STEP + u]
            for begin in range(0, CLASSES, 128):
                count = min(128, CLASSES - begin)
                at = pl.ds(begin * OPROWS + i * TURN_STEP + u, count, stride=OPROWS)
                out_ref[at, :] = widen(one[:, begin : begin + count].T)
        return carry

    lax.fori_loop(0, COEF // TURN_STEP, step, 0)


def join_kernel(*refs):
    out_ref = refs[-1]
    rows = refs[0].shape[0]
    for i, ref in enumerate(refs[:4]):
        out_ref[i * rows : (i + 1) * rows] = ref[...]


def split3(value):
    high = value.astype(jnp.bfloat16).astype(jnp.float32)
    rest = value - high
    middle = rest.astype(jnp.bfloat16).astype(jnp.float32)
    low = (rest - middle).astype(jnp.bfloat16).astype(jnp.float32)
    return high, middle, low


def near_kernel(
    near_ref, own_ref, before_ref, behind_ref, after_ref, out_ref,
    win_ref, src_ref, tgt_ref, source_ref, target_ref, charge_ref,
):
    del after_ref
    targets, width = PAIRS, WPAIRS
    edge = 4 * HPAIRS
    win_ref[:edge] = before_ref[...]
    win_ref[edge : edge + 4 * PAIRS] = own_ref[...]
    win_ref[edge + 4 * PAIRS :] = behind_ref[...]
    shift = lax.axis_index(AXES) * LEAVES - HALO

    def component(c):
        return win_ref[pl.ds(c, width, stride=4), :]

    points = [component(c) for c in range(3)]
    moved = []
    for c in range(3):
        least = jnp.min(points[c], keepdims=True)
        most = jnp.max(points[c], keepdims=True)
        moved.append(points[c] - 0.5 * (least + most))
    norm = moved[0] * moved[0] + moved[1] * moved[1] + moved[2] * moved[2]
    close = jnp.max(norm) <= REACH_SQ
    out_ref[...] = jnp.zeros_like(out_ref)

    @pl.when(close)
    def _():
        own = slice(HPAIRS, HPAIRS + targets)

        def keep(ref, f, feature):
            rows = feature.shape[0]
            ref[f * rows : (f + 1) * rows] = feature

        for c in range(3):
            h, m, l = split3(moved[c])
            for i, feature in enumerate((h, h, m, m, h, l)):
                keep(src_ref, 6 * c + i, feature)
            th, tm, tl = [-2.0 * piece[own] for piece in (h, m, l)]
            for i, feature in enumerate((th, tm, th, tm, tl, th)):
                keep(tgt_ref, 6 * c + i, feature)
        ones = jnp.ones((width, 128), jnp.float32)
        for i, feature in enumerate(split3(norm + SOFTENING)):
            keep(src_ref, 18 + i, feature)
            keep(tgt_ref, 18 + i, ones[own])
        for i, feature in enumerate(split3(norm[own])):
            keep(src_ref, 21 + i, ones)
            keep(tgt_ref, 21 + i, feature)
        charge = component(3)
        charge_ref[pl.ds(0, width, stride=2), :] = charge
        charge_ref[pl.ds(1, width, stride=2), :] = pltpu.roll(charge, PART, 1)
        rest = jnp.zeros((FEAT - FEATS, 128), jnp.float32)

        def build_source(i, carry):
            for u in range(BUILD_STEP):
                r = i * BUILD_STEP + u
                some = src_ref[pl.ds(r, FEATS, stride=width), :]
                some = jnp.concatenate([some, rest], axis=0)
                source_ref[2 * r] = some.astype(jnp.bfloat16)
                source_ref[2 * r + 1] = pltpu.roll(some, PART, 1).astype(jnp.bfloat16)
            return carry

        def build_target(i, carry):
            for u in range(BUILD_STEP):
                r = i * BUILD_STEP + u
                some = tgt_ref[pl.ds(r, FEATS, stride=targets), :]
                some = jnp.concatenate([some, rest], axis=0).T.astype(jnp.bfloat16)
                for p in range(2):
                    target_ref[2 * r + p] = some[p * PART : (p + 1) * PART]
            return carry

        lax.fori_loop(0, width // BUILD_STEP, build_source, 0)
        lax.fori_loop(0, targets // BUILD_STEP, build_target, 0)

        low_block = lanes((FEAT, 128)) < PART
        low_row = lanes((1, 128)) < PART
        lane = lanes((PART, 128))

        def leaf_sums(l):
            total = None
            for k in range(0, NEAR + 1, 4):
                blocks, charges = [], []
                for j in range(k, k + 4, 2):
                    one = near_ref[j, l] - shift
                    two = (near_ref[min(j + 1, NEAR - 1), l] - shift) ^ 1
                    blocks.append(jnp.where(low_block, source_ref[one], source_ref[two]))
                    other = charge_ref[pl.ds(two, 1), :] if j + 1 < NEAR else 0.0
                    charges.append(jnp.where(low_row, charge_ref[pl.ds(one, 1), :], other))
                dist = lax.dot_general(
                    target_ref[l], jnp.concatenate(blocks, axis=1), NN,
                    preferred_element_type=jnp.float32,
                )
                for j in range(2):
                    term = charges[j] * lax.rsqrt(dist[:, j * 128 : (j + 1) * 128])
                    total = term if total is None else total + term
            return total

        def group(i, carry):
            totals = [leaf_sums(i * NEAR_STEP + u) for u in range(NEAR_STEP)]
            for p in range(2):
                at = pl.ds(p * PART, PART)
                wide = out_ref[at, :]
                for u in range(p, NEAR_STEP, 2):
                    sums = jnp.sum(totals[u], axis=1, keepdims=True)
                    wide = jnp.where(lane == i * (NEAR_STEP // 2) + u // 2, sums, wide)
                out_ref[at, :] = wide
            return carry

        lax.fori_loop(0, LEAVES // NEAR_STEP, group, 0)

    @pl.when(jnp.logical_not(close))
    def _():
        lane = lanes((PART, 128))

        def pair(r, carry):
            columns = [
                jnp.broadcast_to(
                    win_ref[pl.ds(4 * (HPAIRS + r) + c, 1), :], (128, 128)
                ).T
                for c in range(3)
            ]
            for p in range(2):
                mine = [column[p * PART : (p + 1) * PART] for column in columns]

                def entry(k, total):
                    leaf = near_ref[k, 2 * r + p] - shift
                    at = 4 * (leaf // 2)
                    gap = SOFTENING
                    for c in range(3):
                        diff = mine[c] - win_ref[pl.ds(at + c, 1), :]
                        gap = gap + diff * diff
                    half = jnp.where((lane // PART) == leaf % 2, 1.0, 0.0)
                    return total + half * (win_ref[pl.ds(at + 3, 1), :] * lax.rsqrt(gap))

                total = lax.fori_loop(0, NEAR, entry, jnp.zeros((PART, 128), jnp.float32))
                at = pl.ds(p * PART, PART)
                sums = jnp.sum(total, axis=1, keepdims=True)
                out_ref[at, :] = jnp.where(lane == r, sums, out_ref[at, :])
            return carry

        lax.fori_loop(0, targets, pair, 0)


def gather_products(codes, ops_ref, rows_ref):
    total = None
    for code in codes:
        at = pl.ds(pl.multiple_of(code >> ROW_BITS, 8), OPROWS)
        row = rows_ref[pl.ds(code & ((1 << ROW_BITS) - 1), 1), :]
        term = ops_ref[at, :] * row
        total = term if total is None else total + term
    return total


def pack_codes(kinds, rows):
    return ((kinds * OPROWS) << ROW_BITS) | rows


def put_sums(total_ref, out_ref, lane):
    sums = jnp.sum(total_ref[...], axis=1, keepdims=True)
    out_ref[...] = jnp.where(lanes((OPROWS, 128)) == lane, sums, out_ref[...])


def halo_kernel(
    list_ref, class_ref, moment_ref, before_ref, behind_ref, code_ref, rows_ref,
    d_ref, q_ref, acc_ref, halo_ref,
):
    shift = lax.axis_index(AXES) * LEAVES - HALO
    code_ref[...] = pack_codes(class_ref[...], list_ref[...] - shift)
    fill = jnp.zeros((PAIRS - 2 * HPAIRS, 128), jnp.float32)

    def component(c):
        at = pl.ds(c, HPAIRS, stride=4)
        return jnp.concatenate([before_ref[at, :], behind_ref[at, :], fill], axis=0)

    for c in range(3):
        d_ref[c] = centred(component(c))
    q_ref[...] = component(3).T
    expand_into(d_ref, q_ref, acc_ref, halo_ref)
    rows_ref[:HALO] = halo_ref[:HALO]
    rows_ref[HALO : HALO + LEAVES] = moment_ref[...]
    rows_ref[HALO + LEAVES :] = halo_ref[HALO : 2 * HALO]


def leaf_kernel(part, code_ref, ops_ref, rows_ref, after_ref, out_ref, total_ref):
    del after_ref
    begin = part * (PAIRS // 2)
    lane = lanes((OPROWS, 128))

    def reduce(i):
        for p in range(2):
            wide = out_ref[p]
            for v in range(p, LEAF_STEP, 2):
                at = begin + i * (LEAF_STEP // 2) + v // 2
                wide = jnp.where(lane == at, jnp.sum(total_ref[v], axis=1, keepdims=True), wide)
            out_ref[p] = wide

    def step(i, carry):
        reduce(i - 1)
        for v in range(LEAF_STEP):
            leaf = 2 * begin + i * LEAF_STEP + v
            total_ref[v] = gather_products(
                [code_ref[k, leaf] for k in range(LLIST)], ops_ref, rows_ref
            )
        return carry

    total_ref[...] = jnp.zeros_like(total_ref)
    out_ref[...] = jnp.zeros_like(out_ref)
    steps = LEAVES // 2 // LEAF_STEP
    lax.fori_loop(0, steps, step, 0)
    reduce(steps - 1)


def fetch_kernel(top_ref, list_ref, class_ref, code_ref, list_vmem, class_vmem, sems):
    at = pl.ds(pl.multiple_of(window_start(top_ref), 128), TOP_WINDOW)
    copies = [
        pltpu.make_async_copy(list_ref.at[:, at], list_vmem, sems.at[0]),
        pltpu.make_async_copy(class_ref.at[:, at], class_vmem, sems.at[1]),
    ]
    for copy in copies:
        copy.start()
    for copy in copies:
        copy.wait()
    codes = pack_codes(class_vmem[...], list_vmem[...])
    shift = top_ref[0] - window_start(top_ref)
    code_ref[...] = pltpu.roll(codes, (TOP_WINDOW - shift) % TOP_WINDOW, 1)[:, :128]


def window_start(top_ref):
    return jnp.minimum(top_ref[0] // 128 * 128, TOPBOX - TOP_WINDOW)


def finish(
    cap, shift, top_ref, code_ref, table_ref, ops_ref, m2m_ref, tops_ref, local_refs, dist_ref,
    near_ref, mask_ref, out_ref, field_ref, pot_ref, total_ref, wide_ref, rows_ref,
):
    first = top_ref[0]
    boxes = top_ref[LEAVES - 1] - first + 1
    spread = jnp.zeros((OPROWS, LEAVES), jnp.float32)
    width = min(cap, 128)
    for block in range(cap // width):
        total_ref[...] = jnp.zeros_like(total_ref)
        wide_ref[...] = jnp.zeros_like(wide_ref)

        def step(b, carry):
            put_sums(total_ref, wide_ref, b - 1)
            column = shift + block * width + b
            total_ref[...] = gather_products(
                [code_ref[k, column] for k in range(TLIST)], ops_ref, table_ref
            )
            return carry

        count = jnp.clip(boxes - block * width, 0, width)
        lax.fori_loop(0, count, step, 0)
        put_sums(total_ref, wide_ref, count - 1)
        place = rows_of((128, LEAVES)) + block * width
        held = jnp.where(place == tops_ref[...] - first, 1.0, 0.0)
        spread += dot_f32(wide_ref[...], held)
    full = jnp.concatenate([spread, jnp.zeros((128 - OPROWS, LEAVES), jnp.float32)], axis=0)
    rows_ref[...] = full.T
    for a in range(8):
        at = pl.ds(a, LEAVES // 8, stride=8)
        rows_ref[at, :] = widen(dot_f32(rows_ref[at, :][:, :COEF], m2m_ref[:, a, :]))
    for p in range(2):
        field_ref[p] = (
            rows_ref[pl.ds(p, PAIRS, stride=2), :].T[:OPROWS]
            + local_refs[0][p] + local_refs[1][p]
        )
    for p in range(2):

        def step(s, carry):
            at = pl.ds(pl.multiple_of(p * PART + s * 16, 16), 16)
            listed = harmonics(dist_ref[0, at, :], dist_ref[1, at, :], dist_ref[2, at, :])
            total = None
            for c, term in enumerate(listed):
                weight = field_ref[p, pl.ds(c, 1), :]
                value = jnp.broadcast_to(weight, (16, 128)) if term is None else term * weight
                total = value if total is None else total + value
            pot_ref[at, :] = total
            return carry

        lax.fori_loop(0, PART // 16, step, 0)
    out_ref[...] = (near_ref[...] + pot_ref[...]).T * mask_ref[...]


def last_kernel(
    top_ref, code_ref, mine_ref, other_ref, ops_ref, m2m_ref, tops_ref, local_a_ref, local_b_ref,
    dist_ref, near_ref, mask_ref, out_ref, over_ref,
    table_ref, rest_ref, meta_ref, ends_ref, packed_ref, scalar_ref, sems, *scratch,
):
    half = mine_ref.shape[0]
    blocks = half // SEND
    table_ref[:half] = mine_ref[...]
    table_ref[half:] = other_ref[...]
    heads = pl.ds(0, 2 * blocks, stride=SEND)
    turned = table_ref[heads, :].T[120:]
    meta_ref[...] = turned.astype(jnp.int32)
    copy = pltpu.make_async_copy(meta_ref, ends_ref, sems.at[0])
    copy.start()
    most = jnp.max(turned[6:7] - turned[7:8]).astype(jnp.int32) + 1
    over_ref[0] = most
    core, my_y, my_x = lax.axis_index("core"), lax.axis_index("y"), lax.axis_index("x")
    my_z = lax.axis_index(("zlo", "zhi"))
    by_z = [((my_z - z) & 3) * 16 for z in range(4)]
    by_x = [((my_x - x) & 3) * 4 for x in range(4)]
    by_y = [(my_y - y) & 3 for y in range(4)]
    by_core = [blocks * (core ^ side) for side in range(2)]
    order = [
        by_z[zlo * 2 + zhi] + by_x[x] + by_y[y] + by_core[side]
        for zlo in range(2) for side in range(2) for y in range(4) for x in range(4)
        for zhi in range(2)
    ]
    copy.wait()

    @pl.when(most < SEND)
    def _():
        code = code_ref[...]
        box = code & ((1 << ROW_BITS) - 1)
        row = code
        last, last_begin = 0, 0
        rest_ref[pl.ds(order[0], 1), :] = jnp.zeros((1, 128), jnp.float32)
        for d, block in enumerate(order):
            begin = ends_ref[7, block]
            base = block * SEND
            if d:
                rest_ref[pl.ds(block, 1), :] = table_ref[pl.ds(last + begin - last_begin, 1), :]
                row += jnp.where(box >= begin, base - begin - last + last_begin, 0)
            else:
                row += base - begin
            last, last_begin = base, begin
        packed_ref[...] = row
        copy = pltpu.make_async_copy(packed_ref, scalar_ref, sems.at[1])
        copy.start()
        table_ref[heads, :] += rest_ref[...]
        copy.wait()
        finish(
            64, 0, top_ref, scalar_ref, table_ref, ops_ref, m2m_ref, tops_ref,
            (local_a_ref, local_b_ref), dist_ref, near_ref, mask_ref, out_ref, *scratch,
        )


def spare_kernel(
    top_ref, code_ref, table_ref, ops_ref, m2m_ref, tops_ref, local_a_ref, local_b_ref,
    dist_ref, near_ref, mask_ref, out_ref, *scratch,
):
    finish(
        LEAVES, top_ref[0] - jnp.minimum(top_ref[0], TOPBOX - LEAVES), top_ref, code_ref, table_ref, ops_ref, m2m_ref, tops_ref,
        (local_a_ref, local_b_ref), dist_ref, near_ref, mask_ref, out_ref, *scratch,
    )


SMEM = pl.BlockSpec(memory_space=pltpu.SMEM)
VMEM = pl.BlockSpec(memory_space=pltpu.VMEM)
F32 = jnp.float32


def shape(*dims):
    return jax.ShapeDtypeStruct(dims, F32)


ANY = pl.BlockSpec(memory_space=pl.ANY)
FINISH_SCRATCH = [
    pltpu.VMEM((2, OPROWS, 128), F32),
    pltpu.VMEM((128, 128), F32),
    pltpu.VMEM((OPROWS, 128), F32),
    pltpu.VMEM((OPROWS, 128), F32),
    pltpu.VMEM((LEAVES, 128), F32),
]


def cost(flops, bytes_accessed):
    return pl.CostEstimate(flops=flops, bytes_accessed=bytes_accessed, transcendentals=0)


def call_first(pts, counts, leaf_top, tops, m2m):
    return pl.pallas_call(
        first_kernel,
        out_shape=(
            shape(4 * PAIRS, 128), shape(4 * HPAIRS, 128), shape(4 * HPAIRS, 128),
            shape(3, PAIRS, 128), shape(LEAVES, 128), shape(SEND, 128), shape(LEAVES, 128),
            shape(PAIRS, 128),
        ),
        in_specs=[VMEM, SMEM, SMEM, VMEM, VMEM],
        out_specs=(VMEM,) * 8,
        scratch_shapes=[
            pltpu.VMEM((128, 128), F32), pltpu.VMEM((COEF, 8, 128), F32),
            pltpu.VMEM((LEAVES, 128), F32),
        ],
        compiler_params=pltpu.CompilerParams(vmem_limit_bytes=16 * MIB),
        cost_estimate=cost(10**9, 10**7),
        name="expand_own",
    )(pts, counts, leaf_top, tops, m2m)


def call_turn(ops, after):
    return pl.pallas_call(
        turn_kernel,
        out_shape=shape(CLASSES * OPROWS, 128),
        in_specs=[VMEM, ANY],
        out_specs=VMEM,
        compiler_params=pltpu.CompilerParams(vmem_limit_bytes=26 * MIB),
        cost_estimate=cost(10**7, 3 * 10**7),
        name="turn_operators",
    )(ops, after)


def call_join(pieces, *after):
    rows = pieces[0].shape[0]
    return pl.pallas_call(
        join_kernel,
        out_shape=shape(4 * rows, 128),
        in_specs=[VMEM] * 4 + [ANY] * len(after),
        out_specs=VMEM,
        compiler_params=pltpu.CompilerParams(vmem_limit_bytes=8 * MIB),
        cost_estimate=cost(10**5, 8 * rows * 512),
        name="join",
    )(*pieces, *after)


def call_near(near, own, before, behind, after):
    targets, width = PAIRS, WPAIRS
    return pl.pallas_call(
        near_kernel,
        out_shape=shape(targets, 128),
        in_specs=[SMEM, VMEM, VMEM, VMEM, ANY],
        out_specs=VMEM,
        scratch_shapes=[
            pltpu.VMEM((4 * WPAIRS, 128), F32),
            pltpu.VMEM((width * FEATS, 128), F32),
            pltpu.VMEM((targets * FEATS, 128), F32),
            pltpu.VMEM((2 * width, FEAT, 128), jnp.bfloat16),
            pltpu.VMEM((LEAVES, PART, FEAT), jnp.bfloat16),
            pltpu.VMEM((2 * width, 128), F32),
        ],
        compiler_params=pltpu.CompilerParams(vmem_limit_bytes=24 * MIB),
        cost_estimate=cost(10 * targets * 2 * 64 * NEAR * 64, 3 * 10**7),
        name="near",
    )(near, own, before, behind, after)


def call_halo(lists, classes, moments, before, behind):
    return pl.pallas_call(
        halo_kernel,
        out_shape=(jax.ShapeDtypeStruct((LLIST, LEAVES), jnp.int32), shape(2 * WPAIRS, 128)),
        in_specs=[VMEM] * 5,
        out_specs=(VMEM, VMEM),
        scratch_shapes=[
            pltpu.VMEM((3, 128, 128), F32),
            pltpu.VMEM((128, 128), F32),
            pltpu.VMEM((COEF, 8, 128), F32),
            pltpu.VMEM((LEAVES, 128), F32),
        ],
        compiler_params=pltpu.CompilerParams(vmem_limit_bytes=16 * MIB),
        cost_estimate=cost(10**8, 10**6),
        name="expand_halo",
    )(lists, classes, moments, before, behind)


def call_leaf(part, code, ops, rows, after):
    return pl.pallas_call(
        functools.partial(leaf_kernel, part),
        out_shape=shape(2, OPROWS, 128),
        in_specs=[SMEM, VMEM, VMEM, ANY],
        out_specs=VMEM,
        scratch_shapes=[pltpu.VMEM((LEAF_STEP, OPROWS, 128), F32)],
        compiler_params=pltpu.CompilerParams(vmem_limit_bytes=17 * MIB),
        cost_estimate=cost(LEAVES * LLIST * COEF * COEF * 8, 2 * 10**7),
        name="leaf_translate",
    )(code, ops, rows, after)


def call_fetch(leaf_top, lists, classes):
    window = (TLIST, TOP_WINDOW)
    return pl.pallas_call(
        fetch_kernel,
        out_shape=jax.ShapeDtypeStruct((TLIST, 128), jnp.int32),
        in_specs=[SMEM, ANY, ANY],
        out_specs=VMEM,
        scratch_shapes=[
            pltpu.VMEM(window, jnp.int32), pltpu.VMEM(window, jnp.int32),
            pltpu.SemaphoreType.DMA((2,)),
        ],
        compiler_params=pltpu.CompilerParams(vmem_limit_bytes=8 * MIB),
        cost_estimate=cost(10**5, 10**5),
        name="fetch_lists",
    )(leaf_top, lists, classes)


def call_last(leaf_top, code, mine, other, *rest):
    return pl.pallas_call(
        last_kernel,
        out_shape=(shape(PAIRS, 128), jax.ShapeDtypeStruct((1,), jnp.int32)),
        in_specs=[SMEM] + [VMEM] * 11,
        out_specs=(VMEM, SMEM),
        scratch_shapes=[
            pltpu.VMEM((2 * mine.shape[0], 128), F32),
            pltpu.VMEM((2 * mine.shape[0] // SEND, 128), F32),
            pltpu.VMEM((8, 128), jnp.int32),
            pltpu.SMEM((8, 128), jnp.int32),
            pltpu.VMEM((TLIST, 128), jnp.int32),
            pltpu.SMEM((TLIST, 128), jnp.int32),
            pltpu.SemaphoreType.DMA((2,)),
        ] + FINISH_SCRATCH,
        compiler_params=pltpu.CompilerParams(vmem_limit_bytes=24 * MIB),
        name="finish",
    )(leaf_top, code, mine, other, *rest)


def call_spare(leaf_top, code, table, *rest):
    return pl.pallas_call(
        spare_kernel,
        out_shape=shape(PAIRS, 128),
        in_specs=[SMEM, SMEM] + [VMEM] * 9,
        out_specs=VMEM,
        scratch_shapes=FINISH_SCRATCH,
        compiler_params=pltpu.CompilerParams(vmem_limit_bytes=24 * MIB),
        name="finish_spare",
    )(leaf_top, code, table, *rest)


def sent_over(block, axis, count):
    return [block] + [
        lax.ppermute(block, axis, [(i, (i + s) % count) for i in range(count)])
        for s in range(1, count)
    ]


def body(
    particles, counts, leaf_top, near_list, leaf_list, leaf_class, top_list, top_class,
    m2l_ops, m2m_ops,
):
    pts = particles.reshape(4, PAIRS, 128).transpose(1, 0, 2).reshape(4 * PAIRS, 128)
    tops = leaf_top.reshape(1, LEAVES)
    m2m = m2m_ops.transpose(1, 0, 2)
    own, low, high, dist, moments, send, partial, mask = call_first(
        pts, counts, leaf_top, tops, m2m
    )
    devices = lax.axis_size(AXES)
    up = [(i, (i + 1) % devices) for i in range(devices)]
    down = [(j, i) for i, j in up]
    over_y = sent_over(send, "y", 4)
    before = lax.ppermute(high, AXES, up)
    behind = lax.ppermute(low, AXES, down)
    ops = call_turn(m2l_ops.transpose(1, 2, 0), send)
    by_y = call_join(over_y, ops, before, behind)
    over_x = sent_over(by_y, "x", 4)
    code, rows = call_halo(leaf_list.T, leaf_class.T, moments, before, behind)
    local_a = call_leaf(0, code, ops, rows, by_y)
    by_x = call_join(over_x, local_a)
    over_z = sent_over(by_x, ("zlo", "zhi"), 4)
    near = call_near(near_list.T, own, before, behind, by_x)
    mine = call_join(over_z, near)
    other = lax.ppermute(mine, "core", [(0, 1), (1, 0)])
    local_b = call_leaf(1, code, ops, rows, mine)
    top_code = call_fetch(leaf_top, top_list.T, top_class.T)
    rest = (ops, m2m, tops, local_a, local_b, dist, near, mask)
    result, over = call_last(leaf_top, top_code, mine, other, *rest)

    def spare():
        table = lax.dynamic_update_slice(
            jnp.zeros((TOPBOX + LEAVES, 128), F32), partial, (leaf_top[0], 0)
        )
        for k in range(7):
            swap = [(i, i ^ (1 << k)) for i in range(devices)]
            table = table + lax.ppermute(table, AXES, swap)
        start = jnp.minimum(leaf_top[0], TOPBOX - LEAVES)
        lists, classes = (
            lax.dynamic_slice_in_dim(x, start, LEAVES, axis=0).T for x in (top_list, top_class)
        )
        again = call_turn(m2l_ops.transpose(1, 2, 0), table)
        return call_spare(leaf_top, pack_codes(classes, lists), table, again, *rest[1:])

    result = lax.cond(over[0] >= SEND, spare, lambda: result)
    return result.reshape(-1)


def solution(mesh):
    fine = Mesh(mesh.devices.reshape(2, 2, 4, 4, 2), AXES)
    return jax.shard_map(
        body,
        mesh=fine,
        in_specs=(
            P(None, AXES), P(AXES), P(AXES), P(AXES, None), P(AXES, None), P(AXES, None),
            P(), P(), P(), P(),
        ),
        out_specs=P(AXES),
        check_vma=False,
    )
```

```python
import functools

import jax
import jax.numpy as jnp
from jax import lax
from jax.experimental import pallas as pl
from jax.experimental.pallas import tpu as pltpu
from jax.sharding import Mesh, PartitionSpec as P

ORDER = 8
COEF = 81
PART = 64
LEAVES = 256
PAIRS = 128
HALO = 32
HPAIRS = 16
WPAIRS = PAIRS + 2 * HPAIRS
NEAR = 27
LLIST = 16
TLIST = 64
TOPBOX = 4096
ROW_BITS = 13
CLASSES = 316
OPROWS = 88
SOFTENING = 0.01
SEND = 56
REACH_SQ = 16.0
FEAT = 32
FEATS = 24
LEAF_STEP = 4
TURN_STEP = 9
TOP_WINDOW = 256
BUILD_STEP = 16
NEAR_STEP = 32

HIGH = lax.Precision.HIGHEST
MIB = 1 << 20
AXES = ("zlo", "core", "y", "x", "zhi")

NN = (((1,), (0,)), ((), ()))
NT = (((1,), (1,)), ((), ()))


def dot_f32(left, right, dims=NN):
    return lax.dot_general(left, right, dims, precision=HIGH, preferred_element_type=jnp.float32)


def lanes(shape):
    return lax.broadcasted_iota(jnp.int32, shape, len(shape) - 1)


def rows_of(shape):
    return lax.broadcasted_iota(jnp.int32, shape, len(shape) - 2)


def harmonics(coord_x, coord_y, coord_z):
    radius_sq = coord_x * coord_x + coord_y * coord_y + coord_z * coord_z
    terms = {(0, 0): (None, None)}
    for m in range(1, ORDER + 1):
        if m == 1:
            terms[1, 1] = (coord_x * 0.5, coord_y * 0.5)
            continue
        re, im = terms[m - 1, m - 1]
        scale = 1.0 / (2.0 * m)
        terms[m, m] = (
            (coord_x * re - coord_y * im) * scale,
            (coord_x * im + coord_y * re) * scale,
        )
    for m in range(ORDER):
        re, im = terms[m, m]
        terms[m + 1, m] = (coord_z, None) if m == 0 else (coord_z * re, coord_z * im)
    for m in range(ORDER - 1):
        for n in range(m + 2, ORDER + 1):
            one = (2.0 * n - 1.0) / ((n - m) * (n + m))
            two = 1.0 / ((n - m) * (n + m))
            z_one = coord_z * one
            r_two = radius_sq * two
            upper, lower = terms[n - 1, m], terms[n - 2, m]
            re = z_one * upper[0] - (r_two if lower[0] is None else r_two * lower[0])
            im = None if m == 0 else z_one * upper[1] - r_two * lower[1]
            terms[n, m] = (re, im)
    listed = []
    for n in range(ORDER + 1):
        listed.append(terms[n, 0][0])
        for m in range(1, n + 1):
            listed.extend(terms[n, m])
    return listed


def centred(block):
    turned = block.T
    halves = []
    for p in range(2):
        half = turned[p * PART : (p + 1) * PART]
        halves.append(half - jnp.sum(half, axis=0, keepdims=True) * (1.0 / PART))
    return jnp.concatenate(halves, axis=0)


def expand_into(d_ref, q_ref, acc_ref, out_ref):
    for p in range(2):
        acc_ref[...] = jnp.zeros_like(acc_ref)

        def step(s, carry):
            at = pl.ds(pl.multiple_of(p * PART + s * 16, 16), 16)
            charge = q_ref[at, :]
            listed = harmonics(d_ref[0, at, :], d_ref[1, at, :], d_ref[2, at, :])
            for c, term in enumerate(listed):
                value = charge if term is None else charge * term
                acc_ref[c] += value[:8] + value[8:]
            return carry

        lax.fori_loop(0, PART // 16, step, 0)
        sums = jnp.sum(acc_ref[...], axis=1)
        full = jnp.concatenate([sums, jnp.zeros((128 - COEF, 128), jnp.float32)], axis=0)
        out_ref[pl.ds(p, PAIRS, stride=2), :] = full.T


def widen(block):
    return jnp.concatenate(
        [block, jnp.zeros((block.shape[0], 128 - block.shape[1]), jnp.float32)], axis=1
    )


def first_kernel(
    pts_ref, count_ref, top_ref, tops_ref, m2m_ref,
    own_ref, near_edge_ref, far_edge_ref, dist_ref, moment_ref, send_ref, part_ref, mask_ref,
    q_ref, acc_ref, lift_ref,
):
    lane = lanes((1, 128))

    def hold(i, carry):
        for u in range(8):
            r = i * 8 + u
            held = jnp.where(lane < PART, count_ref[2 * r], count_ref[2 * r + 1])
            mask_ref[pl.ds(r, 1), :] = jnp.where((lane & (PART - 1)) < held, 1.0, 0.0)
        return carry

    lax.fori_loop(0, PAIRS // 8, hold, 0)
    charge = pts_ref[pl.ds(3, PAIRS, stride=4), :] * mask_ref[...]
    own_ref[...] = pts_ref[...]
    own_ref[pl.ds(3, PAIRS, stride=4), :] = charge
    even = lax.axis_index("zhi") == 0
    low, high = own_ref[: 4 * HPAIRS], own_ref[4 * (PAIRS - HPAIRS) :]
    near_edge_ref[...] = jnp.where(even, high, low)
    far_edge_ref[...] = jnp.where(even, low, high)
    for c in range(3):
        dist_ref[c] = centred(pts_ref[pl.ds(c, PAIRS, stride=4), :])
    q_ref[...] = charge.T
    expand_into(dist_ref, q_ref, acc_ref, moment_ref)
    first, last = top_ref[0], top_ref[LEAVES - 1]
    for a in range(8):
        at = pl.ds(a, LEAVES // 8, stride=8)
        lift_ref[at, :] = widen(dot_f32(moment_ref[at, :][:, :COEF], m2m_ref[:, a, :], NT))
    held = jnp.where(rows_of((LEAVES, LEAVES)) == tops_ref[...] - first, 1.0, 0.0)
    wide = dot_f32(held, lift_ref[...])
    lane = lanes((LEAVES, 128))
    wide = jnp.where(lane == 127, first.astype(jnp.float32), wide)
    wide = jnp.where(lane == 126, last.astype(jnp.float32), wide)
    part_ref[...] = wide
    send_ref[...] = wide[:SEND]


def turn_kernel(in_ref, after_ref, out_ref):
    del after_ref

    def step(i, carry):
        for u in range(TURN_STEP):
            one = in_ref[i * TURN_STEP + u]
            for begin in range(0, CLASSES, 128):
                count = min(128, CLASSES - begin)
                at = pl.ds(begin * OPROWS + i * TURN_STEP + u, count, stride=OPROWS)
                out_ref[at, :] = widen(one[:, begin : begin + count].T)
        return carry

    lax.fori_loop(0, COEF // TURN_STEP, step, 0)


def join_kernel(*refs):
    out_ref = refs[-1]
    rows = refs[0].shape[0]
    for i, ref in enumerate(refs[:4]):
        out_ref[i * rows : (i + 1) * rows] = ref[...]


def split3(value):
    high = value.astype(jnp.bfloat16).astype(jnp.float32)
    rest = value - high
    middle = rest.astype(jnp.bfloat16).astype(jnp.float32)
    low = (rest - middle).astype(jnp.bfloat16).astype(jnp.float32)
    return high, middle, low


def near_kernel(
    near_ref, own_ref, partner_ref, far_ref, after_ref, out_ref,
    win_ref, src_ref, tgt_ref, source_ref, target_ref, charge_ref,
):
    del after_ref
    targets, width = PAIRS, WPAIRS
    edge = 4 * HPAIRS
    even = lax.axis_index("zhi") == 0
    win_ref[:edge] = jnp.where(even, far_ref[...], partner_ref[...])
    win_ref[edge : edge + 4 * PAIRS] = own_ref[...]
    win_ref[edge + 4 * PAIRS :] = jnp.where(even, partner_ref[...], far_ref[...])
    shift = lax.axis_index(AXES) * LEAVES - HALO

    def component(c):
        return win_ref[pl.ds(c, width, stride=4), :]

    points = [component(c) for c in range(3)]
    moved = []
    for c in range(3):
        least = jnp.min(points[c], keepdims=True)
        most = jnp.max(points[c], keepdims=True)
        moved.append(points[c] - 0.5 * (least + most))
    norm = moved[0] * moved[0] + moved[1] * moved[1] + moved[2] * moved[2]
    close = jnp.max(norm) <= REACH_SQ
    out_ref[...] = jnp.zeros_like(out_ref)

    @pl.when(close)
    def _():
        own = slice(HPAIRS, HPAIRS + targets)

        def keep(ref, f, feature):
            rows = feature.shape[0]
            ref[f * rows : (f + 1) * rows] = feature

        for c in range(3):
            h, m, l = split3(moved[c])
            for i, feature in enumerate((h, h, m, m, h, l)):
                keep(src_ref, 6 * c + i, feature)
            th, tm, tl = [-2.0 * piece[own] for piece in (h, m, l)]
            for i, feature in enumerate((th, tm, th, tm, tl, th)):
                keep(tgt_ref, 6 * c + i, feature)
        ones = jnp.ones((width, 128), jnp.float32)
        for i, feature in enumerate(split3(norm + SOFTENING)):
            keep(src_ref, 18 + i, feature)
            keep(tgt_ref, 18 + i, ones[own])
        for i, feature in enumerate(split3(norm[own])):
            keep(src_ref, 21 + i, ones)
            keep(tgt_ref, 21 + i, feature)
        charge = component(3)
        charge_ref[pl.ds(0, width, stride=2), :] = charge
        charge_ref[pl.ds(1, width, stride=2), :] = pltpu.roll(charge, PART, 1)
        rest = jnp.zeros((FEAT - FEATS, 128), jnp.float32)

        def build_source(i, carry):
            for u in range(BUILD_STEP):
                r = i * BUILD_STEP + u
                some = src_ref[pl.ds(r, FEATS, stride=width), :]
                some = jnp.concatenate([some, rest], axis=0)
                source_ref[2 * r] = some.astype(jnp.bfloat16)
                source_ref[2 * r + 1] = pltpu.roll(some, PART, 1).astype(jnp.bfloat16)
            return carry

        def build_target(i, carry):
            for u in range(BUILD_STEP):
                r = i * BUILD_STEP + u
                some = tgt_ref[pl.ds(r, FEATS, stride=targets), :]
                some = jnp.concatenate([some, rest], axis=0).T.astype(jnp.bfloat16)
                for p in range(2):
                    target_ref[2 * r + p] = some[p * PART : (p + 1) * PART]
            return carry

        lax.fori_loop(0, width // BUILD_STEP, build_source, 0)
        lax.fori_loop(0, targets // BUILD_STEP, build_target, 0)

        low_block = lanes((FEAT, 128)) < PART
        low_row = lanes((1, 128)) < PART
        lane = lanes((PART, 128))

        def leaf_sums(l):
            total = None
            for k in range(0, NEAR + 1, 4):
                blocks, charges = [], []
                for j in range(k, k + 4, 2):
                    one = near_ref[j, l] - shift
                    two = (near_ref[min(j + 1, NEAR - 1), l] - shift) ^ 1
                    blocks.append(jnp.where(low_block, source_ref[one], source_ref[two]))
                    other = charge_ref[pl.ds(two, 1), :] if j + 1 < NEAR else 0.0
                    charges.append(jnp.where(low_row, charge_ref[pl.ds(one, 1), :], other))
                dist = lax.dot_general(
                    target_ref[l], jnp.concatenate(blocks, axis=1), NN,
                    preferred_element_type=jnp.float32,
                )
                for j in range(2):
                    term = charges[j] * lax.rsqrt(dist[:, j * 128 : (j + 1) * 128])
                    total = term if total is None else total + term
            return total

        def group(i, carry):
            totals = [leaf_sums(i * NEAR_STEP + u) for u in range(NEAR_STEP)]
            for p in range(2):
                at = pl.ds(p * PART, PART)
                wide = out_ref[at, :]
                for u in range(p, NEAR_STEP, 2):
                    sums = jnp.sum(totals[u], axis=1, keepdims=True)
                    wide = jnp.where(lane == i * (NEAR_STEP // 2) + u // 2, sums, wide)
                out_ref[at, :] = wide
            return carry

        lax.fori_loop(0, LEAVES // NEAR_STEP, group, 0)

    @pl.when(jnp.logical_not(close))
    def _():
        lane = lanes((PART, 128))

        def pair(r, carry):
            columns = [
                jnp.broadcast_to(
                    win_ref[pl.ds(4 * (HPAIRS + r) + c, 1), :], (128, 128)
                ).T
                for c in range(3)
            ]
            for p in range(2):
                mine = [column[p * PART : (p + 1) * PART] for column in columns]

                def entry(k, total):
                    leaf = near_ref[k, 2 * r + p] - shift
                    at = 4 * (leaf // 2)
                    gap = SOFTENING
                    for c in range(3):
                        diff = mine[c] - win_ref[pl.ds(at + c, 1), :]
                        gap = gap + diff * diff
                    half = jnp.where((lane // PART) == leaf % 2, 1.0, 0.0)
                    return total + half * (win_ref[pl.ds(at + 3, 1), :] * lax.rsqrt(gap))

                total = lax.fori_loop(0, NEAR, entry, jnp.zeros((PART, 128), jnp.float32))
                at = pl.ds(p * PART, PART)
                sums = jnp.sum(total, axis=1, keepdims=True)
                out_ref[at, :] = jnp.where(lane == r, sums, out_ref[at, :])
            return carry

        lax.fori_loop(0, targets, pair, 0)


def gather_products(codes, ops_ref, rows_ref):
    total = None
    for code in codes:
        at = pl.ds(pl.multiple_of(code >> ROW_BITS, 8), OPROWS)
        row = rows_ref[pl.ds(code & ((1 << ROW_BITS) - 1), 8, stride=0), :]
        term = ops_ref[at, :].reshape(OPROWS // 8, 8, 128) * row[None]
        total = term if total is None else total + term
    return total.reshape(OPROWS, 128)


def pack_codes(kinds, rows):
    return ((kinds * OPROWS) << ROW_BITS) | rows


def put_sums(total_ref, out_ref, lane):
    sums = jnp.sum(total_ref[...], axis=1, keepdims=True)
    out_ref[...] = jnp.where(lanes((OPROWS, 128)) == lane, sums, out_ref[...])


def halo_kernel(
    top_ref, top_list_ref, top_class_ref,
    list_ref, class_ref, moment_ref, partner_ref, far_ref, code_ref, rows_ref, top_code_ref,
    d_ref, q_ref, acc_ref, halo_ref, list_vmem, class_vmem, sems,
):
    window = pl.ds(pl.multiple_of(window_start(top_ref), 128), TOP_WINDOW)
    copies = [
        pltpu.make_async_copy(top_list_ref.at[:, window], list_vmem, sems.at[0]),
        pltpu.make_async_copy(top_class_ref.at[:, window], class_vmem, sems.at[1]),
    ]
    for copy in copies:
        copy.start()
    even = lax.axis_index("zhi") == 0
    shift = lax.axis_index(AXES) * LEAVES - HALO
    code_ref[...] = pack_codes(class_ref[...], list_ref[...] - shift)
    fill = jnp.zeros((PAIRS - 2 * HPAIRS, 128), jnp.float32)

    def component(c):
        at = pl.ds(c, HPAIRS, stride=4)
        one, two = partner_ref[at, :], far_ref[at, :]
        return jnp.concatenate(
            [jnp.where(even, two, one), jnp.where(even, one, two), fill], axis=0
        )

    for c in range(3):
        d_ref[c] = centred(component(c))
    q_ref[...] = component(3).T
    expand_into(d_ref, q_ref, acc_ref, halo_ref)
    rows_ref[:HALO] = halo_ref[:HALO]
    rows_ref[HALO : HALO + LEAVES] = moment_ref[...]
    rows_ref[HALO + LEAVES :] = halo_ref[HALO : 2 * HALO]
    for copy in copies:
        copy.wait()
    codes = pack_codes(class_vmem[...], list_vmem[...])
    ahead = top_ref[0] - window_start(top_ref)
    top_code_ref[...] = pltpu.roll(codes, (TOP_WINDOW - ahead) % TOP_WINDOW, 1)[:, :128]


def leaf_kernel(part, code_ref, ops_ref, rows_ref, after_ref, out_ref, total_ref):
    del after_ref
    begin = part * (PAIRS // 2)
    lane = lanes((OPROWS, 128))

    def reduce(i):
        for p in range(2):
            wide = out_ref[p]
            for v in range(p, LEAF_STEP, 2):
                at = begin + i * (LEAF_STEP // 2) + v // 2
                wide = jnp.where(lane == at, jnp.sum(total_ref[v], axis=1, keepdims=True), wide)
            out_ref[p] = wide

    def step(i, carry):
        reduce(i - 1)
        for v in range(LEAF_STEP):
            leaf = 2 * begin + i * LEAF_STEP + v
            total_ref[v] = gather_products(
                [code_ref[k, leaf] for k in range(LLIST)], ops_ref, rows_ref
            )
        return carry

    total_ref[...] = jnp.zeros_like(total_ref)
    out_ref[...] = jnp.zeros_like(out_ref)
    steps = LEAVES // 2 // LEAF_STEP
    lax.fori_loop(0, steps, step, 0)
    reduce(steps - 1)


def window_start(top_ref):
    return jnp.minimum(top_ref[0] // 128 * 128, TOPBOX - TOP_WINDOW)


def finish(
    cap, shift, top_ref, code_ref, table_ref, ops_ref, m2m_ref, tops_ref, local_refs, dist_ref,
    near_ref, mask_ref, out_ref, field_ref, pot_ref, total_ref, wide_ref, rows_ref,
):
    first = top_ref[0]
    boxes = top_ref[LEAVES - 1] - first + 1
    spread = jnp.zeros((OPROWS, LEAVES), jnp.float32)
    width = min(cap, 128)
    for block in range(cap // width):
        total_ref[...] = jnp.zeros_like(total_ref)
        wide_ref[...] = jnp.zeros_like(wide_ref)

        def step(b, carry):
            put_sums(total_ref, wide_ref, b - 1)
            column = shift + block * width + b
            total_ref[...] = gather_products(
                [code_ref[k, column] for k in range(TLIST)], ops_ref, table_ref
            )
            return carry

        count = jnp.clip(boxes - block * width, 0, width)
        lax.fori_loop(0, count, step, 0)
        put_sums(total_ref, wide_ref, count - 1)
        place = rows_of((128, LEAVES)) + block * width
        held = jnp.where(place == tops_ref[...] - first, 1.0, 0.0)
        spread += dot_f32(wide_ref[...], held)
    full = jnp.concatenate([spread, jnp.zeros((128 - OPROWS, LEAVES), jnp.float32)], axis=0)
    rows_ref[...] = full.T
    for a in range(8):
        at = pl.ds(a, LEAVES // 8, stride=8)
        rows_ref[at, :] = widen(dot_f32(rows_ref[at, :][:, :COEF], m2m_ref[:, a, :]))
    for p in range(2):
        field_ref[p] = (
            rows_ref[pl.ds(p, PAIRS, stride=2), :].T[:OPROWS]
            + local_refs[0][p] + local_refs[1][p]
        )
    for p in range(2):

        def step(s, carry):
            at = pl.ds(pl.multiple_of(p * PART + s * 16, 16), 16)
            listed = harmonics(dist_ref[0, at, :], dist_ref[1, at, :], dist_ref[2, at, :])
            total = None
            for c, term in enumerate(listed):
                weight = field_ref[p, pl.ds(c, 1), :]
                value = jnp.broadcast_to(weight, (16, 128)) if term is None else term * weight
                total = value if total is None else total + value
            pot_ref[at, :] = total
            return carry

        lax.fori_loop(0, PART // 16, step, 0)
    out_ref[...] = (near_ref[...] + pot_ref[...]).T * mask_ref[...]


def last_kernel(
    top_ref, code_ref, mine_ref, other_ref, ops_ref, m2m_ref, tops_ref, local_a_ref, local_b_ref,
    dist_ref, near_ref, mask_ref, out_ref, over_ref,
    table_ref, rest_ref, meta_ref, ends_ref, packed_ref, scalar_ref, sems, *scratch,
):
    half = mine_ref.shape[0]
    blocks = half // SEND
    table_ref[:half] = mine_ref[...]
    table_ref[half:] = other_ref[...]
    heads = pl.ds(0, 2 * blocks, stride=SEND)
    turned = table_ref[heads, :].T[120:]
    meta_ref[...] = turned.astype(jnp.int32)
    copy = pltpu.make_async_copy(meta_ref, ends_ref, sems.at[0])
    copy.start()
    most = jnp.max(turned[6:7] - turned[7:8]).astype(jnp.int32) + 1
    over_ref[0] = most
    core, my_y, my_x = lax.axis_index("core"), lax.axis_index("y"), lax.axis_index("x")
    my_z = lax.axis_index(("zlo", "zhi"))
    by_z = [(my_z ^ z) * 16 for z in range(4)]
    by_x = [(my_x ^ x) * 4 for x in range(4)]
    by_y = [my_y ^ y for y in range(4)]
    by_core = [blocks * (core ^ side) for side in range(2)]
    order = [
        by_z[zlo * 2 + zhi] + by_x[x] + by_y[y] + by_core[side]
        for zlo in range(2) for side in range(2) for y in range(4) for x in range(4)
        for zhi in range(2)
    ]
    copy.wait()

    @pl.when(most < SEND)
    def _():
        code = code_ref[...]
        box = code & ((1 << ROW_BITS) - 1)
        row = code
        last, last_begin = 0, 0
        rest_ref[pl.ds(order[0], 1), :] = jnp.zeros((1, 128), jnp.float32)
        for d, block in enumerate(order):
            begin = ends_ref[7, block]
            base = block * SEND
            if d:
                rest_ref[pl.ds(block, 1), :] = table_ref[pl.ds(last + begin - last_begin, 1), :]
                row += jnp.where(box >= begin, base - begin - last + last_begin, 0)
            else:
                row += base - begin
            last, last_begin = base, begin
        packed_ref[...] = row
        copy = pltpu.make_async_copy(packed_ref, scalar_ref, sems.at[1])
        copy.start()
        table_ref[heads, :] += rest_ref[...]
        copy.wait()
        finish(
            64, 0, top_ref, scalar_ref, table_ref, ops_ref, m2m_ref, tops_ref,
            (local_a_ref, local_b_ref), dist_ref, near_ref, mask_ref, out_ref, *scratch,
        )


def spare_kernel(
    top_ref, code_ref, table_ref, ops_ref, m2m_ref, tops_ref, local_a_ref, local_b_ref,
    dist_ref, near_ref, mask_ref, out_ref, *scratch,
):
    finish(
        LEAVES, top_ref[0] - jnp.minimum(top_ref[0], TOPBOX - LEAVES), top_ref, code_ref, table_ref, ops_ref, m2m_ref, tops_ref,
        (local_a_ref, local_b_ref), dist_ref, near_ref, mask_ref, out_ref, *scratch,
    )


SMEM = pl.BlockSpec(memory_space=pltpu.SMEM)
VMEM = pl.BlockSpec(memory_space=pltpu.VMEM)
F32 = jnp.float32


def shape(*dims):
    return jax.ShapeDtypeStruct(dims, F32)


ANY = pl.BlockSpec(memory_space=pl.ANY)
HBM = pl.BlockSpec(memory_space=pltpu.HBM)
FINISH_SCRATCH = [
    pltpu.VMEM((2, OPROWS, 128), F32),
    pltpu.VMEM((128, 128), F32),
    pltpu.VMEM((OPROWS, 128), F32),
    pltpu.VMEM((OPROWS, 128), F32),
    pltpu.VMEM((LEAVES, 128), F32),
]


def cost(flops, bytes_accessed):
    return pl.CostEstimate(flops=flops, bytes_accessed=bytes_accessed, transcendentals=0)


def call_first(pts, counts, leaf_top, tops, m2m):
    return pl.pallas_call(
        first_kernel,
        out_shape=(
            shape(4 * PAIRS, 128), shape(4 * HPAIRS, 128), shape(4 * HPAIRS, 128),
            shape(3, PAIRS, 128), shape(LEAVES, 128), shape(SEND, 128), shape(LEAVES, 128),
            shape(PAIRS, 128),
        ),
        in_specs=[VMEM, SMEM, SMEM, VMEM, VMEM],
        out_specs=(VMEM,) * 8,
        scratch_shapes=[
            pltpu.VMEM((128, 128), F32), pltpu.VMEM((COEF, 8, 128), F32),
            pltpu.VMEM((LEAVES, 128), F32),
        ],
        compiler_params=pltpu.CompilerParams(vmem_limit_bytes=16 * MIB),
        cost_estimate=cost(10**9, 10**7),
        name="expand_own",
    )(pts, counts, leaf_top, tops, m2m)


def call_turn(ops, after):
    return pl.pallas_call(
        turn_kernel,
        out_shape=shape(CLASSES * OPROWS, 128),
        in_specs=[VMEM, ANY],
        out_specs=VMEM,
        compiler_params=pltpu.CompilerParams(vmem_limit_bytes=26 * MIB),
        cost_estimate=cost(10**7, 3 * 10**7),
        name="turn_operators",
    )(ops, after)


def call_join(pieces, *after):
    rows = pieces[0].shape[0]
    return pl.pallas_call(
        join_kernel,
        out_shape=shape(4 * rows, 128),
        in_specs=[VMEM] * 4 + [ANY] * len(after),
        out_specs=VMEM,
        compiler_params=pltpu.CompilerParams(vmem_limit_bytes=8 * MIB),
        cost_estimate=cost(10**5, 8 * rows * 512),
        name="join",
    )(*pieces, *after)


def call_near(near, own, before, behind, after):
    targets, width = PAIRS, WPAIRS
    return pl.pallas_call(
        near_kernel,
        out_shape=shape(targets, 128),
        in_specs=[SMEM, VMEM, VMEM, VMEM, ANY],
        out_specs=VMEM,
        scratch_shapes=[
            pltpu.VMEM((4 * WPAIRS, 128), F32),
            pltpu.VMEM((width * FEATS, 128), F32),
            pltpu.VMEM((targets * FEATS, 128), F32),
            pltpu.VMEM((2 * width, FEAT, 128), jnp.bfloat16),
            pltpu.VMEM((LEAVES, PART, FEAT), jnp.bfloat16),
            pltpu.VMEM((2 * width, 128), F32),
        ],
        compiler_params=pltpu.CompilerParams(vmem_limit_bytes=24 * MIB),
        cost_estimate=cost(10 * targets * 2 * 64 * NEAR * 64, 3 * 10**7),
        name="near",
    )(near, own, before, behind, after)


def call_halo(leaf_top, top_lists, top_classes, lists, classes, moments, partner, far):
    return pl.pallas_call(
        halo_kernel,
        out_shape=(
            jax.ShapeDtypeStruct((LLIST, LEAVES), jnp.int32), shape(2 * WPAIRS, 128),
            jax.ShapeDtypeStruct((TLIST, 128), jnp.int32),
        ),
        in_specs=[SMEM, HBM, HBM] + [VMEM] * 5,
        out_specs=(VMEM,) * 3,
        scratch_shapes=[
            pltpu.VMEM((3, 128, 128), F32),
            pltpu.VMEM((128, 128), F32),
            pltpu.VMEM((COEF, 8, 128), F32),
            pltpu.VMEM((LEAVES, 128), F32),
            pltpu.VMEM((TLIST, TOP_WINDOW), jnp.int32),
            pltpu.VMEM((TLIST, TOP_WINDOW), jnp.int32),
            pltpu.SemaphoreType.DMA((2,)),
        ],
        compiler_params=pltpu.CompilerParams(vmem_limit_bytes=16 * MIB),
        cost_estimate=cost(10**8, 10**6),
        name="expand_halo",
    )(leaf_top, top_lists, top_classes, lists, classes, moments, partner, far)


def call_leaf(part, code, ops, rows, after):
    return pl.pallas_call(
        functools.partial(leaf_kernel, part),
        out_shape=shape(2, OPROWS, 128),
        in_specs=[SMEM, VMEM, VMEM, ANY],
        out_specs=VMEM,
        scratch_shapes=[pltpu.VMEM((LEAF_STEP, OPROWS, 128), F32)],
        compiler_params=pltpu.CompilerParams(vmem_limit_bytes=17 * MIB),
        cost_estimate=cost(LEAVES * LLIST * COEF * COEF * 8, 2 * 10**7),
        name="leaf_translate",
    )(code, ops, rows, after)


def call_last(leaf_top, code, mine, other, *rest):
    return pl.pallas_call(
        last_kernel,
        out_shape=(shape(PAIRS, 128), jax.ShapeDtypeStruct((1,), jnp.int32)),
        in_specs=[SMEM] + [VMEM] * 11,
        out_specs=(VMEM, SMEM),
        scratch_shapes=[
            pltpu.VMEM((2 * mine.shape[0], 128), F32),
            pltpu.VMEM((2 * mine.shape[0] // SEND, 128), F32),
            pltpu.VMEM((8, 128), jnp.int32),
            pltpu.SMEM((8, 128), jnp.int32),
            pltpu.VMEM((TLIST, 128), jnp.int32),
            pltpu.SMEM((TLIST, 128), jnp.int32),
            pltpu.SemaphoreType.DMA((2,)),
        ] + FINISH_SCRATCH,
        compiler_params=pltpu.CompilerParams(vmem_limit_bytes=24 * MIB),
        name="finish",
    )(leaf_top, code, mine, other, *rest)


def call_spare(leaf_top, code, table, *rest):
    return pl.pallas_call(
        spare_kernel,
        out_shape=shape(PAIRS, 128),
        in_specs=[SMEM, SMEM] + [VMEM] * 9,
        out_specs=VMEM,
        scratch_shapes=FINISH_SCRATCH,
        compiler_params=pltpu.CompilerParams(vmem_limit_bytes=24 * MIB),
        name="finish_spare",
    )(leaf_top, code, table, *rest)


def sent_over(block, axis):
    return [block] + [
        lax.ppermute(block, axis, [(i, i ^ s) for i in range(4)]) for s in range(1, 4)
    ]


def body(
    particles, counts, leaf_top, near_list, leaf_list, leaf_class, top_list, top_class,
    m2l_ops, m2m_ops,
):
    pts = particles.reshape(4, PAIRS, 128).transpose(1, 0, 2).reshape(4 * PAIRS, 128)
    tops = leaf_top.reshape(1, LEAVES)
    m2m = m2m_ops.transpose(1, 0, 2)
    own, near_edge, far_edge, dist, moments, send, partial, mask = call_first(
        pts, counts, leaf_top, tops, m2m
    )
    devices = lax.axis_size(AXES)
    partner = [(i, i ^ 1) for i in range(devices)]
    far = [(i, (i + 2 * (i & 1) - 1) % devices) for i in range(devices)]
    over_y = sent_over(send, "y")
    from_partner = lax.ppermute(near_edge, AXES, partner)
    from_far = lax.ppermute(far_edge, AXES, far)
    ops = call_turn(m2l_ops.transpose(1, 2, 0), send)
    by_y = call_join(over_y, ops, from_partner, from_far)
    over_x = sent_over(by_y, "x")
    code, rows, top_code = call_halo(
        leaf_top, top_list.T, top_class.T, leaf_list.T, leaf_class.T, moments,
        from_partner, from_far,
    )
    local_a = call_leaf(0, code, ops, rows, by_y)
    by_x = call_join(over_x, local_a)
    over_z = sent_over(by_x, ("zlo", "zhi"))
    near = call_near(near_list.T, own, from_partner, from_far, by_x)
    mine = call_join(over_z, near)
    other = lax.ppermute(mine, "core", [(0, 1), (1, 0)])
    local_b = call_leaf(1, code, ops, rows, mine)
    rest = (ops, m2m, tops, local_a, local_b, dist, near, mask)
    result, over = call_last(leaf_top, top_code, mine, other, *rest)

    def spare():
        table = lax.dynamic_update_slice(
            jnp.zeros((TOPBOX + LEAVES, 128), F32), partial, (leaf_top[0], 0)
        )
        for k in range(7):
            swap = [(i, i ^ (1 << k)) for i in range(devices)]
            table = table + lax.ppermute(table, AXES, swap)
        start = jnp.minimum(leaf_top[0], TOPBOX - LEAVES)
        lists, classes = (
            lax.dynamic_slice_in_dim(x, start, LEAVES, axis=0).T for x in (top_list, top_class)
        )
        again = call_turn(m2l_ops.transpose(1, 2, 0), table)
        return call_spare(leaf_top, pack_codes(classes, lists), table, again, *rest[1:])

    result = lax.cond(over[0] >= SEND, spare, lambda: result)
    return result.reshape(-1)


def solution(mesh):
    fine = Mesh(mesh.devices.reshape(2, 2, 4, 4, 2), AXES)
    return jax.shard_map(
        body,
        mesh=fine,
        in_specs=(
            P(None, AXES), P(AXES), P(AXES), P(AXES, None), P(AXES, None), P(AXES, None),
            P(), P(), P(), P(),
        ),
        out_specs=P(AXES),
        check_vma=False,
    )
```

```python
import functools

import jax
import jax.numpy as jnp
from jax import lax
from jax.experimental import pallas as pl
from jax.experimental.pallas import tpu as pltpu
from jax.sharding import Mesh, PartitionSpec as P

ORDER = 8
COEF = 81
PART = 64
LEAVES = 256
PAIRS = 128
HALO = 32
HPAIRS = 16
WPAIRS = PAIRS + 2 * HPAIRS
NEAR = 27
LLIST = 16
TLIST = 64
TOPBOX = 4096
ROW_BITS = 13
CLASSES = 316
OPROWS = 88
SOFTENING = 0.01
SEND = 56
REACH_SQ = 16.0
FEAT = 32
FEATS = 24
LEAF_STEP = 4
TURN_STEP = 27
TOP_WINDOW = 256
BUILD_STEP = 16
NEAR_STEP = 32

HIGH = lax.Precision.HIGHEST
MIB = 1 << 20
AXES = ("zlo", "core", "y", "x", "zhi")

NN = (((1,), (0,)), ((), ()))
NT = (((1,), (1,)), ((), ()))


def dot_f32(left, right, dims=NN):
    return lax.dot_general(left, right, dims, precision=HIGH, preferred_element_type=jnp.float32)


def lanes(shape):
    return lax.broadcasted_iota(jnp.int32, shape, len(shape) - 1)


def rows_of(shape):
    return lax.broadcasted_iota(jnp.int32, shape, len(shape) - 2)


def harmonics(coord_x, coord_y, coord_z):
    radius_sq = coord_x * coord_x + coord_y * coord_y + coord_z * coord_z
    terms = {(0, 0): (None, None)}
    for m in range(1, ORDER + 1):
        if m == 1:
            terms[1, 1] = (coord_x * 0.5, coord_y * 0.5)
            continue
        re, im = terms[m - 1, m - 1]
        scale = 1.0 / (2.0 * m)
        terms[m, m] = (
            (coord_x * re - coord_y * im) * scale,
            (coord_x * im + coord_y * re) * scale,
        )
    for m in range(ORDER):
        re, im = terms[m, m]
        terms[m + 1, m] = (coord_z, None) if m == 0 else (coord_z * re, coord_z * im)
    for m in range(ORDER - 1):
        for n in range(m + 2, ORDER + 1):
            one = (2.0 * n - 1.0) / ((n - m) * (n + m))
            two = 1.0 / ((n - m) * (n + m))
            z_one = coord_z * one
            r_two = radius_sq * two
            upper, lower = terms[n - 1, m], terms[n - 2, m]
            re = z_one * upper[0] - (r_two if lower[0] is None else r_two * lower[0])
            im = None if m == 0 else z_one * upper[1] - r_two * lower[1]
            terms[n, m] = (re, im)
    listed = []
    for n in range(ORDER + 1):
        listed.append(terms[n, 0][0])
        for m in range(1, n + 1):
            listed.extend(terms[n, m])
    return listed


def centred(block):
    turned = block.T
    halves = []
    for p in range(2):
        half = turned[p * PART : (p + 1) * PART]
        halves.append(half - jnp.sum(half, axis=0, keepdims=True) * (1.0 / PART))
    return jnp.concatenate(halves, axis=0)


def expand_into(d_ref, q_ref, acc_ref, out_ref):
    for p in range(2):
        acc_ref[...] = jnp.zeros_like(acc_ref)

        def step(s, carry):
            at = pl.ds(pl.multiple_of(p * PART + s * 16, 16), 16)
            charge = q_ref[at, :]
            listed = harmonics(d_ref[0, at, :], d_ref[1, at, :], d_ref[2, at, :])
            for c, term in enumerate(listed):
                value = charge if term is None else charge * term
                acc_ref[c] += value[:8] + value[8:]
            return carry

        lax.fori_loop(0, PART // 16, step, 0)
        sums = jnp.sum(acc_ref[...], axis=1)
        full = jnp.concatenate([sums, jnp.zeros((128 - COEF, 128), jnp.float32)], axis=0)
        out_ref[pl.ds(p, PAIRS, stride=2), :] = full.T


def widen(block):
    return jnp.concatenate(
        [block, jnp.zeros((block.shape[0], 128 - block.shape[1]), jnp.float32)], axis=1
    )


def first_kernel(
    pts_ref, count_ref, top_ref, tops_ref, m2m_ref,
    own_ref, near_edge_ref, far_edge_ref, dist_ref, moment_ref, send_ref, lift_ref, mask_ref,
    q_ref, acc_ref,
):
    lane = lanes((1, 128))

    def hold(i, carry):
        for u in range(8):
            r = i * 8 + u
            held = jnp.where(lane < PART, count_ref[0, 2 * r], count_ref[0, 2 * r + 1])
            mask_ref[pl.ds(r, 1), :] = jnp.where((lane & (PART - 1)) < held, 1.0, 0.0)
        return carry

    lax.fori_loop(0, PAIRS // 8, hold, 0)
    charge = pts_ref[pl.ds(3, PAIRS, stride=4), :] * mask_ref[...]
    own_ref[...] = pts_ref[...]
    own_ref[pl.ds(3, PAIRS, stride=4), :] = charge
    even = lax.axis_index("zhi") == 0
    low, high = own_ref[: 4 * HPAIRS], own_ref[4 * (PAIRS - HPAIRS) :]
    near_edge_ref[...] = jnp.where(even, high, low)
    far_edge_ref[...] = jnp.where(even, low, high)
    for c in range(3):
        dist_ref[c] = centred(pts_ref[pl.ds(c, PAIRS, stride=4), :])
    q_ref[...] = charge.T
    expand_into(dist_ref, q_ref, acc_ref, moment_ref)
    first, last = top_ref[0], top_ref[LEAVES - 1]
    for a in range(8):
        at = pl.ds(a, LEAVES // 8, stride=8)
        lift_ref[at, :] = widen(dot_f32(moment_ref[at, :][:, :COEF], m2m_ref[:, a, :], NT))
    held = jnp.where(rows_of((SEND, LEAVES)) == tops_ref[...] - first, 1.0, 0.0)
    wide = dot_f32(held, lift_ref[...])
    lane = lanes((SEND, 128))
    wide = jnp.where(lane == 127, first.astype(jnp.float32), wide)
    wide = jnp.where(lane == 126, last.astype(jnp.float32), wide)
    send_ref[...] = wide


def turn_kernel(in_ref, after_ref, out_ref):
    del after_ref

    def step(i, carry):
        for u in range(TURN_STEP):
            one = in_ref[i * TURN_STEP + u]
            for begin in range(0, CLASSES, 128):
                count = min(128, CLASSES - begin)
                at = pl.ds(begin * OPROWS + i * TURN_STEP + u, count, stride=OPROWS)
                out_ref[at, :] = widen(one[:, begin : begin + count].T)
        return carry

    lax.fori_loop(0, COEF // TURN_STEP, step, 0)


def join_kernel(*refs):
    out_ref = refs[-1]
    rows = refs[0].shape[0]
    for i, ref in enumerate(refs[:4]):
        out_ref[i * rows : (i + 1) * rows] = ref[...]


def split3(value):
    high = value.astype(jnp.bfloat16).astype(jnp.float32)
    rest = value - high
    middle = rest.astype(jnp.bfloat16).astype(jnp.float32)
    low = (rest - middle).astype(jnp.bfloat16).astype(jnp.float32)
    return high, middle, low


def near_kernel(
    list_ref, own_ref, partner_ref, far_ref, after_ref, out_ref,
    win_ref, src_ref, tgt_ref, source_ref, target_ref, charge_ref, near_ref, sem,
):
    del after_ref
    targets, width = PAIRS, WPAIRS
    edge = 4 * HPAIRS
    lists = pltpu.make_async_copy(list_ref, near_ref, sem)
    lists.start()
    even = lax.axis_index("zhi") == 0
    win_ref[:edge] = jnp.where(even, far_ref[...], partner_ref[...])
    win_ref[edge : edge + 4 * PAIRS] = own_ref[...]
    win_ref[edge + 4 * PAIRS :] = jnp.where(even, partner_ref[...], far_ref[...])
    shift = lax.axis_index(AXES) * LEAVES - HALO

    def component(c):
        return win_ref[pl.ds(c, width, stride=4), :]

    points = [component(c) for c in range(3)]
    moved = []
    for c in range(3):
        least = jnp.min(points[c], keepdims=True)
        most = jnp.max(points[c], keepdims=True)
        moved.append(points[c] - 0.5 * (least + most))
    norm = moved[0] * moved[0] + moved[1] * moved[1] + moved[2] * moved[2]
    close = jnp.max(norm) <= REACH_SQ
    out_ref[...] = jnp.zeros_like(out_ref)

    @pl.when(close)
    def _():
        own = slice(HPAIRS, HPAIRS + targets)

        def keep(ref, f, feature):
            rows = feature.shape[0]
            ref[f * rows : (f + 1) * rows] = feature

        for c in range(3):
            h, m, l = split3(moved[c])
            for i, feature in enumerate((h, h, m, m, h, l)):
                keep(src_ref, 6 * c + i, feature)
            th, tm, tl = [-2.0 * piece[own] for piece in (h, m, l)]
            for i, feature in enumerate((th, tm, th, tm, tl, th)):
                keep(tgt_ref, 6 * c + i, feature)
        ones = jnp.ones((width, 128), jnp.float32)
        for i, feature in enumerate(split3(norm + SOFTENING)):
            keep(src_ref, 18 + i, feature)
            keep(tgt_ref, 18 + i, ones[own])
        for i, feature in enumerate(split3(norm[own])):
            keep(src_ref, 21 + i, ones)
            keep(tgt_ref, 21 + i, feature)
        charge = component(3)
        charge_ref[pl.ds(0, width, stride=2), :] = charge
        charge_ref[pl.ds(1, width, stride=2), :] = pltpu.roll(charge, PART, 1)
        rest = jnp.zeros((FEAT - FEATS, 128), jnp.float32)

        def build_source(i, carry):
            for u in range(BUILD_STEP):
                r = i * BUILD_STEP + u
                some = src_ref[pl.ds(r, FEATS, stride=width), :]
                some = jnp.concatenate([some, rest], axis=0)
                source_ref[2 * r] = some.astype(jnp.bfloat16)
                source_ref[2 * r + 1] = pltpu.roll(some, PART, 1).astype(jnp.bfloat16)
            return carry

        def build_target(i, carry):
            for u in range(BUILD_STEP):
                r = i * BUILD_STEP + u
                some = tgt_ref[pl.ds(r, FEATS, stride=targets), :]
                some = jnp.concatenate([some, rest], axis=0).T.astype(jnp.bfloat16)
                for p in range(2):
                    target_ref[2 * r + p] = some[p * PART : (p + 1) * PART]
            return carry

        lax.fori_loop(0, width // BUILD_STEP, build_source, 0)
        lax.fori_loop(0, targets // BUILD_STEP, build_target, 0)
        lists.wait()

        low_block = lanes((FEAT, 128)) < PART
        low_row = lanes((1, 128)) < PART
        lane = lanes((PART, 128))

        def leaf_sums(l):
            total = None
            for k in range(0, NEAR + 1, 4):
                blocks, charges = [], []
                for j in range(k, k + 4, 2):
                    one = near_ref[j, l] - shift
                    two = (near_ref[min(j + 1, NEAR - 1), l] - shift) ^ 1
                    blocks.append(jnp.where(low_block, source_ref[one], source_ref[two]))
                    other = charge_ref[pl.ds(two, 1), :] if j + 1 < NEAR else 0.0
                    charges.append(jnp.where(low_row, charge_ref[pl.ds(one, 1), :], other))
                dist = lax.dot_general(
                    target_ref[l], jnp.concatenate(blocks, axis=1), NN,
                    preferred_element_type=jnp.float32,
                )
                for j in range(2):
                    term = charges[j] * lax.rsqrt(dist[:, j * 128 : (j + 1) * 128])
                    total = term if total is None else total + term
            return total

        def group(i, carry):
            totals = [leaf_sums(i * NEAR_STEP + u) for u in range(NEAR_STEP)]
            for p in range(2):
                at = pl.ds(p * PART, PART)
                wide = out_ref[at, :]
                for u in range(p, NEAR_STEP, 2):
                    sums = jnp.sum(totals[u], axis=1, keepdims=True)
                    wide = jnp.where(lane == i * (NEAR_STEP // 2) + u // 2, sums, wide)
                out_ref[at, :] = wide
            return carry

        lax.fori_loop(0, LEAVES // NEAR_STEP, group, 0)

    @pl.when(jnp.logical_not(close))
    def _():
        lane = lanes((PART, 128))
        lists.wait()

        def pair(r, carry):
            columns = [
                jnp.broadcast_to(
                    win_ref[pl.ds(4 * (HPAIRS + r) + c, 1), :], (128, 128)
                ).T
                for c in range(3)
            ]
            for p in range(2):
                mine = [column[p * PART : (p + 1) * PART] for column in columns]

                def entry(k, total):
                    leaf = near_ref[k, 2 * r + p] - shift
                    at = 4 * (leaf // 2)
                    gap = SOFTENING
                    for c in range(3):
                        diff = mine[c] - win_ref[pl.ds(at + c, 1), :]
                        gap = gap + diff * diff
                    half = jnp.where((lane // PART) == leaf % 2, 1.0, 0.0)
                    return total + half * (win_ref[pl.ds(at + 3, 1), :] * lax.rsqrt(gap))

                total = lax.fori_loop(0, NEAR, entry, jnp.zeros((PART, 128), jnp.float32))
                at = pl.ds(p * PART, PART)
                sums = jnp.sum(total, axis=1, keepdims=True)
                out_ref[at, :] = jnp.where(lane == r, sums, out_ref[at, :])
            return carry

        lax.fori_loop(0, targets, pair, 0)


def gather_products(codes, ops_ref, rows_ref):
    total = None
    for code in codes:
        at = pl.ds(pl.multiple_of(code >> ROW_BITS, 8), OPROWS)
        row = rows_ref[pl.ds(code & ((1 << ROW_BITS) - 1), 8, stride=0), :]
        term = ops_ref[at, :].reshape(OPROWS // 8, 8, 128) * row[None]
        total = term if total is None else total + term
    return total.reshape(OPROWS, 128)


def pack_codes(kinds, rows):
    return ((kinds * OPROWS) << ROW_BITS) | rows


def put_sums(total_ref, out_ref, lane):
    sums = jnp.sum(total_ref[...], axis=1, keepdims=True)
    out_ref[...] = jnp.where(lanes((OPROWS, 128)) == lane, sums, out_ref[...])


def halo_kernel(
    top_ref, top_list_ref, top_class_ref,
    list_ref, class_ref, moment_ref, partner_ref, far_ref, code_a_ref, code_b_ref, rows_ref, top_code_ref,
    d_ref, q_ref, acc_ref, halo_ref, list_vmem, class_vmem, sems,
):
    window = pl.ds(pl.multiple_of(window_start(top_ref), 128), TOP_WINDOW)
    copies = [
        pltpu.make_async_copy(top_list_ref.at[:, window], list_vmem, sems.at[0]),
        pltpu.make_async_copy(top_class_ref.at[:, window], class_vmem, sems.at[1]),
    ]
    for copy in copies:
        copy.start()
    even = lax.axis_index("zhi") == 0
    shift = lax.axis_index(AXES) * LEAVES - HALO
    packed = pack_codes(class_ref[...], list_ref[...] - shift)
    code_a_ref[...] = packed[:, : LEAVES // 2]
    code_b_ref[...] = packed[:, LEAVES // 2 :]
    fill = jnp.zeros((PAIRS - 2 * HPAIRS, 128), jnp.float32)

    def component(c):
        at = pl.ds(c, HPAIRS, stride=4)
        one, two = partner_ref[at, :], far_ref[at, :]
        return jnp.concatenate(
            [jnp.where(even, two, one), jnp.where(even, one, two), fill], axis=0
        )

    for c in range(3):
        d_ref[c] = centred(component(c))
    q_ref[...] = component(3).T
    expand_into(d_ref, q_ref, acc_ref, halo_ref)
    rows_ref[:HALO] = halo_ref[:HALO]
    rows_ref[HALO : HALO + LEAVES] = moment_ref[...]
    rows_ref[HALO + LEAVES :] = halo_ref[HALO : 2 * HALO]
    for copy in copies:
        copy.wait()
    codes = pack_codes(class_vmem[...], list_vmem[...])
    ahead = top_ref[0] - window_start(top_ref)
    top_code_ref[...] = pltpu.roll(codes, (TOP_WINDOW - ahead) % TOP_WINDOW, 1)[:, :128]


def leaf_kernel(part, code_ref, ops_ref, rows_ref, after_ref, out_ref, total_ref):
    del after_ref
    begin = part * (PAIRS // 2)
    lane = lanes((OPROWS, 128))

    def reduce(i):
        for p in range(2):
            wide = out_ref[p]
            for v in range(p, LEAF_STEP, 2):
                at = begin + i * (LEAF_STEP // 2) + v // 2
                wide = jnp.where(lane == at, jnp.sum(total_ref[v], axis=1, keepdims=True), wide)
            out_ref[p] = wide

    def step(i, carry):
        reduce(i - 1)
        for v in range(LEAF_STEP):
            leaf = i * LEAF_STEP + v
            total_ref[v] = gather_products(
                [code_ref[k, leaf] for k in range(LLIST)], ops_ref, rows_ref
            )
        return carry

    total_ref[...] = jnp.zeros_like(total_ref)
    out_ref[...] = jnp.zeros_like(out_ref)
    steps = LEAVES // 2 // LEAF_STEP
    lax.fori_loop(0, steps, step, 0)
    reduce(steps - 1)


def window_start(top_ref):
    return jnp.minimum(top_ref[0] // 128 * 128, TOPBOX - TOP_WINDOW)


def finish(
    cap, shift, ends, code_ref, table_ref, ops_ref, m2m_ref, tops_ref, local_refs, dist_ref,
    near_ref, mask_ref, out_ref, field_ref, pot_ref, total_ref, wide_ref, rows_ref,
):
    first, last = ends
    boxes = last - first + 1
    spread = jnp.zeros((OPROWS, LEAVES), jnp.float32)
    width = min(cap, 128)
    for block in range(cap // width):
        total_ref[...] = jnp.zeros_like(total_ref)
        wide_ref[...] = jnp.zeros_like(wide_ref)

        def step(b, carry):
            put_sums(total_ref, wide_ref, b - 1)
            column = shift + block * width + b
            total_ref[...] = gather_products(
                [code_ref[k, column] for k in range(TLIST)], ops_ref, table_ref
            )
            return carry

        count = jnp.clip(boxes - block * width, 0, width)
        lax.fori_loop(0, count, step, 0)
        put_sums(total_ref, wide_ref, count - 1)
        place = rows_of((128, LEAVES)) + block * width
        held = jnp.where(place == tops_ref[...] - first, 1.0, 0.0)
        spread += dot_f32(wide_ref[...], held)
    full = jnp.concatenate([spread, jnp.zeros((128 - OPROWS, LEAVES), jnp.float32)], axis=0)
    rows_ref[...] = full.T
    for a in range(8):
        at = pl.ds(a, LEAVES // 8, stride=8)
        rows_ref[at, :] = widen(dot_f32(rows_ref[at, :][:, :COEF], m2m_ref[:, a, :]))
    for p in range(2):
        field_ref[p] = (
            rows_ref[pl.ds(p, PAIRS, stride=2), :].T[:OPROWS]
            + local_refs[0][p] + local_refs[1][p]
        )
    for p in range(2):

        def step(s, carry):
            at = pl.ds(pl.multiple_of(p * PART + s * 16, 16), 16)
            listed = harmonics(dist_ref[0, at, :], dist_ref[1, at, :], dist_ref[2, at, :])
            total = None
            for c, term in enumerate(listed):
                weight = field_ref[p, pl.ds(c, 1), :]
                value = jnp.broadcast_to(weight, (16, 128)) if term is None else term * weight
                total = value if total is None else total + value
            pot_ref[at, :] = total
            return carry

        lax.fori_loop(0, PART // 16, step, 0)
    out_ref[...] = (near_ref[...] + pot_ref[...]).T * mask_ref[...]


def last_kernel(
    code_ref, mine_ref, other_ref, ops_ref, m2m_ref, tops_ref, local_a_ref, local_b_ref,
    dist_ref, near_ref, mask_ref, out_ref, over_ref,
    most_ref, table_ref, rest_ref, meta_ref, ends_ref, packed_ref, scalar_ref, sems, *scratch,
):
    half = mine_ref.shape[0]
    blocks = half // SEND
    heads = pl.ds(0, 2 * blocks, stride=SEND)
    some = pl.ds(0, blocks, stride=SEND)
    turned = jnp.concatenate([mine_ref[some, :], other_ref[some, :]], axis=0).T[120:]
    meta_ref[...] = turned.astype(jnp.int32)
    copy = pltpu.make_async_copy(meta_ref, ends_ref, sems.at[0])
    copy.start()
    table_ref[:half] = mine_ref[...]
    table_ref[half:] = other_ref[...]
    most = jnp.max(turned[6:7] - turned[7:8]).astype(jnp.int32) + 1
    most_ref[0] = most
    tell = pltpu.make_async_copy(most_ref, over_ref, sems.at[2])
    tell.start()
    core, my_y, my_x = lax.axis_index("core"), lax.axis_index("y"), lax.axis_index("x")
    my_z = lax.axis_index(("zlo", "zhi"))
    by_z = [(my_z ^ z) * 16 for z in range(4)]
    by_x = [(my_x ^ x) * 4 for x in range(4)]
    by_y = [my_y ^ y for y in range(4)]
    by_core = [blocks * (core ^ side) for side in range(2)]
    order = [
        by_z[zlo * 2 + zhi] + by_x[x] + by_y[y] + by_core[side]
        for zlo in range(2) for side in range(2) for y in range(4) for x in range(4)
        for zhi in range(2)
    ]
    copy.wait()

    @pl.when(most < SEND)
    def _():
        code = code_ref[...]
        box = code & ((1 << ROW_BITS) - 1)
        row = code
        last, last_begin = 0, 0
        rest_ref[pl.ds(order[0], 1), :] = jnp.zeros((1, 128), jnp.float32)
        for d, block in enumerate(order):
            begin = ends_ref[7, block]
            base = block * SEND
            if d:
                rest_ref[pl.ds(block, 1), :] = table_ref[pl.ds(last + begin - last_begin, 1), :]
                row += jnp.where(box >= begin, base - begin - last + last_begin, 0)
            else:
                row += base - begin
            last, last_begin = base, begin
        packed_ref[...] = row
        copy = pltpu.make_async_copy(packed_ref, scalar_ref, sems.at[1])
        copy.start()
        table_ref[heads, :] += rest_ref[...]
        copy.wait()
        finish(
            64, 0, (ends_ref[7, 0], ends_ref[6, 0]), scalar_ref, table_ref, ops_ref, m2m_ref, tops_ref,
            (local_a_ref, local_b_ref), dist_ref, near_ref, mask_ref, out_ref, *scratch,
        )

    tell.wait()


def spare_kernel(
    top_ref, code_ref, table_ref, ops_ref, m2m_ref, tops_ref, local_a_ref, local_b_ref,
    dist_ref, near_ref, mask_ref, out_ref, *scratch,
):
    finish(
        LEAVES, top_ref[0] - jnp.minimum(top_ref[0], TOPBOX - LEAVES),
        (top_ref[0], top_ref[LEAVES - 1]), code_ref, table_ref, ops_ref, m2m_ref, tops_ref,
        (local_a_ref, local_b_ref), dist_ref, near_ref, mask_ref, out_ref, *scratch,
    )


SMEM = pl.BlockSpec(memory_space=pltpu.SMEM)
VMEM = pl.BlockSpec(memory_space=pltpu.VMEM)
F32 = jnp.float32


def shape(*dims):
    return jax.ShapeDtypeStruct(dims, F32)


ANY = pl.BlockSpec(memory_space=pl.ANY)
HBM = pl.BlockSpec(memory_space=pltpu.HBM)
FINISH_SCRATCH = [
    pltpu.VMEM((2, OPROWS, 128), F32),
    pltpu.VMEM((128, 128), F32),
    pltpu.VMEM((OPROWS, 128), F32),
    pltpu.VMEM((OPROWS, 128), F32),
    pltpu.VMEM((LEAVES, 128), F32),
]


def cost(flops, bytes_accessed):
    return pl.CostEstimate(flops=flops, bytes_accessed=bytes_accessed, transcendentals=0)


def call_first(pts, counts, leaf_top, tops, m2m):
    return pl.pallas_call(
        first_kernel,
        out_shape=(
            shape(4 * PAIRS, 128), shape(4 * HPAIRS, 128), shape(4 * HPAIRS, 128),
            shape(3, PAIRS, 128), shape(LEAVES, 128), shape(SEND, 128), shape(LEAVES, 128),
            shape(PAIRS, 128),
        ),
        in_specs=[VMEM, SMEM, SMEM, VMEM, VMEM],
        out_specs=(VMEM,) * 8,
        scratch_shapes=[
            pltpu.VMEM((128, 128), F32), pltpu.VMEM((COEF, 8, 128), F32),
        ],
        compiler_params=pltpu.CompilerParams(vmem_limit_bytes=16 * MIB),
        cost_estimate=cost(10**9, 10**7),
        name="expand_own",
    )(pts, counts, leaf_top, tops, m2m)


def call_turn(ops, after):
    return pl.pallas_call(
        turn_kernel,
        out_shape=shape(CLASSES * OPROWS, 128),
        in_specs=[VMEM, ANY],
        out_specs=VMEM,
        compiler_params=pltpu.CompilerParams(vmem_limit_bytes=26 * MIB),
        cost_estimate=cost(10**7, 3 * 10**7),
        name="turn_operators",
    )(ops, after)


def call_join(pieces, *after):
    rows = pieces[0].shape[0]
    return pl.pallas_call(
        join_kernel,
        out_shape=shape(4 * rows, 128),
        in_specs=[VMEM] * 4 + [ANY] * len(after),
        out_specs=VMEM,
        compiler_params=pltpu.CompilerParams(vmem_limit_bytes=8 * MIB),
        cost_estimate=cost(10**5, 8 * rows * 512),
        name="join",
    )(*pieces, *after)


def call_near(near, own, before, behind, after):
    targets, width = PAIRS, WPAIRS
    return pl.pallas_call(
        near_kernel,
        out_shape=shape(targets, 128),
        in_specs=[VMEM, VMEM, VMEM, VMEM, ANY],
        out_specs=VMEM,
        scratch_shapes=[
            pltpu.VMEM((4 * WPAIRS, 128), F32),
            pltpu.VMEM((width * FEATS, 128), F32),
            pltpu.VMEM((targets * FEATS, 128), F32),
            pltpu.VMEM((2 * width, FEAT, 128), jnp.bfloat16),
            pltpu.VMEM((LEAVES, PART, FEAT), jnp.bfloat16),
            pltpu.VMEM((2 * width, 128), F32),
            pltpu.SMEM((NEAR, LEAVES), jnp.int32),
            pltpu.SemaphoreType.DMA,
        ],
        compiler_params=pltpu.CompilerParams(vmem_limit_bytes=24 * MIB),
        cost_estimate=cost(10 * targets * 2 * 64 * NEAR * 64, 3 * 10**7),
        name="near",
    )(near, own, before, behind, after)


def call_halo(leaf_top, top_lists, top_classes, lists, classes, moments, partner, far):
    return pl.pallas_call(
        halo_kernel,
        out_shape=(
            jax.ShapeDtypeStruct((LLIST, LEAVES // 2), jnp.int32),
            jax.ShapeDtypeStruct((LLIST, LEAVES // 2), jnp.int32), shape(2 * WPAIRS, 128),
            jax.ShapeDtypeStruct((TLIST, 128), jnp.int32),
        ),
        in_specs=[SMEM, HBM, HBM] + [VMEM] * 5,
        out_specs=(VMEM,) * 4,
        scratch_shapes=[
            pltpu.VMEM((3, 128, 128), F32),
            pltpu.VMEM((128, 128), F32),
            pltpu.VMEM((COEF, 8, 128), F32),
            pltpu.VMEM((LEAVES, 128), F32),
            pltpu.VMEM((TLIST, TOP_WINDOW), jnp.int32),
            pltpu.VMEM((TLIST, TOP_WINDOW), jnp.int32),
            pltpu.SemaphoreType.DMA((2,)),
        ],
        compiler_params=pltpu.CompilerParams(vmem_limit_bytes=16 * MIB),
        cost_estimate=cost(10**8, 10**6),
        name="expand_halo",
    )(leaf_top, top_lists, top_classes, lists, classes, moments, partner, far)


def call_leaf(part, code, ops, rows, after):
    return pl.pallas_call(
        functools.partial(leaf_kernel, part),
        out_shape=shape(2, OPROWS, 128),
        in_specs=[SMEM, VMEM, VMEM, ANY],
        out_specs=VMEM,
        scratch_shapes=[pltpu.VMEM((LEAF_STEP, OPROWS, 128), F32)],
        compiler_params=pltpu.CompilerParams(vmem_limit_bytes=17 * MIB),
        cost_estimate=cost(LEAVES * LLIST * COEF * COEF * 8, 2 * 10**7),
        name="leaf_translate",
    )(code, ops, rows, after)


def call_last(code, mine, other, *rest):
    return pl.pallas_call(
        last_kernel,
        out_shape=(shape(PAIRS, 128), jax.ShapeDtypeStruct((1,), jnp.int32)),
        in_specs=[VMEM] * 11,
        out_specs=(VMEM, ANY),
        scratch_shapes=[
            pltpu.SMEM((1,), jnp.int32),
            pltpu.VMEM((2 * mine.shape[0], 128), F32),
            pltpu.VMEM((2 * mine.shape[0] // SEND, 128), F32),
            pltpu.VMEM((8, 128), jnp.int32),
            pltpu.SMEM((8, 128), jnp.int32),
            pltpu.VMEM((TLIST, 128), jnp.int32),
            pltpu.SMEM((TLIST, 128), jnp.int32),
            pltpu.SemaphoreType.DMA((3,)),
        ] + FINISH_SCRATCH,
        compiler_params=pltpu.CompilerParams(vmem_limit_bytes=24 * MIB),
        name="finish",
    )(code, mine, other, *rest)


def call_spare(leaf_top, code, table, *rest):
    return pl.pallas_call(
        spare_kernel,
        out_shape=shape(PAIRS, 128),
        in_specs=[SMEM, SMEM] + [VMEM] * 9,
        out_specs=VMEM,
        scratch_shapes=FINISH_SCRATCH,
        compiler_params=pltpu.CompilerParams(vmem_limit_bytes=24 * MIB),
        name="finish_spare",
    )(leaf_top, code, table, *rest)


def sent_over(block, axis):
    return [block] + [
        lax.ppermute(block, axis, [(i, i ^ s) for i in range(4)]) for s in range(1, 4)
    ]


def body(
    particles, counts, leaf_top, near_list, leaf_list, leaf_class, top_list, top_class,
    m2l_ops, m2m_ops,
):
    pts = particles.reshape(4, PAIRS, 128).transpose(1, 0, 2).reshape(4 * PAIRS, 128)
    tops = leaf_top.reshape(1, LEAVES)
    m2m = m2m_ops.transpose(1, 0, 2)
    own, near_edge, far_edge, dist, moments, send, lifted, mask = call_first(
        pts, counts.reshape(1, LEAVES), leaf_top, tops, m2m
    )
    devices = lax.axis_size(AXES)
    partner = [(i, i ^ 1) for i in range(devices)]
    far = [(i, (i + 2 * (i & 1) - 1) % devices) for i in range(devices)]
    over_y = sent_over(send, "y")
    from_partner = lax.ppermute(near_edge, AXES, partner)
    from_far = lax.ppermute(far_edge, AXES, far)
    ops = call_turn(m2l_ops.transpose(1, 2, 0), send)
    by_y = call_join(over_y, ops, from_partner, from_far)
    over_x = sent_over(by_y, "x")
    code_a, code_b, rows, top_code = call_halo(
        leaf_top, top_list.T, top_class.T, leaf_list.T, leaf_class.T, moments,
        from_partner, from_far,
    )
    local_a = call_leaf(0, code_a, ops, rows, by_y)
    by_x = call_join(over_x, local_a)
    over_z = sent_over(by_x, ("zlo", "zhi"))
    near = call_near(near_list.T, own, from_partner, from_far, by_x)
    mine = call_join(over_z, near)
    other = lax.ppermute(mine, "core", [(0, 1), (1, 0)])
    local_b = call_leaf(1, code_b, ops, rows, mine)
    rest = (ops, m2m, tops, local_a, local_b, dist, near, mask)
    result, over = call_last(top_code, mine, other, *rest)

    def spare():
        held = jnp.arange(LEAVES, dtype=jnp.int32)[:, None] == (leaf_top - leaf_top[0])[None]
        partial = jnp.matmul(held.astype(F32), lifted, precision=HIGH)
        table = lax.dynamic_update_slice(
            jnp.zeros((TOPBOX + LEAVES, 128), F32), partial, (leaf_top[0], 0)
        )
        for k in range(7):
            swap = [(i, i ^ (1 << k)) for i in range(devices)]
            table = table + lax.ppermute(table, AXES, swap)
        start = jnp.minimum(leaf_top[0], TOPBOX - LEAVES)
        lists, classes = (
            lax.dynamic_slice_in_dim(x, start, LEAVES, axis=0).T for x in (top_list, top_class)
        )
        again = call_turn(m2l_ops.transpose(1, 2, 0), table)
        return call_spare(leaf_top, pack_codes(classes, lists), table, again, *rest[1:])

    result = lax.cond(over[0] >= SEND, spare, lambda: result)
    return result.reshape(-1)


def solution(mesh):
    fine = Mesh(mesh.devices.reshape(2, 2, 4, 4, 2), AXES)
    return jax.shard_map(
        body,
        mesh=fine,
        in_specs=(
            P(None, AXES), P(AXES), P(AXES), P(AXES, None), P(AXES, None), P(AXES, None),
            P(), P(), P(), P(),
        ),
        out_specs=P(AXES),
        check_vma=False,
    )
```

```python
import functools

import jax
import jax.numpy as jnp
from jax import lax
from jax.experimental import pallas as pl
from jax.experimental.pallas import tpu as pltpu
from jax.sharding import Mesh, PartitionSpec as P

ORDER = 8
COEF = 81
PART = 64
LEAVES = 256
PAIRS = 128
HALO = 32
HPAIRS = 16
WPAIRS = PAIRS + 2 * HPAIRS
NEAR = 27
LLIST = 16
TLIST = 64
TOPBOX = 4096
ROW_BITS = 13
CLASSES = 316
OPROWS = 88
SOFTENING = 0.01
SEND = 56
REACH_SQ = 16.0
FEAT = 32
FEATS = 24
LEAF_STEP = 8
CHAIN = 8
TURN_STEP = 27
TOP_WINDOW = 256
BUILD_STEP = 32
NEAR_STEP = 64

HIGH = lax.Precision.HIGHEST
MIB = 1 << 20
AXES = ("zlo", "core", "y", "x", "zhi")

NN = (((1,), (0,)), ((), ()))
NT = (((1,), (1,)), ((), ()))


def dot_f32(left, right, dims=NN):
    return lax.dot_general(left, right, dims, precision=HIGH, preferred_element_type=jnp.float32)


def lanes(shape):
    return lax.broadcasted_iota(jnp.int32, shape, len(shape) - 1)


def rows_of(shape):
    return lax.broadcasted_iota(jnp.int32, shape, len(shape) - 2)


def harmonics(coord_x, coord_y, coord_z):
    radius_sq = coord_x * coord_x + coord_y * coord_y + coord_z * coord_z
    terms = {(0, 0): (None, None)}
    for m in range(1, ORDER + 1):
        if m == 1:
            terms[1, 1] = (coord_x * 0.5, coord_y * 0.5)
            continue
        re, im = terms[m - 1, m - 1]
        scale = 1.0 / (2.0 * m)
        terms[m, m] = (
            (coord_x * re - coord_y * im) * scale,
            (coord_x * im + coord_y * re) * scale,
        )
    for m in range(ORDER):
        re, im = terms[m, m]
        terms[m + 1, m] = (coord_z, None) if m == 0 else (coord_z * re, coord_z * im)
    for m in range(ORDER - 1):
        for n in range(m + 2, ORDER + 1):
            one = (2.0 * n - 1.0) / ((n - m) * (n + m))
            two = 1.0 / ((n - m) * (n + m))
            z_one = coord_z * one
            r_two = radius_sq * two
            upper, lower = terms[n - 1, m], terms[n - 2, m]
            re = z_one * upper[0] - (r_two if lower[0] is None else r_two * lower[0])
            im = None if m == 0 else z_one * upper[1] - r_two * lower[1]
            terms[n, m] = (re, im)
    listed = []
    for n in range(ORDER + 1):
        listed.append(terms[n, 0][0])
        for m in range(1, n + 1):
            listed.extend(terms[n, m])
    return listed


def centred(block):
    turned = block.T
    halves = []
    for p in range(2):
        half = turned[p * PART : (p + 1) * PART]
        halves.append(half - jnp.sum(half, axis=0, keepdims=True) * (1.0 / PART))
    return jnp.concatenate(halves, axis=0)


def expand_into(d_ref, q_ref, acc_ref, out_ref):
    for p in range(2):
        acc_ref[...] = jnp.zeros_like(acc_ref)

        def step(s, carry):
            at = pl.ds(pl.multiple_of(p * PART + s * 16, 16), 16)
            charge = q_ref[at, :]
            listed = harmonics(d_ref[0, at, :], d_ref[1, at, :], d_ref[2, at, :])
            for c, term in enumerate(listed):
                value = charge if term is None else charge * term
                acc_ref[c] += value[:8] + value[8:]
            return carry

        lax.fori_loop(0, PART // 16, step, 0)
        sums = jnp.sum(acc_ref[...], axis=1)
        full = jnp.concatenate([sums, jnp.zeros((128 - COEF, 128), jnp.float32)], axis=0)
        out_ref[pl.ds(p, PAIRS, stride=2), :] = full.T


def widen(block):
    return jnp.concatenate(
        [block, jnp.zeros((block.shape[0], 128 - block.shape[1]), jnp.float32)], axis=1
    )


def first_kernel(
    pts_ref, count_ref, top_ref, tops_ref, m2m_ref,
    own_ref, near_edge_ref, far_edge_ref, dist_ref, moment_ref, send_ref, lift_ref, mask_ref,
    q_ref, acc_ref,
):
    lane = lanes((1, 128))

    def hold(i, carry):
        for u in range(8):
            r = i * 8 + u
            held = jnp.where(lane < PART, count_ref[0, 2 * r], count_ref[0, 2 * r + 1])
            mask_ref[pl.ds(r, 1), :] = jnp.where((lane & (PART - 1)) < held, 1.0, 0.0)
        return carry

    lax.fori_loop(0, PAIRS // 8, hold, 0)
    charge = pts_ref[pl.ds(3, PAIRS, stride=4), :] * mask_ref[...]
    own_ref[...] = pts_ref[...]
    own_ref[pl.ds(3, PAIRS, stride=4), :] = charge
    even = lax.axis_index("zhi") == 0
    low, high = own_ref[: 4 * HPAIRS], own_ref[4 * (PAIRS - HPAIRS) :]
    near_edge_ref[...] = jnp.where(even, high, low)
    far_edge_ref[...] = jnp.where(even, low, high)
    for c in range(3):
        dist_ref[c] = centred(pts_ref[pl.ds(c, PAIRS, stride=4), :])
    q_ref[...] = charge.T
    expand_into(dist_ref, q_ref, acc_ref, moment_ref)
    first, last = top_ref[0], top_ref[LEAVES - 1]
    for a in range(8):
        at = pl.ds(a, LEAVES // 8, stride=8)
        lift_ref[at, :] = widen(dot_f32(moment_ref[at, :][:, :COEF], m2m_ref[:, a, :], NT))
    held = jnp.where(rows_of((SEND, LEAVES)) == tops_ref[...] - first, 1.0, 0.0)
    wide = dot_f32(held, lift_ref[...])
    lane = lanes((SEND, 128))
    wide = jnp.where(lane == 127, first.astype(jnp.float32), wide)
    wide = jnp.where(lane == 126, last.astype(jnp.float32), wide)
    send_ref[...] = wide


def turn_kernel(in_ref, after_ref, out_ref):
    del after_ref

    def step(i, carry):
        for u in range(TURN_STEP):
            one = in_ref[i * TURN_STEP + u]
            for begin in range(0, CLASSES, 128):
                count = min(128, CLASSES - begin)
                at = pl.ds(begin * OPROWS + i * TURN_STEP + u, count, stride=OPROWS)
                out_ref[at, :] = widen(one[:, begin : begin + count].T)
        return carry

    lax.fori_loop(0, COEF // TURN_STEP, step, 0)


def join_kernel(*refs):
    out_ref = refs[-1]
    rows = refs[0].shape[0]
    for i, ref in enumerate(refs[:4]):
        out_ref[i * rows : (i + 1) * rows] = ref[...]


def split3(value):
    high = value.astype(jnp.bfloat16).astype(jnp.float32)
    rest = value - high
    middle = rest.astype(jnp.bfloat16).astype(jnp.float32)
    low = (rest - middle).astype(jnp.bfloat16).astype(jnp.float32)
    return high, middle, low


def near_kernel(
    list_ref, own_ref, partner_ref, far_ref, after_ref, out_ref,
    win_ref, src_ref, tgt_ref, source_ref, target_ref, charge_ref, near_ref, sem,
):
    del after_ref
    targets, width = PAIRS, WPAIRS
    edge = 4 * HPAIRS
    lists = pltpu.make_async_copy(list_ref, near_ref, sem)
    lists.start()
    even = lax.axis_index("zhi") == 0
    win_ref[:edge] = jnp.where(even, far_ref[...], partner_ref[...])
    win_ref[edge : edge + 4 * PAIRS] = own_ref[...]
    win_ref[edge + 4 * PAIRS :] = jnp.where(even, partner_ref[...], far_ref[...])
    shift = lax.axis_index(AXES) * LEAVES - HALO

    def component(c):
        return win_ref[pl.ds(c, width, stride=4), :]

    points = [component(c) for c in range(3)]
    moved = []
    for c in range(3):
        least = jnp.min(points[c], keepdims=True)
        most = jnp.max(points[c], keepdims=True)
        moved.append(points[c] - 0.5 * (least + most))
    norm = moved[0] * moved[0] + moved[1] * moved[1] + moved[2] * moved[2]
    close = jnp.max(norm) <= REACH_SQ
    out_ref[...] = jnp.zeros_like(out_ref)

    @pl.when(close)
    def _():
        own = slice(HPAIRS, HPAIRS + targets)

        def keep(ref, f, feature):
            rows = feature.shape[0]
            ref[f * rows : (f + 1) * rows] = feature

        for c in range(3):
            h, m, l = split3(moved[c])
            for i, feature in enumerate((h, h, m, m, h, l)):
                keep(src_ref, 6 * c + i, feature)
            th, tm, tl = [-2.0 * piece[own] for piece in (h, m, l)]
            for i, feature in enumerate((th, tm, th, tm, tl, th)):
                keep(tgt_ref, 6 * c + i, feature)
        ones = jnp.ones((width, 128), jnp.float32)
        for i, feature in enumerate(split3(norm + SOFTENING)):
            keep(src_ref, 18 + i, feature)
            keep(tgt_ref, 18 + i, ones[own])
        for i, feature in enumerate(split3(norm[own])):
            keep(src_ref, 21 + i, ones)
            keep(tgt_ref, 21 + i, feature)
        charge = component(3)
        charge_ref[pl.ds(0, width, stride=2), :] = charge
        charge_ref[pl.ds(1, width, stride=2), :] = pltpu.roll(charge, PART, 1)
        rest = jnp.zeros((FEAT - FEATS, 128), jnp.float32)

        def build_source(i, carry):
            for u in range(BUILD_STEP):
                r = i * BUILD_STEP + u
                some = src_ref[pl.ds(r, FEATS, stride=width), :]
                some = jnp.concatenate([some, rest], axis=0)
                source_ref[2 * r] = some.astype(jnp.bfloat16)
                source_ref[2 * r + 1] = pltpu.roll(some, PART, 1).astype(jnp.bfloat16)
            return carry

        def build_target(i, carry):
            for u in range(BUILD_STEP):
                r = i * BUILD_STEP + u
                some = tgt_ref[pl.ds(r, FEATS, stride=targets), :]
                some = jnp.concatenate([some, rest], axis=0).T.astype(jnp.bfloat16)
                for p in range(2):
                    target_ref[2 * r + p] = some[p * PART : (p + 1) * PART]
            return carry

        lax.fori_loop(0, width // BUILD_STEP, build_source, 0)
        lax.fori_loop(0, targets // BUILD_STEP, build_target, 0)
        lists.wait()

        low_block = lanes((FEAT, 128)) < PART
        low_row = lanes((1, 128)) < PART
        lane = lanes((PART, 128))

        def leaf_sums(l):
            total = None
            for k in range(0, NEAR + 1, 4):
                blocks, charges = [], []
                for j in range(k, k + 4, 2):
                    one = near_ref[j, l] - shift
                    two = (near_ref[min(j + 1, NEAR - 1), l] - shift) ^ 1
                    blocks.append(jnp.where(low_block, source_ref[one], source_ref[two]))
                    other = charge_ref[pl.ds(two, 1), :] if j + 1 < NEAR else 0.0
                    charges.append(jnp.where(low_row, charge_ref[pl.ds(one, 1), :], other))
                dist = lax.dot_general(
                    target_ref[l], jnp.concatenate(blocks, axis=1), NN,
                    preferred_element_type=jnp.float32,
                )
                for j in range(2):
                    term = charges[j] * lax.rsqrt(dist[:, j * 128 : (j + 1) * 128])
                    total = term if total is None else total + term
            return total

        def group(i, carry):
            totals = [leaf_sums(i * NEAR_STEP + u) for u in range(NEAR_STEP)]
            for p in range(2):
                at = pl.ds(p * PART, PART)
                wide = out_ref[at, :]
                for u in range(p, NEAR_STEP, 2):
                    sums = jnp.sum(totals[u], axis=1, keepdims=True)
                    wide = jnp.where(lane == i * (NEAR_STEP // 2) + u // 2, sums, wide)
                out_ref[at, :] = wide
            return carry

        lax.fori_loop(0, LEAVES // NEAR_STEP, group, 0)

    @pl.when(jnp.logical_not(close))
    def _():
        lane = lanes((PART, 128))
        lists.wait()

        def pair(r, carry):
            columns = [
                jnp.broadcast_to(
                    win_ref[pl.ds(4 * (HPAIRS + r) + c, 1), :], (128, 128)
                ).T
                for c in range(3)
            ]
            for p in range(2):
                mine = [column[p * PART : (p + 1) * PART] for column in columns]

                def entry(k, total):
                    leaf = near_ref[k, 2 * r + p] - shift
                    at = 4 * (leaf // 2)
                    gap = SOFTENING
                    for c in range(3):
                        diff = mine[c] - win_ref[pl.ds(at + c, 1), :]
                        gap = gap + diff * diff
                    half = jnp.where((lane // PART) == leaf % 2, 1.0, 0.0)
                    return total + half * (win_ref[pl.ds(at + 3, 1), :] * lax.rsqrt(gap))

                total = lax.fori_loop(0, NEAR, entry, jnp.zeros((PART, 128), jnp.float32))
                at = pl.ds(p * PART, PART)
                sums = jnp.sum(total, axis=1, keepdims=True)
                out_ref[at, :] = jnp.where(lane == r, sums, out_ref[at, :])
            return carry

        lax.fori_loop(0, targets, pair, 0)


def gather_products(codes, ops_ref, rows_ref):
    total = None
    for begin in range(0, len(codes), CHAIN):
        part = None
        for code in codes[begin : begin + CHAIN]:
            at = pl.ds(pl.multiple_of(code >> ROW_BITS, 8), OPROWS)
            row = rows_ref[pl.ds(code & ((1 << ROW_BITS) - 1), 8, stride=0), :]
            term = ops_ref[at, :].reshape(OPROWS // 8, 8, 128) * row[None]
            part = term if part is None else part + term
        total = part if total is None else total + part
    return total.reshape(OPROWS, 128)


def pack_codes(kinds, rows):
    return ((kinds * OPROWS) << ROW_BITS) | rows


def put_sums(total_ref, out_ref, lane):
    sums = jnp.sum(total_ref[...], axis=1, keepdims=True)
    out_ref[...] = jnp.where(lanes((OPROWS, 128)) == lane, sums, out_ref[...])


def halo_kernel(
    top_ref, top_list_ref, top_class_ref,
    list_ref, class_ref, moment_ref, partner_ref, far_ref, code_a_ref, code_b_ref, rows_ref, top_code_ref,
    d_ref, q_ref, acc_ref, halo_ref, list_vmem, class_vmem, sems,
):
    window = pl.ds(pl.multiple_of(window_start(top_ref), 128), TOP_WINDOW)
    copies = [
        pltpu.make_async_copy(top_list_ref.at[:, window], list_vmem, sems.at[0]),
        pltpu.make_async_copy(top_class_ref.at[:, window], class_vmem, sems.at[1]),
    ]
    for copy in copies:
        copy.start()
    even = lax.axis_index("zhi") == 0
    shift = lax.axis_index(AXES) * LEAVES - HALO
    packed = pack_codes(class_ref[...], list_ref[...] - shift)
    code_a_ref[...] = packed[:, : LEAVES // 2]
    code_b_ref[...] = packed[:, LEAVES // 2 :]
    fill = jnp.zeros((PAIRS - 2 * HPAIRS, 128), jnp.float32)

    def component(c):
        at = pl.ds(c, HPAIRS, stride=4)
        one, two = partner_ref[at, :], far_ref[at, :]
        return jnp.concatenate(
            [jnp.where(even, two, one), jnp.where(even, one, two), fill], axis=0
        )

    for c in range(3):
        d_ref[c] = centred(component(c))
    q_ref[...] = component(3).T
    expand_into(d_ref, q_ref, acc_ref, halo_ref)
    rows_ref[:HALO] = halo_ref[:HALO]
    rows_ref[HALO : HALO + LEAVES] = moment_ref[...]
    rows_ref[HALO + LEAVES :] = halo_ref[HALO : 2 * HALO]
    for copy in copies:
        copy.wait()
    codes = pack_codes(class_vmem[...], list_vmem[...])
    ahead = top_ref[0] - window_start(top_ref)
    top_code_ref[...] = pltpu.roll(codes, (TOP_WINDOW - ahead) % TOP_WINDOW, 1)[:, :128]


def leaf_kernel(part, code_ref, ops_ref, rows_ref, after_ref, out_ref, total_ref):
    del after_ref
    begin = part * (PAIRS // 2)
    lane = lanes((OPROWS, 128))

    def reduce(i):
        for p in range(2):
            wide = out_ref[p]
            for v in range(p, LEAF_STEP, 2):
                at = begin + i * (LEAF_STEP // 2) + v // 2
                wide = jnp.where(lane == at, jnp.sum(total_ref[v], axis=1, keepdims=True), wide)
            out_ref[p] = wide

    def step(i, carry):
        reduce(i - 1)
        for v in range(LEAF_STEP):
            leaf = i * LEAF_STEP + v
            total_ref[v] = gather_products(
                [code_ref[k, leaf] for k in range(LLIST)], ops_ref, rows_ref
            )
        return carry

    total_ref[...] = jnp.zeros_like(total_ref)
    out_ref[...] = jnp.zeros_like(out_ref)
    steps = LEAVES // 2 // LEAF_STEP
    lax.fori_loop(0, steps, step, 0)
    reduce(steps - 1)


def window_start(top_ref):
    return jnp.minimum(top_ref[0] // 128 * 128, TOPBOX - TOP_WINDOW)


def finish(
    cap, shift, ends, code_ref, table_ref, ops_ref, m2m_ref, tops_ref, local_refs, dist_ref,
    near_ref, mask_ref, out_ref, field_ref, pot_ref, total_ref, wide_ref, rows_ref,
):
    first, last = ends
    boxes = last - first + 1
    spread = jnp.zeros((OPROWS, LEAVES), jnp.float32)
    width = min(cap, 128)
    for block in range(cap // width):
        total_ref[...] = jnp.zeros_like(total_ref)
        wide_ref[...] = jnp.zeros_like(wide_ref)

        def step(b, carry):
            put_sums(total_ref, wide_ref, b - 1)
            column = shift + block * width + b
            total_ref[...] = gather_products(
                [code_ref[k, column] for k in range(TLIST)], ops_ref, table_ref
            )
            return carry

        count = jnp.clip(boxes - block * width, 0, width)
        lax.fori_loop(0, count, step, 0)
        put_sums(total_ref, wide_ref, count - 1)
        place = rows_of((128, LEAVES)) + block * width
        held = jnp.where(place == tops_ref[...] - first, 1.0, 0.0)
        spread += dot_f32(wide_ref[...], held)
    full = jnp.concatenate([spread, jnp.zeros((128 - OPROWS, LEAVES), jnp.float32)], axis=0)
    rows_ref[...] = full.T
    for a in range(8):
        at = pl.ds(a, LEAVES // 8, stride=8)
        rows_ref[at, :] = widen(dot_f32(rows_ref[at, :][:, :COEF], m2m_ref[:, a, :]))
    for p in range(2):
        field_ref[p] = (
            rows_ref[pl.ds(p, PAIRS, stride=2), :].T[:OPROWS]
            + local_refs[0][p] + local_refs[1][p]
        )
    for p in range(2):

        def step(s, carry):
            at = pl.ds(pl.multiple_of(p * PART + s * 16, 16), 16)
            listed = harmonics(dist_ref[0, at, :], dist_ref[1, at, :], dist_ref[2, at, :])
            total = None
            for c, term in enumerate(listed):
                weight = field_ref[p, pl.ds(c, 1), :]
                value = jnp.broadcast_to(weight, (16, 128)) if term is None else term * weight
                total = value if total is None else total + value
            pot_ref[at, :] = total
            return carry

        lax.fori_loop(0, PART // 16, step, 0)
    out_ref[...] = (near_ref[...] + pot_ref[...]).T * mask_ref[...]


def last_kernel(
    code_ref, mine_ref, other_ref, ops_ref, m2m_ref, tops_ref, local_a_ref, local_b_ref,
    dist_ref, near_ref, mask_ref, out_ref, over_ref,
    most_ref, table_ref, rest_ref, meta_ref, ends_ref, packed_ref, scalar_ref, sems, *scratch,
):
    half = mine_ref.shape[0]
    blocks = half // SEND
    heads = pl.ds(0, 2 * blocks, stride=SEND)
    some = pl.ds(0, blocks, stride=SEND)
    turned = jnp.concatenate([mine_ref[some, :], other_ref[some, :]], axis=0).T[120:]
    meta_ref[...] = turned.astype(jnp.int32)
    copy = pltpu.make_async_copy(meta_ref, ends_ref, sems.at[0])
    copy.start()
    table_ref[:half] = mine_ref[...]
    table_ref[half:] = other_ref[...]
    most = jnp.max(turned[6:7] - turned[7:8]).astype(jnp.int32) + 1
    most_ref[0] = most
    tell = pltpu.make_async_copy(most_ref, over_ref, sems.at[2])
    tell.start()
    core, my_y, my_x = lax.axis_index("core"), lax.axis_index("y"), lax.axis_index("x")
    my_z = lax.axis_index(("zlo", "zhi"))
    by_z = [(my_z ^ z) * 16 for z in range(4)]
    by_x = [(my_x ^ x) * 4 for x in range(4)]
    by_y = [my_y ^ y for y in range(4)]
    by_core = [blocks * (core ^ side) for side in range(2)]
    order = [
        by_z[zlo * 2 + zhi] + by_x[x] + by_y[y] + by_core[side]
        for zlo in range(2) for side in range(2) for y in range(4) for x in range(4)
        for zhi in range(2)
    ]
    copy.wait()

    @pl.when(most < SEND)
    def _():
        code = code_ref[...]
        box = code & ((1 << ROW_BITS) - 1)
        row = code
        last, last_begin = 0, 0
        rest_ref[pl.ds(order[0], 1), :] = jnp.zeros((1, 128), jnp.float32)
        for d, block in enumerate(order):
            begin = ends_ref[7, block]
            base = block * SEND
            if d:
                rest_ref[pl.ds(block, 1), :] = table_ref[pl.ds(last + begin - last_begin, 1), :]
                row += jnp.where(box >= begin, base - begin - last + last_begin, 0)
            else:
                row += base - begin
            last, last_begin = base, begin
        packed_ref[...] = row
        copy = pltpu.make_async_copy(packed_ref, scalar_ref, sems.at[1])
        copy.start()
        table_ref[heads, :] += rest_ref[...]
        copy.wait()
        finish(
            64, 0, (ends_ref[7, 0], ends_ref[6, 0]), scalar_ref, table_ref, ops_ref, m2m_ref, tops_ref,
            (local_a_ref, local_b_ref), dist_ref, near_ref, mask_ref, out_ref, *scratch,
        )

    tell.wait()


def spare_kernel(
    top_ref, code_ref, table_ref, ops_ref, m2m_ref, tops_ref, local_a_ref, local_b_ref,
    dist_ref, near_ref, mask_ref, out_ref, *scratch,
):
    finish(
        LEAVES, top_ref[0] - jnp.minimum(top_ref[0], TOPBOX - LEAVES),
        (top_ref[0], top_ref[LEAVES - 1]), code_ref, table_ref, ops_ref, m2m_ref, tops_ref,
        (local_a_ref, local_b_ref), dist_ref, near_ref, mask_ref, out_ref, *scratch,
    )


SMEM = pl.BlockSpec(memory_space=pltpu.SMEM)
VMEM = pl.BlockSpec(memory_space=pltpu.VMEM)
F32 = jnp.float32


def shape(*dims):
    return jax.ShapeDtypeStruct(dims, F32)


ANY = pl.BlockSpec(memory_space=pl.ANY)
HBM = pl.BlockSpec(memory_space=pltpu.HBM)
FINISH_SCRATCH = [
    pltpu.VMEM((2, OPROWS, 128), F32),
    pltpu.VMEM((128, 128), F32),
    pltpu.VMEM((OPROWS, 128), F32),
    pltpu.VMEM((OPROWS, 128), F32),
    pltpu.VMEM((LEAVES, 128), F32),
]


def cost(flops, bytes_accessed):
    return pl.CostEstimate(flops=flops, bytes_accessed=bytes_accessed, transcendentals=0)


def call_first(pts, counts, leaf_top, tops, m2m):
    return pl.pallas_call(
        first_kernel,
        out_shape=(
            shape(4 * PAIRS, 128), shape(4 * HPAIRS, 128), shape(4 * HPAIRS, 128),
            shape(3, PAIRS, 128), shape(LEAVES, 128), shape(SEND, 128), shape(LEAVES, 128),
            shape(PAIRS, 128),
        ),
        in_specs=[VMEM, SMEM, SMEM, VMEM, VMEM],
        out_specs=(VMEM,) * 8,
        scratch_shapes=[
            pltpu.VMEM((128, 128), F32), pltpu.VMEM((COEF, 8, 128), F32),
        ],
        compiler_params=pltpu.CompilerParams(vmem_limit_bytes=16 * MIB),
        cost_estimate=cost(10**9, 10**7),
        name="expand_own",
    )(pts, counts, leaf_top, tops, m2m)


def call_turn(ops, after):
    return pl.pallas_call(
        turn_kernel,
        out_shape=shape(CLASSES * OPROWS, 128),
        in_specs=[VMEM, ANY],
        out_specs=VMEM,
        compiler_params=pltpu.CompilerParams(vmem_limit_bytes=26 * MIB),
        cost_estimate=cost(10**7, 3 * 10**7),
        name="turn_operators",
    )(ops, after)


def call_join(pieces, *after):
    rows = pieces[0].shape[0]
    return pl.pallas_call(
        join_kernel,
        out_shape=shape(4 * rows, 128),
        in_specs=[VMEM] * 4 + [ANY] * len(after),
        out_specs=VMEM,
        compiler_params=pltpu.CompilerParams(vmem_limit_bytes=8 * MIB),
        cost_estimate=cost(10**5, 8 * rows * 512),
        name="join",
    )(*pieces, *after)


def call_near(near, own, before, behind, after):
    targets, width = PAIRS, WPAIRS
    return pl.pallas_call(
        near_kernel,
        out_shape=shape(targets, 128),
        in_specs=[VMEM, VMEM, VMEM, VMEM, ANY],
        out_specs=VMEM,
        scratch_shapes=[
            pltpu.VMEM((4 * WPAIRS, 128), F32),
            pltpu.VMEM((width * FEATS, 128), F32),
            pltpu.VMEM((targets * FEATS, 128), F32),
            pltpu.VMEM((2 * width, FEAT, 128), jnp.bfloat16),
            pltpu.VMEM((LEAVES, PART, FEAT), jnp.bfloat16),
            pltpu.VMEM((2 * width, 128), F32),
            pltpu.SMEM((NEAR, LEAVES), jnp.int32),
            pltpu.SemaphoreType.DMA,
        ],
        compiler_params=pltpu.CompilerParams(vmem_limit_bytes=24 * MIB),
        cost_estimate=cost(10 * targets * 2 * 64 * NEAR * 64, 3 * 10**7),
        name="near",
    )(near, own, before, behind, after)


def call_halo(leaf_top, top_lists, top_classes, lists, classes, moments, partner, far):
    return pl.pallas_call(
        halo_kernel,
        out_shape=(
            jax.ShapeDtypeStruct((LLIST, LEAVES // 2), jnp.int32),
            jax.ShapeDtypeStruct((LLIST, LEAVES // 2), jnp.int32), shape(2 * WPAIRS, 128),
            jax.ShapeDtypeStruct((TLIST, 128), jnp.int32),
        ),
        in_specs=[SMEM, HBM, HBM] + [VMEM] * 5,
        out_specs=(VMEM,) * 4,
        scratch_shapes=[
            pltpu.VMEM((3, 128, 128), F32),
            pltpu.VMEM((128, 128), F32),
            pltpu.VMEM((COEF, 8, 128), F32),
            pltpu.VMEM((LEAVES, 128), F32),
            pltpu.VMEM((TLIST, TOP_WINDOW), jnp.int32),
            pltpu.VMEM((TLIST, TOP_WINDOW), jnp.int32),
            pltpu.SemaphoreType.DMA((2,)),
        ],
        compiler_params=pltpu.CompilerParams(vmem_limit_bytes=16 * MIB),
        cost_estimate=cost(10**8, 10**6),
        name="expand_halo",
    )(leaf_top, top_lists, top_classes, lists, classes, moments, partner, far)


def call_leaf(part, code, ops, rows, after):
    return pl.pallas_call(
        functools.partial(leaf_kernel, part),
        out_shape=shape(2, OPROWS, 128),
        in_specs=[SMEM, VMEM, VMEM, ANY],
        out_specs=VMEM,
        scratch_shapes=[pltpu.VMEM((LEAF_STEP, OPROWS, 128), F32)],
        compiler_params=pltpu.CompilerParams(vmem_limit_bytes=17 * MIB),
        cost_estimate=cost(LEAVES * LLIST * COEF * COEF * 8, 2 * 10**7),
        name="leaf_translate",
    )(code, ops, rows, after)


def call_last(code, mine, other, *rest):
    return pl.pallas_call(
        last_kernel,
        out_shape=(shape(PAIRS, 128), jax.ShapeDtypeStruct((1,), jnp.int32)),
        in_specs=[VMEM] * 11,
        out_specs=(VMEM, ANY),
        scratch_shapes=[
            pltpu.SMEM((1,), jnp.int32),
            pltpu.VMEM((2 * mine.shape[0], 128), F32),
            pltpu.VMEM((2 * mine.shape[0] // SEND, 128), F32),
            pltpu.VMEM((8, 128), jnp.int32),
            pltpu.SMEM((8, 128), jnp.int32),
            pltpu.VMEM((TLIST, 128), jnp.int32),
            pltpu.SMEM((TLIST, 128), jnp.int32),
            pltpu.SemaphoreType.DMA((3,)),
        ] + FINISH_SCRATCH,
        compiler_params=pltpu.CompilerParams(vmem_limit_bytes=24 * MIB),
        name="finish",
    )(code, mine, other, *rest)


def call_spare(leaf_top, code, table, *rest):
    return pl.pallas_call(
        spare_kernel,
        out_shape=shape(PAIRS, 128),
        in_specs=[SMEM, SMEM] + [VMEM] * 9,
        out_specs=VMEM,
        scratch_shapes=FINISH_SCRATCH,
        compiler_params=pltpu.CompilerParams(vmem_limit_bytes=24 * MIB),
        name="finish_spare",
    )(leaf_top, code, table, *rest)


def sent_over(block, axis):
    return [block] + [
        lax.ppermute(block, axis, [(i, i ^ s) for i in range(4)]) for s in range(1, 4)
    ]


def body(
    particles, counts, leaf_top, near_list, leaf_list, leaf_class, top_list, top_class,
    m2l_ops, m2m_ops,
):
    pts = particles.reshape(4, PAIRS, 128).transpose(1, 0, 2).reshape(4 * PAIRS, 128)
    tops = leaf_top.reshape(1, LEAVES)
    m2m = m2m_ops.transpose(1, 0, 2)
    own, near_edge, far_edge, dist, moments, send, lifted, mask = call_first(
        pts, counts.reshape(1, LEAVES), leaf_top, tops, m2m
    )
    devices = lax.axis_size(AXES)
    partner = [(i, i ^ 1) for i in range(devices)]
    far = [(i, (i + 2 * (i & 1) - 1) % devices) for i in range(devices)]
    over_y = sent_over(send, "y")
    from_partner = lax.ppermute(near_edge, AXES, partner)
    from_far = lax.ppermute(far_edge, AXES, far)
    ops = call_turn(m2l_ops.transpose(1, 2, 0), send)
    by_y = call_join(over_y, ops, from_partner, from_far)
    over_x = sent_over(by_y, "x")
    code_a, code_b, rows, top_code = call_halo(
        leaf_top, top_list.T, top_class.T, leaf_list.T, leaf_class.T, moments,
        from_partner, from_far,
    )
    local_a = call_leaf(0, code_a, ops, rows, by_y)
    by_x = call_join(over_x, local_a)
    over_z = sent_over(by_x, ("zlo", "zhi"))
    near = call_near(near_list.T, own, from_partner, from_far, by_x)
    mine = call_join(over_z, near)
    other = lax.ppermute(mine, "core", [(0, 1), (1, 0)])
    local_b = call_leaf(1, code_b, ops, rows, mine)
    rest = (ops, m2m, tops, local_a, local_b, dist, near, mask)
    result, over = call_last(top_code, mine, other, *rest)

    def spare():
        held = jnp.arange(LEAVES, dtype=jnp.int32)[:, None] == (leaf_top - leaf_top[0])[None]
        partial = jnp.matmul(held.astype(F32), lifted, precision=HIGH)
        table = lax.dynamic_update_slice(
            jnp.zeros((TOPBOX + LEAVES, 128), F32), partial, (leaf_top[0], 0)
        )
        for k in range(7):
            swap = [(i, i ^ (1 << k)) for i in range(devices)]
            table = table + lax.ppermute(table, AXES, swap)
        start = jnp.minimum(leaf_top[0], TOPBOX - LEAVES)
        lists, classes = (
            lax.dynamic_slice_in_dim(x, start, LEAVES, axis=0).T for x in (top_list, top_class)
        )
        again = call_turn(m2l_ops.transpose(1, 2, 0), table)
        return call_spare(leaf_top, pack_codes(classes, lists), table, again, *rest[1:])

    result = lax.cond(over[0] >= SEND, spare, lambda: result)
    return result.reshape(-1)


def solution(mesh):
    fine = Mesh(mesh.devices.reshape(2, 2, 4, 4, 2), AXES)
    return jax.shard_map(
        body,
        mesh=fine,
        in_specs=(
            P(None, AXES), P(AXES), P(AXES), P(AXES, None), P(AXES, None), P(AXES, None),
            P(), P(), P(), P(),
        ),
        out_specs=P(AXES),
        check_vma=False,
    )
```
